32 devices in a mesh: group: 4 (over y, x), shard: 8 (over z, core).
Axes of the slice: x: 2, y: 2, z: 4, core: 2. Of those that a mesh axis runs over, the one named last changes fastest.
Arguments:
- features: bfloat16 [131072, 100], P(('group', 'shard')), may hold values from -6 to 6
- node_counts: int32 [32], P(('group', 'shard')), may hold values from 2048 to 4096, as said below
- degrees: int32 [131072], P(('group', 'shard')), may hold values from 1 to 16, as said below
- neighbours: int32 [131072, 16], P(('group', 'shard')), may hold values from 0 to 4479, as said below
- send_rows: int32 [1024, 12], P(('group', 'shard')), may hold values from 0 to 4095, as said below
- labels: int32 [131072], P(('group', 'shard')), may hold values from 0 to 46
- train_mask: int32 [131072], P(('group', 'shard')), may hold values from 0 to 1
- weight_first: float32 [200, 256], P(None, 'shard'), may hold values from -0.4375 to 0.4375
- weight_rest: float32 [2, 512, 256], P(None, None, 'shard'), may hold values from -0.25 to 0.25
- weight_head: float32 [256, 47], P('shard'), may hold values from -0.375 to 0.375
- biases: float32 [3, 256], P(None, 'shard'), may hold values from -4 to 4
- gains: float32 [3, 256], P(None, 'shard')
- moment_first: float32 [200, 256], P(None, 'shard'), may hold values from -1.9073486e-05 to 1.9073486e-05
- square_first: float32 [200, 256], P(None, 'shard'), may hold values from 1.2235708e-12 to 4.8942833e-12
- moment_rest: float32 [2, 512, 256], P(None, None, 'shard'), may hold values from -5.340576e-05 to 5.340576e-05
- square_rest: float32 [2, 512, 256], P(None, None, 'shard'), may hold values from 1.2235709e-11 to 4.8942836e-11
- moment_head: float32 [256, 47], P('shard'), may hold values from -5.340576e-05 to 5.340576e-05
- square_head: float32 [256, 47], P('shard'), may hold values from 1.2235709e-11 to 4.8942836e-11
- moment_bias: float32 [3, 256], P(None, 'shard'), may hold values from -0.00015258789 to 0.00015258789
- square_bias: float32 [3, 256], P(None, 'shard'), may hold values from 1.1012138e-10 to 4.404855e-10
- moment_gain: float32 [3, 256], P(None, 'shard'), may hold values from -0.00015258789 to 0.00015258789
- square_gain: float32 [3, 256], P(None, 'shard'), may hold values from 1.1012138e-10 to 4.404855e-10
Outputs:
- loss_sum: float32 [], replicated
- label_count: float32 [], replicated
- grad_norm: float32 [], replicated
- new_first: float32 [200, 256], P(None, 'shard')
- new_moment_first: float32 [200, 256], P(None, 'shard')
- new_square_first: float32 [200, 256], P(None, 'shard')
- new_rest: float32 [2, 512, 256], P(None, None, 'shard')
- new_moment_rest: float32 [2, 512, 256], P(None, None, 'shard')
- new_square_rest: float32 [2, 512, 256], P(None, None, 'shard')
- new_head: float32 [256, 47], P('shard')
- new_moment_head: float32 [256, 47], P('shard')
- new_square_head: float32 [256, 47], P('shard')
- new_biases: float32 [3, 256], P(None, 'shard')
- new_moment_bias: float32 [3, 256], P(None, 'shard')
- new_square_bias: float32 [3, 256], P(None, 'shard')
- new_gains: float32 [3, 256], P(None, 'shard')
- new_moment_gain: float32 [3, 256], P(None, 'shard')
- new_square_gain: float32 [3, 256], P(None, 'shard')
- copy_first: bfloat16 [200, 256], P(None, 'shard')
- copy_rest: bfloat16 [2, 512, 256], P(None, None, 'shard')
- copy_head: bfloat16 [256, 47], P('shard')
The draws below stay inside these ranges and needn't reach their ends.
Inputs may be any that keep to these rules, and one draw needn't show every extreme that they name: `node_counts`: between half of 4096 and 4096; some device holds exactly 4096 nodes. `degrees`: some node uses all 16 slots. `neighbours`: for a counted slot's device d, each used neighbour column is either an own row below node_counts[d] or a received row at 4096 or above; unused slots hold any column. `send_rows`: each entry is below node_counts of the sending device; the largest value is reached.
All inputs are finite; a program needn't handle non-finite values.
Results may differ from the reference program's by a relative error of at most 0.0083.
Values may be sent and summed in bfloat16 or wider, within the bound.
A program may use at most 320 MiB of HBM per device.

```python
import math
import jax
import jax.numpy as jnp
from jax import lax

FIN = 100
HID = 256
CLS = 47
LAYERS = 3
NODE_CAPACITY = 4096
SEND_CAP = 12
DEG = 16
STEP = 10
NODES = 131072
PARAMS = 326912
N_GROUP = 4
N_SHARD = 8
DEVICES = 32


def counts_common(key):
    base = jax.random.fold_in(key, 11)
    first_key, second_key = jax.random.split(base)
    drawn = jax.random.randint(first_key, (DEVICES,), NODE_CAPACITY // 2, NODE_CAPACITY + 1)
    chosen = jax.random.randint(second_key, (), 0, DEVICES)
    return jnp.where(jnp.arange(DEVICES) == chosen, NODE_CAPACITY, drawn).astype(jnp.int32)


def draw_node_counts(key, part):
    return counts_common(key)


def draw_degrees(key, part):
    base = jax.random.fold_in(key, 53)
    first_key, second_key = jax.random.split(base)
    drawn = jax.random.randint(first_key, (NODES,), 1, DEG + 1)
    chosen = jax.random.randint(second_key, (), 0, NODES)
    return jnp.where(jnp.arange(NODES) == chosen, DEG, drawn).astype(jnp.int32)


def draw_neighbours(key, part):
    counts = counts_common(key)
    base = jax.random.fold_in(key, 23)
    local_key, remote_key, pick_key = jax.random.split(base, 3)
    limit = jnp.repeat(counts, NODE_CAPACITY)[:, None]
    local = jax.random.randint(local_key, (NODES, DEG), 0, limit)
    remote = jax.random.randint(remote_key, (NODES, DEG), NODE_CAPACITY, NODE_CAPACITY + DEVICES * SEND_CAP)
    picked = jax.random.randint(pick_key, (NODES, DEG), 0, 2)
    return jnp.where(picked == 1, remote, local).astype(jnp.int32)


def draw_send_rows(key, part):
    counts = counts_common(key)
    base = jax.random.fold_in(key, 37)
    limit = jnp.repeat(counts, DEVICES)[:, None]
    drawn = jax.random.randint(base, (DEVICES * DEVICES, SEND_CAP), 0, limit)
    slot = jnp.arange(SEND_CAP)[None, :]
    return jnp.where(slot == 0, limit - 1, drawn).astype(jnp.int32)


def draw_train_mask(key, part):
    base = jax.random.fold_in(key, 41)
    device = jnp.arange(NODES) // NODE_CAPACITY
    shard_place = device % N_SHARD
    group_place = device // N_SHARD
    level = 10 * (N_SHARD - 1 + 2 * shard_place) * (N_GROUP - 1 + 2 * group_place) // ((N_SHARD - 1) * (N_GROUP - 1))
    drawn = jax.random.randint(base, (NODES,), 0, 100)
    return (drawn < level).astype(jnp.int32)


def draw_gains(key, part):
    base = jax.random.fold_in(key, 61)
    across = jnp.arange(HID, dtype=jnp.float32) / (HID - 1)
    noise = jax.random.uniform(base, (LAYERS, HID), jnp.float32, 0.85, 1.15)
    return (1.0 + 2.0 * across)[None, :] * noise


def with_ends(entries, rng, least, top_value):
    extent = entries.shape
    index_at = [jax.random.randint(jax.random.fold_in(rng, axis), (), 0, extent[axis]) for axis in range(len(extent))]
    entries = entries.at[tuple(index_at)].set(least)
    longest = extent.index(max(extent))
    index_at[longest] = (index_at[longest] + 1) % extent[longest]
    return entries.at[tuple(index_at)].set(top_value)


def level_of(key, extent, cuts, smallest, top_value):
    loudness = 1.0
    for dim, blocks in cuts:
        steps = jax.random.uniform(jax.random.fold_in(jax.random.fold_in(key, 6), dim), (blocks,), jnp.float32, smallest / len(cuts), top_value / len(cuts))
        loudness = loudness * jnp.repeat(jnp.exp(steps), extent[dim] // blocks).reshape((-1,) + (1,) * (len(extent) - 1 - dim))
    return loudness


def scatter_about(own_key, dims, scale, most, cuts=(), kind=jnp.bfloat16):
    values = jax.random.normal(own_key, dims, jnp.float32) * scale
    if len(cuts) > 0:
        values = level_of(own_key, dims, cuts, -0.22, 0.18) * values
    return jnp.clip(values, min=-most, max=most).astype(kind)


def setup_inputs(seed: int = 0) -> dict:
    splits = jax.random.split(jax.random.key(seed), 23)
    return {
        "features": scatter_about(splits[0], (NODES, FIN), 1.0, 6.0, ((0, 32),)),
        "node_counts": draw_node_counts(jax.random.fold_in(splits[22], 71), 0),
        "degrees": draw_degrees(jax.random.fold_in(splits[22], 71), 0),
        "neighbours": draw_neighbours(jax.random.fold_in(splits[22], 71), 0),
        "send_rows": draw_send_rows(jax.random.fold_in(splits[22], 71), 0),
        "labels": with_ends(jax.random.randint(splits[5], (NODES,), 0, CLS), jax.random.fold_in(splits[5], 1), 0, CLS - 1).astype(jnp.int32),
        "train_mask": draw_train_mask(jax.random.fold_in(splits[22], 71), 0),
        "weight_first": scatter_about(splits[7], (2 * FIN, HID), (2 * FIN) ** -0.5, 0.4375, ((1, 8),), jnp.float32),
        "weight_rest": scatter_about(splits[8], (LAYERS - 1, 2 * HID, HID), (2 * HID) ** -0.5, 0.25, ((2, 8),), jnp.float32),
        "weight_head": scatter_about(splits[9], (HID, CLS), HID ** -0.5, 0.375, ((0, 8),), jnp.float32),
        "biases": scatter_about(splits[10], (LAYERS, HID), 0.3, 4.0, ((1, 8),), jnp.float32),
        "gains": draw_gains(jax.random.fold_in(splits[22], 71), 0),
        "moment_first": scatter_about(splits[12], (2 * FIN, HID), (0.0007 / PARAMS ** 0.5), 1.9073486328125e-05, ((1, 8),), jnp.float32),
        "square_first": jnp.clip(jnp.exp(math.log(4.8942833293097454e-12) - 1.3862944 * jax.random.uniform(splits[13], (2 * FIN, HID), jnp.float32) ** level_of(splits[13], (2 * FIN, HID), ((1, 8),), -0.2, 0.2)), 1.2235708323274364e-12, 4.8942833293097454e-12),
        "moment_rest": scatter_about(splits[14], (LAYERS - 1, 2 * HID, HID), (0.002 / PARAMS ** 0.5), 5.340576171875e-05, ((2, 8),), jnp.float32),
        "square_rest": jnp.clip(jnp.exp(math.log(4.894283589518267e-11) - 1.3862944 * jax.random.uniform(splits[15], (LAYERS - 1, 2 * HID, HID), jnp.float32) ** level_of(splits[15], (LAYERS - 1, 2 * HID, HID), ((2, 8),), -0.2, 0.2)), 1.2235708973795667e-11, 4.894283589518267e-11),
        "moment_head": scatter_about(splits[16], (HID, CLS), (0.002 / PARAMS ** 0.5), 5.340576171875e-05, ((0, 8),), jnp.float32),
        "square_head": jnp.clip(jnp.exp(math.log(4.894283589518267e-11) - 1.3862944 * jax.random.uniform(splits[17], (HID, CLS), jnp.float32) ** level_of(splits[17], (HID, CLS), ((0, 8),), -0.2, 0.2)), 1.2235708973795667e-11, 4.894283589518267e-11),
        "moment_bias": scatter_about(splits[18], (LAYERS, HID), (0.006 / PARAMS ** 0.5), 0.00015258789, ((1, 8),), jnp.float32),
        "square_bias": jnp.clip(jnp.exp(math.log(4.404855091788562e-10) - 1.3862944 * jax.random.uniform(splits[19], (LAYERS, HID), jnp.float32) ** level_of(splits[19], (LAYERS, HID), ((1, 8),), -0.2, 0.2)), 1.1012137729471405e-10, 4.404855091788562e-10),
        "moment_gain": scatter_about(splits[20], (LAYERS, HID), (0.006 / PARAMS ** 0.5), 0.00015258789, ((1, 8),), jnp.float32),
        "square_gain": jnp.clip(jnp.exp(math.log(4.404855091788562e-10) - 1.3862944 * jax.random.uniform(splits[21], (LAYERS, HID), jnp.float32) ** level_of(splits[21], (LAYERS, HID), ((1, 8),), -0.2, 0.2)), 1.1012137729471405e-10, 4.404855091788562e-10),
    }


@jax.custom_vjp
def low(v):
    return lax.optimization_barrier(v.astype(jnp.bfloat16)).astype(jnp.float32)

@jax.custom_vjp
def low_back(v):
    return v

def low_keep(v):
    return (low(v), None)

def low_pass(kept, grad):
    return (grad,)

def back_keep(v):
    return (v, None)

def back_low(kept, grad):
    return (low(grad),)
low.defvjp(low_keep, low_pass)
low_back.defvjp(back_keep, back_low)
precise = lax.Precision.HIGHEST
norm_epsilon = 1e-05
threshold = 0.002
beta_one = 0.5
beta_two = 0.5
adam_epsilon = 1e-08

def aggregate(hidden_low, neighbours, degrees, send_rows):
    feature = hidden_low.shape[1]
    owned_nodes = hidden_low.reshape(DEVICES, NODE_CAPACITY, feature)
    sources = jnp.arange(DEVICES, dtype=jnp.int32)[:, None, None] * NODE_CAPACITY
    picked_rows = sources + send_rows.reshape(DEVICES, DEVICES, SEND_CAP).astype(jnp.int32)
    picked_rows = picked_rows.transpose(1, 0, 2).reshape(DEVICES, DEVICES * SEND_CAP)
    neighbour_index = neighbours.reshape(DEVICES, NODE_CAPACITY, DEG).astype(jnp.int32)
    node_slots = jnp.arange(DEG, dtype=jnp.int32)[None, None, :]
    alive_mask = (node_slots < degrees.reshape(DEVICES, NODE_CAPACITY, 1)).astype(jnp.float32)

    @jax.checkpoint
    def single_device(operands):
        own_rows, pick_rows, neigh_rows, live_rows = operands
        received = low_back(hidden_low[pick_rows])
        table = jnp.concatenate([own_rows, received], axis=0)
        return lax.optimization_barrier(jnp.sum(table[neigh_rows] * live_rows[:, :, None], axis=1))
    summed_rows = lax.map(single_device, (owned_nodes, picked_rows, neighbour_index, alive_mask))
    return summed_rows.reshape(DEVICES * NODE_CAPACITY, feature)

def sage_layer(hidden_low, weight, bias, gain, graph):
    neighbours, degrees, send_rows = graph
    summed_rows = aggregate(hidden_low, neighbours, degrees, send_rows)
    mean_rows = low(low_back(summed_rows) / degrees.astype(jnp.float32)[:, None])
    joined = jnp.concatenate([hidden_low, mean_rows], axis=1)
    before = low_back(jnp.dot(joined, low(weight), precision=precise, preferred_element_type=jnp.float32) + low(bias))
    activity = jax.nn.silu(before)
    inverse_rms = lax.rsqrt(lax.optimization_barrier(jnp.mean(activity * activity, axis=1, keepdims=True)) + norm_epsilon)
    return low(gain) * (activity * inverse_rms)

def adamw(weight, grad, moment, square, rate, decay):
    moment_new = beta_one * moment + (1.0 - beta_one) * grad
    square_new = beta_two * square + (1.0 - beta_two) * grad * grad
    moment_hat = moment_new / (1.0 - beta_one ** STEP)
    square_hat = square_new / (1.0 - beta_two ** STEP)
    weight_new = weight - rate * (moment_hat / (jnp.sqrt(square_hat) + adam_epsilon) + decay * weight)
    return (weight_new, moment_new, square_new)

def reference(features, node_counts, degrees, neighbours, send_rows, labels, train_mask, weight_first, weight_rest, weight_head, biases, gains, moment_first, square_first, moment_rest, square_rest, moment_head, square_head, moment_bias, square_bias, moment_gain, square_gain):
    rows_index = jnp.arange(NODES, dtype=jnp.int32)
    valid = rows_index % NODE_CAPACITY < jnp.repeat(node_counts, NODE_CAPACITY)
    counted = (valid & (train_mask > 0)).astype(jnp.float32)
    label_count = jnp.sum(counted)
    labels_hot = (labels[:, None] == jnp.arange(CLS, dtype=jnp.int32)[None, :]).astype(jnp.float32)
    graph = (neighbours, degrees, send_rows)
    inputs = features.astype(jnp.float32)

    def objective(first, rest, head, bias_all, gain_all):
        hidden = sage_layer(inputs, first, bias_all[0], gain_all[0], graph)
        for level in range(LAYERS - 1):
            hidden = sage_layer(low(hidden), rest[level], bias_all[level + 1], gain_all[level + 1], graph)
        logits = low_back(jnp.dot(low(hidden), low(head), precision=precise, preferred_element_type=jnp.float32))
        logp = jax.nn.log_softmax(logits, axis=1)
        total = -jnp.sum(lax.optimization_barrier(jnp.sum(logp * labels_hot, axis=1)) * counted)
        return (total / label_count, total)
    value, pullback, loss_sum = jax.vjp(objective, weight_first, weight_rest, weight_head, biases, gains, has_aux=True)
    grads = pullback(jnp.ones_like(value))
    grad_norm = jnp.sqrt(sum((jnp.sum(member * member) for member in grads)))
    factor = jnp.minimum(1.0, threshold / grad_norm)
    clipped = [member * factor for member in grads]
    first_out = adamw(weight_first, clipped[0], moment_first, square_first, 0.05, 0.01)
    rest_out = adamw(weight_rest, clipped[1], moment_rest, square_rest, 0.05, 0.01)
    head_out = adamw(weight_head, clipped[2], moment_head, square_head, 0.05, 0.01)
    bias_out = adamw(biases, clipped[3], moment_bias, square_bias, 0.3, 0.0)
    gain_out = adamw(gains, clipped[4], moment_gain, square_gain, 0.3, 0.0)
    return (loss_sum, label_count, grad_norm, first_out[0], first_out[1], first_out[2], rest_out[0], rest_out[1], rest_out[2], head_out[0], head_out[1], head_out[2], bias_out[0], bias_out[1], bias_out[2], gain_out[0], gain_out[1], gain_out[2], first_out[0].astype(jnp.bfloat16), rest_out[0].astype(jnp.bfloat16), head_out[0].astype(jnp.bfloat16))
```

```python
import functools

import jax
import jax.numpy as jnp
from jax import lax
from jax.experimental import pallas as pl
from jax.experimental.pallas import tpu as pltpu
from jax.sharding import PartitionSpec as P

STEP = 10
MESH = pl.DeviceIdType.MESH
bf16 = jnp.bfloat16
f32 = jnp.float32
i32 = jnp.int32

norm_epsilon = 1e-05
threshold = 0.002
beta_one = 0.5
beta_two = 0.5
adam_epsilon = 1e-08

LANE = 128
LOW = 256
STRIP = 32

NN = (((1,), (0,)), ((), ()))
NT = (((1,), (1,)), ((), ()))
TN = (((0,), (0,)), ((), ()))


def dot(a, b, dims):
    return lax.dot_general(a, b, dims, preferred_element_type=f32)


def round_up(value, unit):
    return -(-value // unit) * unit


def twice(half, width):
    return jnp.concatenate([half] * (width // LANE), axis=1)


def step_kernel(
    cfg,
    feat_ref,
    key_ref,
    deg_ref,
    label_ref,
    mask_ref,
    count_ref,
    send_ref,
    first_ref,
    rest_ref,
    head_ref,
    bias_ref,
    gain_ref,
    grad_out,
    scalar_out,
    counts,
    table1,
    table2,
    table3,
    mean1,
    mean2,
    gmean,
    wide,
    out1,
    in1,
    outs,
    ins,
    info,
    wsend,
    wwire,
    wfull,
    vectors,
    before,
    active,
    slope,
    ghid,
    gacc,
    bacc,
    hacc,
    gfull,
    gwire,
    recv1,
    send2,
    recv2,
    part3,
    recv3,
    scal_send,
    scal_recv,
    row_ssem,
    row_rsem,
    w_ssem,
    w_rsem,
    g_ssem,
    g_rsem,
    s_ssem,
    s_rsem,
):
    n_group, n_shard = cfg["n_group"], cfg["n_shard"]
    nodes, fin, cls = cfg["nodes"], cfg["fin"], cfg["cls"]
    pad, remote, chunk, wire = cfg["pad"], cfg["remote"], cfg["chunk"], cfg["wire"]
    block, fin_pad, hid = cfg["block"], cfg["fin_pad"], cfg["hid"]
    devices = n_group * n_shard
    columns = nodes + remote
    my_group, my_shard = lax.axis_index("group"), lax.axis_index("shard")
    me = my_group * n_shard + my_shard
    blocks = nodes // block

    def target(group, shard):
        return {"group": group, "shard": shard}

    barrier = pltpu.get_barrier_semaphore()

    def greet(i, carry):
        peer = lax.rem(me + i, devices)
        pl.semaphore_signal(
            barrier,
            inc=1,
            device_id=target(lax.div(peer, n_shard), lax.rem(peer, n_shard)),
            device_id_type=MESH,
        )
        return carry

    lax.fori_loop(1, devices, greet, 0)

    def start_rows(source, landing, ssem, rsem):
        def start(i, carry):
            peer = lax.rem(me + i, devices)
            pltpu.make_async_remote_copy(
                src_ref=source.at[pl.ds(pl.multiple_of(peer * pad, pad), pad), :],
                dst_ref=landing.at[pl.ds(pl.multiple_of(me * pad, pad), pad), :],
                send_sem=ssem,
                recv_sem=rsem,
                device_id=target(lax.div(peer, n_shard), lax.rem(peer, n_shard)),
                device_id_type=MESH,
            ).start()
            return carry

        lax.fori_loop(1, devices, start, 0)
        own = pl.ds(pl.multiple_of(me * pad, pad), pad)
        landing[own, :] = source[own, :]

    def wait_bytes(ref, sem):
        pltpu.make_async_copy(ref, ref, sem).wait()

    def wait_rows(source, landing, ssem, rsem):
        rows = pl.ds(0, (devices - 1) * pad)
        wait_bytes(source.at[rows, :], ssem)
        wait_bytes(landing.at[rows, :], rsem)

    some = min(remote, 512)
    row_parts = [slice(r, r + some) for r in range(0, remote, some)]

    def picks(i, rows):
        lanes = lax.broadcasted_iota(i32, (some, LANE), 1) + i * block
        parts = [
            jnp.where(send_ref[rows, :] == lanes + LANE * j, 1.0, 0.0).astype(bf16)
            for j in range(block // LANE)
        ]
        return jnp.concatenate(parts, axis=1)

    def pick_rows(table, into):
        for rows in row_parts:

            def add(i, total):
                off = pl.multiple_of(i * block, block)
                return total + dot(picks(i, rows), table[:, pl.ds(off, block)], NT)

            total = lax.fori_loop(0, blocks, add, jnp.zeros((some, table.shape[0]), f32))
            into[rows, :] = total.astype(bf16)

    total_counted = jnp.zeros((1, LANE), f32)
    lane_row = lax.broadcasted_iota(i32, (1, LANE), 1)
    for r in range(nodes // LANE):
        lanes = slice(r * LANE, (r + 1) * LANE)
        info[0:1, lanes] = 1.0 / deg_ref[r : r + 1, :].astype(f32)
        info[1:2, lanes] = label_ref[r : r + 1, :].astype(f32)
        counted = jnp.where(
            (lane_row + r * LANE < count_ref[0]) & (mask_ref[r : r + 1, :] > 0), 1.0, 0.0
        )
        info[2:3, lanes] = counted
        total_counted = total_counted + counted
    my_count = jnp.sum(total_counted, axis=1, keepdims=True)
    count_high = jnp.floor(my_count * (1.0 / 256.0))
    count_low = my_count - 256.0 * count_high

    table1[...] = jnp.zeros(table1.shape, bf16)
    table1[0:fin, 0:nodes] = feat_ref[...]

    wsend[...] = jnp.zeros(wsend.shape, wire)
    wsend[:, 0:fin] = first_ref[:, 0:fin].astype(bf16).astype(wire)
    wsend[:, LANE : LANE + fin] = first_ref[:, fin : 2 * fin].astype(bf16).astype(wire)
    wsend[:, 2 * LANE : 2 * LANE + cls] = head_ref[...].astype(bf16).astype(wire)
    small = jnp.concatenate(
        [bias_ref[...], gain_ref[...], jnp.zeros((2, chunk), f32)], axis=0
    )
    wsend[:, 3 * LANE : 3 * LANE + 8] = small.T.astype(bf16).astype(wire)
    for level in range(2):
        lanes = slice(4 * LANE + level * 2 * hid, 4 * LANE + (level + 1) * 2 * hid)
        wsend[:, lanes] = rest_ref[level].astype(bf16).astype(wire)

    pick_rows(table1, out1)
    spare = lax.rem(lax.broadcasted_iota(i32, (remote, fin_pad), 0), pad)
    picked = out1[...].astype(f32)
    picked = jnp.where(spare == pad - 2, count_high, picked)
    picked = jnp.where(spare == pad - 1, count_low, picked)
    out1[...] = picked.astype(bf16)

    pl.semaphore_wait(barrier, devices - 1)
    start_rows(out1, in1, row_ssem.at[0], row_rsem.at[0])

    own_chunk = pl.ds(pl.multiple_of(my_shard * chunk, chunk), chunk)

    def send_weights(i, carry):
        shard = lax.rem(my_shard + i, n_shard)
        pltpu.make_async_remote_copy(
            src_ref=wsend,
            dst_ref=wwire.at[own_chunk, :],
            send_sem=w_ssem,
            recv_sem=w_rsem,
            device_id=target(my_group, shard),
            device_id_type=MESH,
        ).start()
        return carry

    lax.fori_loop(1, n_shard, send_weights, 0)
    wwire[own_chunk, :] = wsend[...]

    high_rows = columns // LOW
    low_iota = lax.broadcasted_iota(i32, (LOW, LOW), 0).astype(f32).astype(bf16)
    same_node = (
        lax.div(lax.broadcasted_iota(i32, (16, LOW), 1), 16)
        == lax.broadcasted_iota(i32, (16, LOW), 0)
    ).astype(f32).astype(bf16)
    zero_tile = jnp.zeros((16, LOW), bf16)
    one_low = jnp.ones((LOW, LOW), bf16)
    zero_low = jnp.zeros((LOW, LOW), bf16)
    group_rows = 16 if counts.dtype == bf16 else 32
    fold = group_rows // 16

    def build(it, carry):
        keys = key_ref[pl.ds(pl.multiple_of(it * 8, 8), 8), :]
        high = (keys >> 8).astype(f32)
        low = (keys & 255).astype(f32)
        for k in range(0, 8, fold):
            made = []
            for kk in range(k, k + fold):
                high_row = jnp.broadcast_to(high[kk : kk + 1, :], (16, LOW)).astype(bf16)
                low_row = jnp.broadcast_to(low[kk : kk + 1, :], (16, LOW)).astype(bf16)
                left = jnp.concatenate(
                    [
                        jnp.where(high_row == jnp.asarray(h, bf16), same_node, zero_tile)
                        for h in range(high_rows)
                    ],
                    axis=0,
                )
                right = jnp.where(
                    low_iota == jnp.concatenate([low_row] * (LOW // 16), axis=0),
                    one_low,
                    zero_low,
                )
                made.append(dot(left, right, NT))
            row = pl.multiple_of(it * 128 + k * 16, group_rows)
            for h in range(high_rows):
                tile = jnp.concatenate([m[h * 16 : h * 16 + 16, :] for m in made], axis=0)
                counts[pl.ds(row, group_rows), h * LOW : (h + 1) * LOW] = tile.astype(
                    counts.dtype
                )
        return carry

    lax.fori_loop(0, nodes // 128, build, 0)

    wait_bytes(wwire.at[pl.ds(0, (n_shard - 1) * chunk), :], w_rsem)
    for _ in range(n_shard - 1):
        wait_bytes(wsend, w_ssem)
    wfull[...] = wwire[...].astype(bf16)
    weight_lanes = (
        slice(0, 2 * LANE),
        slice(4 * LANE, 4 * LANE + 2 * hid),
        slice(4 * LANE + 2 * hid, 4 * LANE + 4 * hid),
    )
    small_full = wfull[:, 3 * LANE : 4 * LANE].astype(f32)
    for v in range(6):
        vectors[v] = jnp.broadcast_to(small_full[:, v : v + 1], (hid, LANE))

    def matrix(level):
        return wfull[:, weight_lanes[level]]

    wait_rows(out1, in1, row_ssem.at[0], row_rsem.at[0])
    received = in1[...].astype(f32)
    scale = jnp.where(spare == pad - 2, 256.0, jnp.where(spare == pad - 1, 1.0, 0.0))
    label_count = jnp.sum(received * scale, axis=0, keepdims=True)
    table1[:, nodes:] = in1[...].T

    def c_block(off, lanes):
        return counts[pl.ds(off, block), lanes].astype(bf16)

    strips = [slice(r, r + STRIP) for r in range(0, hid, STRIP)]

    def fold_rows(value):
        return jnp.sum(value.reshape(STRIP // 8, 8, value.shape[1]), axis=0)

    def activate(level, keep_slope, store_before):
        squares = jnp.zeros((8, block), f32)
        for st in strips:
            b = before[st, :] + twice(vectors[level, st, :], block)
            s = 0.5 + 0.5 * jnp.tanh(0.5 * b)
            a = b * s
            active[st, :] = a
            if keep_slope:
                slope[st, :] = s + a * (1.0 - s)
            squares = squares + fold_rows(a * a)
        mean_square = jnp.sum(squares, axis=0, keepdims=True) * (1.0 / hid)
        return lax.rsqrt(mean_square + norm_epsilon)

    def hidden_strip(level, st, inverse):
        return (twice(vectors[3 + level, st, :], block) * (active[st, :] * inverse)).astype(bf16)

    def forward_block(level, off, summed, table, mean, keep_slope):
        lanes = pl.ds(off, block)
        mean_low = (summed * info[0:1, lanes]).astype(bf16)
        if mean is not None:
            mean[:, lanes] = mean_low
        joined = jnp.concatenate([table[:, lanes], mean_low], axis=0)
        before[...] = dot(matrix(level), joined, NN)
        return joined, activate(level, keep_slope, False)

    def layer_one(i, carry):
        off = pl.multiple_of(i * block, block)
        summed = dot(table1[...], c_block(off, slice(0, columns)), NT)
        _, inverse = forward_block(0, off, summed, table1, mean1, False)
        for st in strips:
            table2[st, pl.ds(off, block)] = hidden_strip(0, st, inverse)
        return carry

    lax.fori_loop(0, blocks, layer_one, 0)

    def own_sums(table):
        def add(i, carry):
            off = pl.multiple_of(i * block, block)
            wide[:, pl.ds(off, block)] = dot(
                table[:, 0:nodes], c_block(off, slice(0, nodes)), NT
            )
            return carry

        lax.fori_loop(0, blocks, add, 0)

    def exchange_forward(table, x):
        pick_rows(table, outs)
        start_rows(outs, ins.at[x], row_ssem.at[x + 1], row_rsem.at[x + 1])
        own_sums(table)
        wait_rows(outs, ins.at[x], row_ssem.at[x + 1], row_rsem.at[x + 1])
        table[:, nodes:] = ins[x].T

    def all_sums(table, off):
        return wide[:, pl.ds(off, block)] + dot(
            table[:, nodes:], c_block(off, slice(nodes, columns)), NT
        )

    exchange_forward(table2, 0)

    def layer_two(i, carry):
        off = pl.multiple_of(i * block, block)
        _, inverse = forward_block(1, off, all_sums(table2, off), table2, mean2, False)
        for st in strips:
            table3[st, pl.ds(off, block)] = hidden_strip(1, st, inverse)
        return carry

    lax.fori_loop(0, blocks, layer_two, 0)

    exchange_forward(table3, 1)
    gfull[...] = jnp.zeros(gfull.shape, f32)
    gacc[...] = jnp.zeros(gacc.shape, f32)
    bacc[...] = jnp.zeros(bacc.shape, f32)
    head_low = wfull[:, 2 * LANE : 3 * LANE]
    cls_pad = round_up(cls, 16)
    one_over_count = 1.0 / label_count[0:1, 0:1]
    class_iota = lax.broadcasted_iota(i32, (cls_pad, block), 0)

    def backward_block(level, off, joined, inverse, need_input):
        lanes = pl.ds(off, block)
        crossed = jnp.zeros((8, block), f32)
        for st in strips:
            u = ghid[st, :] * twice(vectors[3 + level, st, :], block)
            crossed = crossed + fold_rows(u * active[st, :])
        factor = jnp.sum(crossed, axis=0, keepdims=True) * (1.0 / hid) * inverse
        factor = factor * inverse * inverse
        low_parts = []
        for st in strips:
            g = ghid[st, :]
            a = active[st, :]
            u = g * twice(vectors[3 + level, st, :], block)
            low = ((inverse * u - a * factor) * slope[st, :]).astype(bf16)
            low_parts.append(low)
            gain_term = g * (a * inverse)
            bias_term = low.astype(f32)
            gain_sum = gain_term[:, 0:LANE]
            bias_sum = bias_term[:, 0:LANE]
            for j in range(1, block // LANE):
                gain_sum = gain_sum + gain_term[:, j * LANE : (j + 1) * LANE]
                bias_sum = bias_sum + bias_term[:, j * LANE : (j + 1) * LANE]
            gacc[level, st, :] += gain_sum
            bacc[level, st, :] += bias_sum
        low = jnp.concatenate(low_parts, axis=0)
        seg = (0, 1, 2)[level]
        pieces = joined.shape[0] // LANE
        added = dot(low, joined, NT)
        for j in range(pieces):
            gfull[seg, j] += added[:, j * LANE : (j + 1) * LANE]
        if need_input:
            back = dot(matrix(level), low, TN)
            wide[:, lanes] = back[0:hid, :]
            gmean[:, lanes] = (back[hid:, :] * info[0:1, lanes]).astype(bf16)

    def layer_three(i, loss):
        off = pl.multiple_of(i * block, block)
        lanes = pl.ds(off, block)
        joined, inverse = forward_block(2, off, all_sums(table3, off), table3, None, True)
        last = jnp.concatenate([hidden_strip(2, st, inverse) for st in strips], axis=0)
        logits = dot(head_low, last, TN)[0:cls_pad, :]
        logits = jnp.where(class_iota < cls, logits, -jnp.inf)
        highest = jnp.max(logits, axis=0, keepdims=True)
        shifted = logits - highest
        grown = jnp.exp(shifted)
        total = jnp.sum(grown, axis=0, keepdims=True)
        hot = class_iota == info[1:2, lanes].astype(i32)
        counted = info[2:3, lanes]
        chosen = jnp.sum(jnp.where(hot, shifted, 0.0), axis=0, keepdims=True)
        loss = loss + (jnp.log(total) - chosen) * counted
        g_logits = (grown / total - jnp.where(hot, 1.0, 0.0)) * (counted * one_over_count)
        g_low = jnp.concatenate(
            [g_logits, jnp.zeros((LANE - cls_pad, block), f32)], axis=0
        ).astype(bf16)
        gfull[0, 2] += dot(last, g_low, NT)
        ghid[...] = dot(head_low, g_low, NN)
        backward_block(2, off, joined, inverse, True)
        return loss

    loss = lax.fori_loop(0, blocks, layer_three, jnp.zeros((1, block), f32))

    def start_first(seg):
        for piece in range(n_group):
            gwire[seg, piece] = gfull[seg, piece].astype(wire)

        def start(i, carry):
            group = lax.rem(my_group + i, n_group)
            pltpu.make_async_remote_copy(
                src_ref=gwire.at[seg, group],
                dst_ref=recv1.at[seg, my_group],
                send_sem=g_ssem.at[0, seg],
                recv_sem=g_rsem.at[0, seg],
                device_id=target(group, my_shard),
                device_id_type=MESH,
            ).start()
            return carry

        lax.fori_loop(1, n_group, start, 0)
        recv1[seg, my_group] = jnp.zeros(recv1.shape[2:], wire)

    def start_second(seg):
        wait_bytes(gwire.at[seg, pl.ds(0, n_group - 1)], g_ssem.at[0, seg])
        wait_bytes(recv1.at[seg, pl.ds(0, n_group - 1)], g_rsem.at[0, seg])
        total = gfull[seg, my_group]
        for group in range(n_group):
            total = total + recv1[seg, group].astype(f32)
        gfull[seg, my_group] = total
        send2[seg] = total.astype(wire).reshape(n_shard, chunk, LANE)

        def start(i, carry):
            shard = lax.rem(my_shard + i, n_shard)
            pltpu.make_async_remote_copy(
                src_ref=send2.at[seg, shard],
                dst_ref=recv2.at[seg, my_shard],
                send_sem=g_ssem.at[1, seg],
                recv_sem=g_rsem.at[1, seg],
                device_id=target(my_group, shard),
                device_id_type=MESH,
            ).start()
            return carry

        lax.fori_loop(1, n_shard, start, 0)
        recv2[seg, my_shard] = jnp.zeros(recv2.shape[2:], wire)

    def start_third(seg):
        wait_bytes(send2.at[seg, pl.ds(0, n_shard - 1)], g_ssem.at[1, seg])
        wait_bytes(recv2.at[seg, pl.ds(0, n_shard - 1)], g_rsem.at[1, seg])
        total = gfull[seg, my_group, own_chunk, :]
        for shard in range(n_shard):
            total = total + recv2[seg, shard].astype(f32)
        part3[seg] = total

        def start(i, carry):
            group = lax.rem(my_group + i, n_group)
            pltpu.make_async_remote_copy(
                src_ref=part3.at[seg],
                dst_ref=recv3.at[seg, my_group],
                send_sem=g_ssem.at[2, seg],
                recv_sem=g_rsem.at[2, seg],
                device_id=target(group, my_shard),
                device_id_type=MESH,
            ).start()
            return carry

        lax.fori_loop(1, n_group, start, 0)
        recv3[seg, my_group] = total
        return jnp.sum(total * total)

    def wait_third(seg):
        for _ in range(n_group - 1):
            wait_bytes(part3.at[seg], g_ssem.at[2, seg])
        wait_bytes(recv3.at[seg, pl.ds(0, n_group - 1)], g_rsem.at[2, seg])

    def exchange_backward(x):
        for rows in row_parts:
            lanes = slice(nodes + rows.start, nodes + rows.stop)
            back = dot(gmean[...], counts[:, lanes].astype(bf16), NN)
            outs[rows, :] = back.astype(bf16).T
        start_rows(outs, ins.at[x], row_ssem.at[x + 1], row_rsem.at[x + 1])

        def add(i, carry):
            off = pl.multiple_of(i * block, block)
            lanes = pl.ds(off, block)
            wide[:, lanes] += dot(gmean[...], counts[:, lanes].astype(bf16), NN)
            return carry

        lax.fori_loop(0, blocks, add, 0)
        wait_rows(outs, ins.at[x], row_ssem.at[x + 1], row_rsem.at[x + 1])

    def returned(x, i):
        off = pl.multiple_of(i * block, block)
        total = wide[:, pl.ds(off, block)]
        for rows in row_parts:
            total = total + dot(ins[x, rows, :], picks(i, rows), TN)
        return total

    start_first(2)
    exchange_backward(2)
    start_second(2)

    def backward_two(i, carry):
        off = pl.multiple_of(i * block, block)
        lanes = pl.ds(off, block)
        ghid[...] = returned(2, i)
        joined = jnp.concatenate([table2[:, lanes], mean2[:, lanes]], axis=0)
        before[...] = dot(matrix(1), joined, NN)
        inverse = activate(1, True, False)
        backward_block(1, off, joined, inverse, True)
        return carry

    lax.fori_loop(0, blocks, backward_two, 0)
    start_first(1)
    square = start_third(2)
    exchange_backward(3)
    start_second(1)

    def backward_one(i, carry):
        off = pl.multiple_of(i * block, block)
        lanes = pl.ds(off, block)
        ghid[...] = returned(3, i)
        joined = jnp.concatenate([table1[:, lanes], mean1[:, lanes]], axis=0)
        before[...] = dot(matrix(0), joined, NN)
        inverse = activate(0, True, False)
        backward_block(0, off, joined, inverse, False)
        return carry

    lax.fori_loop(0, blocks, backward_one, 0)
    lane_wide = lax.broadcasted_iota(i32, (hid, LANE), 1)
    small_grad = jnp.zeros((hid, LANE), f32)
    for level in range(3):
        small_grad = jnp.where(
            lane_wide == level, jnp.sum(bacc[level], axis=1, keepdims=True), small_grad
        )
        small_grad = jnp.where(
            lane_wide == 3 + level, jnp.sum(gacc[level], axis=1, keepdims=True), small_grad
        )
    gfull[0, 3] = small_grad
    start_first(0)
    square = square + start_third(1)
    start_second(0)
    square = square + start_third(0)

    row8 = lax.broadcasted_iota(i32, (8, LANE), 0)
    mine = jnp.where(row8 == 0, square, jnp.where(row8 == 1, jnp.sum(loss), 0.0))
    scal_send[...] = mine

    def send_scalars(i, carry):
        peer = lax.rem(me + i, devices)
        pltpu.make_async_remote_copy(
            src_ref=scal_send,
            dst_ref=scal_recv.at[me],
            send_sem=s_ssem,
            recv_sem=s_rsem,
            device_id=target(lax.div(peer, n_shard), lax.rem(peer, n_shard)),
            device_id_type=MESH,
        ).start()
        return carry

    lax.fori_loop(1, devices, send_scalars, 0)
    scal_recv[me] = mine
    for seg in range(3):
        wait_third(seg)
    grad_out[...] = recv3[...]
    wait_bytes(scal_recv.at[pl.ds(0, devices - 1)], s_rsem)

    def drain(i, carry):
        wait_bytes(scal_send, s_ssem)
        return carry

    lax.fori_loop(1, devices, drain, 0)
    scalar_out[...] = jnp.where(
        row8 == 2, label_count[0:1, 0:1], jnp.sum(scal_recv[...], axis=0)
    )


def adamw(weight, grad, moment, square, rate, decay):
    moment_new = beta_one * moment + (1.0 - beta_one) * grad
    square_new = beta_two * square + (1.0 - beta_two) * grad * grad
    moment_hat = moment_new / (1.0 - beta_one**STEP)
    square_hat = square_new / (1.0 - beta_two**STEP)
    weight_new = weight - rate * (
        moment_hat / (jnp.sqrt(square_hat) + adam_epsilon) + decay * weight
    )
    return (weight_new, moment_new, square_new)


def per_device(
    n_group,
    n_shard,
    features,
    node_counts,
    degrees,
    neighbours,
    send_rows,
    labels,
    train_mask,
    weight_first,
    weight_rest,
    weight_head,
    biases,
    gains,
    moment_first,
    square_first,
    moment_rest,
    square_rest,
    moment_head,
    square_head,
    moment_bias,
    square_bias,
    moment_gain,
    square_gain,
):
    nodes, fin = features.shape
    devices = n_group * n_shard
    hid = weight_rest.shape[1] // 2
    chunk = hid // n_shard
    cls = weight_head.shape[1]
    cap = send_rows.shape[1]
    slots = neighbours.shape[1]
    pad = round_up(cap + 2, 16)
    remote = devices * pad
    columns = nodes + remote
    block = 256
    wire = bf16 if chunk % 16 == 0 else f32
    counts_dtype = bf16 if nodes * columns * 2 <= 40 * 2**20 else jnp.float8_e4m3fn
    fin_pad = LANE
    cfg = dict(
        n_group=n_group,
        n_shard=n_shard,
        nodes=nodes,
        fin=fin,
        cls=cls,
        pad=pad,
        remote=remote,
        chunk=chunk,
        wire=wire,
        block=block,
        fin_pad=fin_pad,
        hid=hid,
    )

    away = neighbours - nodes
    source = away // cap
    moved = nodes + source * pad + (away - source * cap)
    mapped = jnp.where(away < 0, neighbours, moved)
    live = lax.broadcasted_iota(i32, mapped.shape, 1) < degrees[:, None]
    keys = jnp.where(live, mapped, -1).reshape(nodes // 16, 16 * slots)
    send_padded = jnp.pad(send_rows, ((0, 0), (0, pad - cap)), constant_values=-1)
    send_wide = jnp.broadcast_to(send_padded.reshape(remote, 1), (remote, LANE))

    vmem = pl.BlockSpec(memory_space=pltpu.VMEM)
    smem = pl.BlockSpec(memory_space=pltpu.SMEM)
    width = 4 * LANE + 4 * hid
    dma = pltpu.SemaphoreType.DMA
    scratch = [
        pltpu.VMEM((nodes, columns), counts_dtype),
        pltpu.VMEM((fin_pad, columns), bf16),
        pltpu.VMEM((hid, columns), bf16),
        pltpu.VMEM((hid, columns), bf16),
        pltpu.VMEM((fin_pad, nodes), bf16),
        pltpu.VMEM((hid, nodes), bf16),
        pltpu.VMEM((hid, nodes), bf16),
        pltpu.VMEM((hid, nodes), f32),
        pltpu.VMEM((remote, fin_pad), bf16),
        pltpu.VMEM((remote, fin_pad), bf16),
        pltpu.VMEM((remote, hid), bf16),
        pltpu.VMEM((4, remote, hid), bf16),
        pltpu.VMEM((8, nodes), f32),
        pltpu.VMEM((chunk, width), wire),
        pltpu.VMEM((hid, width), wire),
        pltpu.VMEM((hid, width), bf16),
        pltpu.VMEM((6, hid, LANE), f32),
        pltpu.VMEM((hid, block), f32),
        pltpu.VMEM((hid, block), f32),
        pltpu.VMEM((hid, block), f32),
        pltpu.VMEM((hid, block), f32),
        pltpu.VMEM((3, hid, LANE), f32),
        pltpu.VMEM((3, hid, LANE), f32),
        pltpu.VMEM((8, LANE), f32),
        pltpu.VMEM((3, n_group, hid, LANE), f32),
        pltpu.VMEM((3, n_group, hid, LANE), wire),
        pltpu.VMEM((3, n_group, hid, LANE), wire),
        pltpu.VMEM((3, n_shard, chunk, LANE), wire),
        pltpu.VMEM((3, n_shard, chunk, LANE), wire),
        pltpu.VMEM((3, chunk, LANE), f32),
        pltpu.VMEM((3, n_group, chunk, LANE), f32),
        pltpu.VMEM((8, LANE), f32),
        pltpu.VMEM((devices, 8, LANE), f32),
        dma((5,)),
        dma((5,)),
        dma,
        dma,
        dma((3, 3)),
        dma((3, 3)),
        dma,
        dma,
    ]
    grads, scalars = pl.pallas_call(
        functools.partial(step_kernel, cfg),
        out_shape=(
            jax.ShapeDtypeStruct((3, n_group, chunk, LANE), f32),
            jax.ShapeDtypeStruct((8, LANE), f32),
        ),
        in_specs=[vmem] * 5 + [smem] + [vmem] * 6,
        out_specs=(vmem, vmem),
        scratch_shapes=scratch,
        compiler_params=pltpu.CompilerParams(
            collective_id=0, has_side_effects=True, vmem_limit_bytes=63 * 2**20
        ),
    )(
        features.T,
        keys,
        degrees.reshape(nodes // LANE, LANE),
        labels.reshape(nodes // LANE, LANE),
        train_mask.reshape(nodes // LANE, LANE),
        node_counts,
        send_wide,
        weight_first.T,
        weight_rest.transpose(0, 2, 1),
        weight_head,
        biases,
        gains,
    )
    grad_norm = jnp.sqrt(scalars[0, 0])
    loss_sum = scalars[1, 0]
    label_count = scalars[2, 0]
    factor = jnp.minimum(1.0, threshold / grad_norm)
    grads = grads * factor
    grad_first = jnp.concatenate([grads[0, 0, :, :fin], grads[0, 1, :, :fin]], axis=1).T
    grad_rest = jnp.stack(
        [jnp.concatenate([grads[s, j] for j in range(n_group)], axis=1).T for s in (1, 2)]
    )
    grad_head = grads[0, 2, :, :cls]
    grad_bias = grads[0, 3, :, 0:3].T
    grad_gain = grads[0, 3, :, 3:6].T
    first_out = adamw(weight_first, grad_first, moment_first, square_first, 0.05, 0.01)
    rest_out = adamw(weight_rest, grad_rest, moment_rest, square_rest, 0.05, 0.01)
    head_out = adamw(weight_head, grad_head, moment_head, square_head, 0.05, 0.01)
    bias_out = adamw(biases, grad_bias, moment_bias, square_bias, 0.3, 0.0)
    gain_out = adamw(gains, grad_gain, moment_gain, square_gain, 0.3, 0.0)
    return (
        (loss_sum, label_count, grad_norm)
        + first_out
        + rest_out
        + head_out
        + bias_out
        + gain_out
        + (first_out[0].astype(bf16), rest_out[0].astype(bf16), head_out[0].astype(bf16))
    )


def solution(mesh):
    nodes_split = P(("group", "shard"))
    nodes_rows = P(("group", "shard"), None)
    first = P(None, "shard")
    rest = P(None, None, "shard")
    head = P("shard", None)
    return jax.shard_map(
        functools.partial(per_device, mesh.shape["group"], mesh.shape["shard"]),
        mesh=mesh,
        in_specs=(
            nodes_rows,
            nodes_split,
            nodes_split,
            nodes_rows,
            nodes_rows,
            nodes_split,
            nodes_split,
            first,
            rest,
            head,
            first,
            first,
            first,
            first,
            rest,
            rest,
            head,
            head,
            first,
            first,
            first,
            first,
        ),
        out_specs=(P(), P(), P())
        + (first,) * 3
        + (rest,) * 3
        + (head,) * 3
        + (first,) * 6
        + (first, rest, head),
        check_vma=False,
    )
```

```python
import functools

import jax
import jax.numpy as jnp
from jax import lax
from jax.experimental import pallas as pl
from jax.experimental.pallas import tpu as pltpu
from jax.sharding import PartitionSpec as P

STEP = 10
MESH = pl.DeviceIdType.MESH
bf16 = jnp.bfloat16
f32 = jnp.float32
i32 = jnp.int32

norm_epsilon = 1e-05
threshold = 0.002
beta_one = 0.5
beta_two = 0.5
adam_epsilon = 1e-08

LANE = 128
LOW = 256
narrow = jnp.float8_e4m3fn
STRIP = 32

NN = (((1,), (0,)), ((), ()))
NT = (((1,), (1,)), ((), ()))
TN = (((0,), (0,)), ((), ()))


def dot(a, b, dims):
    return lax.dot_general(a, b, dims, preferred_element_type=f32)


def round_up(value, unit):
    return -(-value // unit) * unit


def twice(half, width):
    return jnp.concatenate([half] * (width // LANE), axis=1)


def step_kernel(
    cfg,
    feat_ref,
    key_ref,
    deg_ref,
    label_ref,
    mask_ref,
    count_ref,
    send_ref,
    first_ref,
    rest_ref,
    head_ref,
    bias_ref,
    gain_ref,
    part_out,
    head_out,
    first_out,
    scalar_out,
    counts,
    picked,
    table1,
    table2,
    table3,
    first_own,
    first_remote,
    mean1,
    mean2,
    before1,
    before2,
    gmean,
    wide,
    out1,
    in1,
    outs,
    ins,
    info,
    wsend,
    wwire,
    wfull,
    vectors,
    before,
    active,
    slope,
    ghid,
    gacc,
    bacc,
    gfull,
    gwire,
    recv1,
    send2,
    recv2,
    part3,
    recv3,
    gfirst,
    fwire,
    frecv,
    fpart,
    ffinal,
    ghead,
    hwire,
    hrecv,
    hpart,
    hfinal,
    scal_send,
    scal_recv,
    row_ssem,
    row_rsem,
    w_ssem,
    w_rsem,
    g_ssem,
    g_rsem,
    f_ssem,
    f_rsem,
    h_ssem,
    h_rsem,
    s_ssem,
    s_rsem,
):
    n_group, n_shard = cfg["n_group"], cfg["n_shard"]
    nodes, fin, cls = cfg["nodes"], cfg["fin"], cfg["cls"]
    pad, remote, chunk, wire = cfg["pad"], cfg["remote"], cfg["chunk"], cfg["wire"]
    block, fin_pad, hid = cfg["block"], cfg["fin_pad"], cfg["hid"]
    devices = n_group * n_shard
    columns = nodes + remote
    my_group, my_shard = lax.axis_index("group"), lax.axis_index("shard")
    me = my_group * n_shard + my_shard
    blocks = nodes // block

    def target(group, shard):
        return {"group": group, "shard": shard}

    barrier = pltpu.get_barrier_semaphore()

    def greet(i, carry):
        peer = lax.rem(me + i, devices)
        pl.semaphore_signal(
            barrier,
            inc=1,
            device_id=target(lax.div(peer, n_shard), lax.rem(peer, n_shard)),
            device_id_type=MESH,
        )
        return carry

    lax.fori_loop(1, devices, greet, 0)

    def start_rows(source, landing, ssem, rsem):
        def start(i, carry):
            peer = lax.rem(me + i, devices)
            pltpu.make_async_remote_copy(
                src_ref=source.at[pl.ds(pl.multiple_of(peer * pad, pad), pad), :],
                dst_ref=landing.at[pl.ds(pl.multiple_of(me * pad, pad), pad), :],
                send_sem=ssem,
                recv_sem=rsem,
                device_id=target(lax.div(peer, n_shard), lax.rem(peer, n_shard)),
                device_id_type=MESH,
            ).start()
            return carry

        lax.fori_loop(1, devices, start, 0)
        own = pl.ds(pl.multiple_of(me * pad, pad), pad)
        landing[own, :] = source[own, :]

    def wait_bytes(ref, sem):
        pltpu.make_async_copy(ref, ref, sem).wait()

    def wait_rows(source, landing, ssem, rsem):
        rows = pl.ds(0, (devices - 1) * pad)
        wait_bytes(source.at[rows, :], ssem)
        wait_bytes(landing.at[rows, :], rsem)

    some = min(remote, 512)
    row_parts = [slice(r, r + some) for r in range(0, remote, some)]

    def make_picks(rows, off, width):
        lanes = lax.broadcasted_iota(i32, (some, LANE), 1) + off
        parts = [
            jnp.where(send_ref[rows, :] == lanes + LANE * j, 1.0, 0.0).astype(bf16)
            for j in range(width // LANE)
        ]
        return jnp.concatenate(parts, axis=1)

    def picks(rows, off):
        if picked.shape[0] == remote:
            return picked[rows, pl.ds(off, block)].astype(bf16)
        return make_picks(rows, off, block)

    def pick_rows(table, into):
        for rows in row_parts:
            if picked.shape[0] == remote:
                total = dot(picked[rows, :].astype(bf16), table[:, 0:nodes], NT)
            else:

                def add(i, total):
                    off = pl.multiple_of(i * block, block)
                    return total + dot(picks(rows, off), table[:, pl.ds(off, block)], NT)

                total = lax.fori_loop(0, blocks, add, jnp.zeros((some, table.shape[0]), f32))
            into[rows, :] = total.astype(bf16)

    total_counted = jnp.zeros((1, LANE), f32)
    lane_row = lax.broadcasted_iota(i32, (1, LANE), 1)
    for r in range(nodes // LANE):
        lanes = slice(r * LANE, (r + 1) * LANE)
        info[0:1, lanes] = 1.0 / deg_ref[r : r + 1, :].astype(f32)
        info[1:2, lanes] = label_ref[r : r + 1, :].astype(f32)
        counted = jnp.where(
            (lane_row + r * LANE < count_ref[0]) & (mask_ref[r : r + 1, :] > 0), 1.0, 0.0
        )
        info[2:3, lanes] = counted
        total_counted = total_counted + counted
    my_count = jnp.sum(total_counted, axis=1, keepdims=True)
    count_high = jnp.floor(my_count * (1.0 / 256.0))
    count_low = my_count - 256.0 * count_high

    table1[fin // 16 * 16 :, :] = jnp.zeros((fin_pad - fin // 16 * 16, nodes), bf16)
    table1[0:fin, :] = feat_ref[...]

    if picked.shape[0] == remote:

        def store_picks(i, carry):
            off = pl.multiple_of(i * 512, 512)
            picked[:, pl.ds(off, 512)] = make_picks(row_parts[0], off, 512).astype(narrow)
            return carry

        lax.fori_loop(0, nodes // 512, store_picks, 0)

    def split_in_two(value, into):
        value = value.astype(f32)
        largest = jnp.max(jnp.abs(value), axis=1, keepdims=True)
        scale = jnp.ones_like(largest)
        for power in (32, 16, 8, 4, 2, 1):
            larger = scale * 2.0**power
            scale = jnp.where(largest * larger <= 448.0, larger, scale)
        scaled = value * scale
        high = scaled.astype(narrow)
        into[0:fin_pad, :] = high
        into[fin_pad:, :] = ((scaled - high.astype(f32)) * 16.0).astype(narrow)
        return 1.0 / scale

    def joined_parts(both, unscale):
        return (both[0:fin_pad, :] + both[fin_pad:, :] * (1.0 / 16.0)) * unscale

    wsend[...] = jnp.zeros(wsend.shape, wire)
    wsend[:, 0:fin] = first_ref[:, 0:fin].astype(bf16).astype(wire)
    wsend[:, LANE : LANE + fin] = first_ref[:, fin : 2 * fin].astype(bf16).astype(wire)
    wsend[:, 2 * LANE : 2 * LANE + cls] = head_ref[...].astype(bf16).astype(wire)
    small = jnp.concatenate(
        [bias_ref[...], gain_ref[...], jnp.zeros((2, chunk), f32)], axis=0
    )
    wsend[:, 3 * LANE : 3 * LANE + 8] = small.T.astype(bf16).astype(wire)
    for level in range(2):
        lanes = slice(4 * LANE + level * 2 * hid, 4 * LANE + (level + 1) * 2 * hid)
        wsend[:, lanes] = rest_ref[level].astype(bf16).astype(wire)

    pick_rows(table1, out1)
    spare = lax.rem(lax.broadcasted_iota(i32, (remote, fin_pad), 0), pad)
    sent = out1[...].astype(f32)
    sent = jnp.where(spare == pad - 2, count_high, sent)
    sent = jnp.where(spare == pad - 1, count_low, sent)
    out1[...] = sent.astype(bf16)

    pl.semaphore_wait(barrier, devices - 1)
    start_rows(out1, in1, row_ssem.at[0], row_rsem.at[0])

    own_chunk = pl.ds(pl.multiple_of(my_shard * chunk, chunk), chunk)
    weight_parts = (
        slice(0, 4 * LANE),
        slice(4 * LANE, 4 * LANE + 2 * hid),
        slice(4 * LANE + 2 * hid, 4 * LANE + 4 * hid),
    )

    def send_weights(part):
        lanes = weight_parts[part]

        def start(i, carry):
            shard = lax.rem(my_shard + i, n_shard)
            pltpu.make_async_remote_copy(
                src_ref=wsend.at[:, lanes],
                dst_ref=wwire.at[own_chunk, lanes],
                send_sem=w_ssem.at[part],
                recv_sem=w_rsem.at[part],
                device_id=target(my_group, shard),
                device_id_type=MESH,
            ).start()
            return carry

        lax.fori_loop(1, n_shard, start, 0)

    def wait_weights(part):
        lanes = weight_parts[part]
        rows = pl.ds(0, (n_shard - 1) * chunk)
        wait_bytes(wwire.at[rows, lanes], w_rsem.at[part])
        wait_bytes(wwire.at[rows, lanes], w_ssem.at[part])
        wfull[:, lanes] = wwire[:, lanes].astype(bf16)

    wwire[own_chunk, :] = wsend[...]
    for part in range(3):
        send_weights(part)
    unscale_own = split_in_two(table1[...], first_own)

    high_rows = columns // LOW
    low_iota = lax.broadcasted_iota(i32, (LOW, LOW), 0).astype(f32).astype(bf16)
    same_node = (
        lax.div(lax.broadcasted_iota(i32, (16, LOW), 1), 16)
        == lax.broadcasted_iota(i32, (16, LOW), 0)
    ).astype(f32).astype(bf16)
    zero_tile = jnp.zeros((16, LOW), bf16)
    one_low = jnp.ones((LOW, LOW), bf16)
    zero_low = jnp.zeros((LOW, LOW), bf16)
    group_rows = 32
    fold = group_rows // 16

    def build(it, carry):
        keys = key_ref[pl.ds(pl.multiple_of(it * 8, 8), 8), :]
        high = (keys >> 8).astype(f32)
        low = (keys & 255).astype(f32)
        for k in range(0, 8, fold):
            made = []
            for kk in range(k, k + fold):
                high_row = jnp.broadcast_to(high[kk : kk + 1, :], (16, LOW)).astype(bf16)
                low_row = jnp.broadcast_to(low[kk : kk + 1, :], (16, LOW)).astype(bf16)
                left = jnp.concatenate(
                    [
                        jnp.where(high_row == jnp.asarray(h, bf16), same_node, zero_tile)
                        for h in range(high_rows)
                    ],
                    axis=0,
                ).astype(narrow)
                right = jnp.where(
                    low_iota == jnp.concatenate([low_row] * (LOW // 16), axis=0),
                    one_low,
                    zero_low,
                ).astype(narrow)
                made.append(dot(left, right, NT))
            row = pl.multiple_of(it * 128 + k * 16, group_rows)
            for h in range(high_rows):
                tile = jnp.concatenate([m[h * 16 : h * 16 + 16, :] for m in made], axis=0)
                counts[pl.ds(row, group_rows), h * LOW : (h + 1) * LOW] = tile.astype(
                    counts.dtype
                )
        return carry

    lax.fori_loop(0, nodes // 128, build, 0)

    wait_weights(0)
    weight_lanes = (
        slice(0, 2 * LANE),
        weight_parts[1],
        weight_parts[2],
    )
    small_full = wfull[:, 3 * LANE : 4 * LANE].astype(f32)
    for v in range(6):
        vectors[v] = jnp.broadcast_to(small_full[:, v : v + 1], (hid, LANE))

    def matrix(level):
        return wfull[:, weight_lanes[level]]

    wait_rows(out1, in1, row_ssem.at[0], row_rsem.at[0])
    received = in1[...].astype(f32)
    scale = jnp.where(spare == pad - 2, 256.0, jnp.where(spare == pad - 1, 1.0, 0.0))
    label_count = jnp.sum(received * scale, axis=0, keepdims=True)
    unscale_remote = split_in_two(
        jnp.where(spare < pad - 2, received, 0.0).T, first_remote
    )

    def c_block(off, lanes):
        return counts[pl.ds(off, block), lanes].astype(bf16)

    strips = [slice(r, r + STRIP) for r in range(0, hid, STRIP)]

    def fold_rows(value):
        return jnp.sum(value.reshape(STRIP // 8, 8, value.shape[1]), axis=0)

    def activate(level, keep_slope, kept, off):
        squares = jnp.zeros((8, block), f32)
        for st in strips:
            if kept is not None and keep_slope:
                b = kept[st, pl.ds(off, block)]
            else:
                b = before[st, :] + twice(vectors[level, st, :], block)
            if kept is not None and not keep_slope:
                kept[st, pl.ds(off, block)] = b
            s = 0.5 + 0.5 * jnp.tanh(0.5 * b)
            a = b * s
            active[st, :] = a
            if keep_slope:
                slope[st, :] = s + a * (1.0 - s)
            squares = squares + fold_rows(a * a)
        mean_square = jnp.sum(squares, axis=0, keepdims=True) * (1.0 / hid)
        return lax.rsqrt(mean_square + norm_epsilon)

    def hidden_strip(level, st, inverse):
        return (twice(vectors[3 + level, st, :], block) * (active[st, :] * inverse)).astype(bf16)

    def kept_or_none(kept):
        return kept if kept is not None and kept.shape[1] == nodes else None

    def forward_block(level, off, summed, table, mean, kept, keep_slope):
        lanes = pl.ds(off, block)
        mean_low = (summed * info[0:1, lanes]).astype(bf16)
        if mean is not None:
            mean[:, lanes] = mean_low
        joined = jnp.concatenate([table[:, lanes], mean_low], axis=0)
        before[...] = dot(matrix(level), joined, NN)
        return joined, activate(level, keep_slope, kept_or_none(kept), off)

    def layer_one(i, carry):
        off = pl.multiple_of(i * block, block)
        own = dot(first_own[...], counts[pl.ds(off, block), 0:nodes], NT)
        away = dot(first_remote[...], counts[pl.ds(off, block), nodes:], NT)
        summed = joined_parts(own, unscale_own) + joined_parts(away, unscale_remote)
        _, inverse = forward_block(0, off, summed, table1, mean1, before1, False)
        for st in strips:
            table2[st, pl.ds(off, block)] = hidden_strip(0, st, inverse)
        return carry

    lax.fori_loop(0, blocks, layer_one, 0)

    def own_sums(table):
        def add(i, carry):
            off = pl.multiple_of(i * block, block)
            wide[:, pl.ds(off, block)] = dot(
                table[:, 0:nodes], c_block(off, slice(0, nodes)), NT
            )
            return carry

        lax.fori_loop(0, blocks, add, 0)

    def exchange_forward(table, x):
        pick_rows(table, outs)
        start_rows(outs, ins.at[x % 2], row_ssem.at[x + 1], row_rsem.at[x + 1])
        own_sums(table)
        wait_rows(outs, ins.at[x % 2], row_ssem.at[x + 1], row_rsem.at[x + 1])
        table[:, nodes:] = ins[x % 2].T

    def all_sums(table, off):
        return wide[:, pl.ds(off, block)] + dot(
            table[:, nodes:], c_block(off, slice(nodes, columns)), NT
        )

    exchange_forward(table2, 0)
    wait_weights(1)

    def layer_two(i, carry):
        off = pl.multiple_of(i * block, block)
        _, inverse = forward_block(1, off, all_sums(table2, off), table2, mean2, before2, False)
        for st in strips:
            table3[st, pl.ds(off, block)] = hidden_strip(1, st, inverse)
        return carry

    lax.fori_loop(0, blocks, layer_two, 0)

    exchange_forward(table3, 1)
    wait_weights(2)
    gfirst[...] = jnp.zeros(gfirst.shape, f32)
    ghead[...] = jnp.zeros(ghead.shape, f32)
    gfull[...] = jnp.zeros(gfull.shape, f32)
    gacc[...] = jnp.zeros(gacc.shape, f32)
    bacc[...] = jnp.zeros(bacc.shape, f32)
    head_low = wfull[:, 2 * LANE : 3 * LANE]
    cls_pad = round_up(cls, 16)
    one_over_count = 1.0 / label_count[0:1, 0:1]
    class_iota = lax.broadcasted_iota(i32, (cls_pad, block), 0)

    def backward_block(level, off, joined, inverse, need_input):
        lanes = pl.ds(off, block)
        crossed = jnp.zeros((8, block), f32)
        for st in strips:
            u = ghid[st, :] * twice(vectors[3 + level, st, :], block)
            crossed = crossed + fold_rows(u * active[st, :])
        factor = jnp.sum(crossed, axis=0, keepdims=True) * (1.0 / hid) * inverse
        factor = factor * inverse * inverse
        low_parts = []
        for st in strips:
            g = ghid[st, :]
            a = active[st, :]
            u = g * twice(vectors[3 + level, st, :], block)
            low = ((inverse * u - a * factor) * slope[st, :]).astype(bf16)
            low_parts.append(low)
            gain_term = g * (a * inverse)
            bias_term = low.astype(f32)
            gain_sum = gain_term[:, 0:LANE]
            bias_sum = bias_term[:, 0:LANE]
            for j in range(1, block // LANE):
                gain_sum = gain_sum + gain_term[:, j * LANE : (j + 1) * LANE]
                bias_sum = bias_sum + bias_term[:, j * LANE : (j + 1) * LANE]
            gacc[level, st, :] += gain_sum
            bacc[level, st, :] += bias_sum
        low = jnp.concatenate(low_parts, axis=0)
        into = gfirst if level == 0 else gfull.at[level - 1]
        added = dot(low, joined, NT)
        for j in range(joined.shape[0] // LANE):
            into[j] += added[:, j * LANE : (j + 1) * LANE]
        if need_input:
            back = dot(matrix(level), low, TN)
            wide[:, lanes] = back[0:hid, :]
            gmean[:, lanes] = (back[hid:, :] * info[0:1, lanes]).astype(bf16)

    def layer_three(i, loss):
        off = pl.multiple_of(i * block, block)
        lanes = pl.ds(off, block)
        joined, inverse = forward_block(2, off, all_sums(table3, off), table3, None, None, True)
        last = jnp.concatenate([hidden_strip(2, st, inverse) for st in strips], axis=0)
        logits = dot(head_low, last, TN)[0:cls_pad, :]
        logits = jnp.where(class_iota < cls, logits, -jnp.inf)
        highest = jnp.max(logits, axis=0, keepdims=True)
        shifted = logits - highest
        grown = jnp.exp(shifted)
        total = jnp.sum(grown, axis=0, keepdims=True)
        hot = class_iota == info[1:2, lanes].astype(i32)
        counted = info[2:3, lanes]
        chosen = jnp.sum(jnp.where(hot, shifted, 0.0), axis=0, keepdims=True)
        loss = loss + (jnp.log(total) - chosen) * counted
        g_logits = (grown / total - jnp.where(hot, 1.0, 0.0)) * (counted * one_over_count)
        g_low = jnp.concatenate(
            [g_logits, jnp.zeros((LANE - cls_pad, block), f32)], axis=0
        ).astype(bf16)
        ghead[...] += dot(last, g_low, NT)
        ghid[...] = dot(head_low, g_low, NN)
        backward_block(2, off, joined, inverse, True)
        return loss

    loss = lax.fori_loop(0, blocks, layer_three, jnp.zeros((1, block), f32))

    def start_first(seg):
        for piece in range(n_group):
            gwire[seg, piece] = gfull[seg, piece].astype(wire)

        def start(i, carry):
            group = lax.rem(my_group + i, n_group)
            pltpu.make_async_remote_copy(
                src_ref=gwire.at[seg, group],
                dst_ref=recv1.at[seg, my_group],
                send_sem=g_ssem.at[0, seg],
                recv_sem=g_rsem.at[0, seg],
                device_id=target(group, my_shard),
                device_id_type=MESH,
            ).start()
            return carry

        lax.fori_loop(1, n_group, start, 0)
        recv1[seg, my_group] = jnp.zeros(recv1.shape[2:], wire)

    def start_second(seg):
        wait_bytes(gwire.at[seg, pl.ds(0, n_group - 1)], g_ssem.at[0, seg])
        wait_bytes(recv1.at[seg, pl.ds(0, n_group - 1)], g_rsem.at[0, seg])
        total = gfull[seg, my_group]
        for group in range(n_group):
            total = total + recv1[seg, group].astype(f32)
        gfull[seg, my_group] = total
        send2[seg] = total.astype(wire).reshape(n_shard, chunk, LANE)

        def start(i, carry):
            shard = lax.rem(my_shard + i, n_shard)
            pltpu.make_async_remote_copy(
                src_ref=send2.at[seg, shard],
                dst_ref=recv2.at[seg, my_shard],
                send_sem=g_ssem.at[1, seg],
                recv_sem=g_rsem.at[1, seg],
                device_id=target(my_group, shard),
                device_id_type=MESH,
            ).start()
            return carry

        lax.fori_loop(1, n_shard, start, 0)
        recv2[seg, my_shard] = jnp.zeros(recv2.shape[2:], wire)

    def start_third(seg):
        wait_bytes(send2.at[seg, pl.ds(0, n_shard - 1)], g_ssem.at[1, seg])
        wait_bytes(recv2.at[seg, pl.ds(0, n_shard - 1)], g_rsem.at[1, seg])
        total = gfull[seg, my_group, own_chunk, :]
        for shard in range(n_shard):
            total = total + recv2[seg, shard].astype(f32)
        part3[seg] = total

        def start(i, carry):
            group = lax.rem(my_group + i, n_group)
            pltpu.make_async_remote_copy(
                src_ref=part3.at[seg],
                dst_ref=recv3.at[seg, my_group],
                send_sem=g_ssem.at[2, seg],
                recv_sem=g_rsem.at[2, seg],
                device_id=target(group, my_shard),
                device_id_type=MESH,
            ).start()
            return carry

        lax.fori_loop(1, n_group, start, 0)
        recv3[seg, my_group] = total
        return jnp.sum(total * total)

    def wait_third(seg):
        for _ in range(n_group - 1):
            wait_bytes(part3.at[seg], g_ssem.at[2, seg])
        wait_bytes(recv3.at[seg, pl.ds(0, n_group - 1)], g_rsem.at[2, seg])

    def bias_and_gain(levels, first_lane):
        lane_wide = lax.broadcasted_iota(i32, (hid, LANE), 1)
        total = jnp.zeros((hid, LANE), f32)
        for n, level in enumerate(levels):
            for acc, shift in ((bacc, 0), (gacc, len(levels))):
                total = jnp.where(
                    lane_wide == first_lane + shift + n,
                    jnp.sum(acc[level], axis=1, keepdims=True),
                    total,
                )
        return total

    def start_head():
        total = ghead[...] + bias_and_gain((1, 2), cls)
        ghead[...] = total
        hwire[...] = total.astype(wire).reshape(n_shard, chunk, LANE)

        def start(i, carry):
            shard = lax.rem(my_shard + i, n_shard)
            pltpu.make_async_remote_copy(
                src_ref=hwire.at[shard],
                dst_ref=hrecv.at[my_shard],
                send_sem=h_ssem.at[0],
                recv_sem=h_rsem.at[0],
                device_id=target(my_group, shard),
                device_id_type=MESH,
            ).start()
            return carry

        lax.fori_loop(1, n_shard, start, 0)
        hrecv[my_shard] = jnp.zeros(hrecv.shape[1:], wire)

    def share_head():
        wait_bytes(hwire.at[pl.ds(0, n_shard - 1)], h_ssem.at[0])
        wait_bytes(hrecv.at[pl.ds(0, n_shard - 1)], h_rsem.at[0])
        total = ghead[own_chunk, :]
        for shard in range(n_shard):
            total = total + hrecv[shard].astype(f32)
        hpart[...] = total

        def start(i, carry):
            group = lax.rem(my_group + i, n_group)
            pltpu.make_async_remote_copy(
                src_ref=hpart,
                dst_ref=hfinal.at[my_group],
                send_sem=h_ssem.at[1],
                recv_sem=h_rsem.at[1],
                device_id=target(group, my_shard),
                device_id_type=MESH,
            ).start()
            return carry

        lax.fori_loop(1, n_group, start, 0)
        hfinal[my_group] = total

    def wait_head():
        wait_bytes(hfinal.at[pl.ds(0, n_group - 1)], h_ssem.at[1])
        wait_bytes(hfinal.at[pl.ds(0, n_group - 1)], h_rsem.at[1])
        total = hfinal[0]
        for group in range(1, n_group):
            total = total + hfinal[group]
        head_out[...] = total
        return jnp.sum(total * total) * (1.0 / n_group)

    units, unit_rows, row_parts_first = cfg["units"], cfg["unit_rows"], cfg["units"] // 2

    def start_first_layer():
        gfirst[0] += bias_and_gain((0,), fin)
        for unit in range(units):
            tile, part = unit // row_parts_first, unit % row_parts_first
            whole = gfirst[tile].reshape(n_shard, chunk, LANE)
            fwire[unit] = whole[:, part * unit_rows : (part + 1) * unit_rows, :].astype(wire)

        def start(i, carry):
            peer = lax.rem(me + i, devices)
            group, shard = lax.div(peer, n_shard), lax.rem(peer, n_shard)
            pltpu.make_async_remote_copy(
                src_ref=fwire.at[lax.rem(group, units), shard],
                dst_ref=frecv.at[me],
                send_sem=f_ssem.at[0],
                recv_sem=f_rsem.at[0],
                device_id=target(group, shard),
                device_id_type=MESH,
            ).start()
            return carry

        lax.fori_loop(1, devices, start, 0)
        frecv[me] = fwire[lax.rem(my_group, units), my_shard]

    def share_first_layer():
        wait_bytes(frecv.at[pl.ds(0, devices - 1)], f_ssem.at[0])
        wait_bytes(frecv.at[pl.ds(0, devices - 1)], f_rsem.at[0])
        total = jnp.sum(frecv[...].astype(f32), axis=0)
        fpart[...] = total

        def start(i, carry):
            group = lax.rem(my_group + i, n_group)
            pltpu.make_async_remote_copy(
                src_ref=fpart,
                dst_ref=ffinal.at[my_group],
                send_sem=f_ssem.at[1],
                recv_sem=f_rsem.at[1],
                device_id=target(group, my_shard),
                device_id_type=MESH,
            ).start()
            return carry

        lax.fori_loop(1, n_group, start, 0)
        ffinal[my_group] = total
        return jnp.sum(total * total) * (units / n_group)

    def wait_first_layer():
        wait_bytes(ffinal.at[pl.ds(0, n_group - 1)], f_ssem.at[1])
        wait_bytes(ffinal.at[pl.ds(0, n_group - 1)], f_rsem.at[1])
        for unit in range(units):
            tile, part = unit // row_parts_first, unit % row_parts_first
            first_out[tile, part * unit_rows : (part + 1) * unit_rows, :] = ffinal[unit]

    def exchange_backward(x, meanwhile):
        for rows in row_parts:
            lanes = slice(nodes + rows.start, nodes + rows.stop)
            back = dot(gmean[...], counts[:, lanes].astype(bf16), NN)
            outs[rows, :] = back.astype(bf16).T
        start_rows(outs, ins.at[x % 2], row_ssem.at[x + 1], row_rsem.at[x + 1])
        meanwhile()

        def add(i, carry):
            off = pl.multiple_of(i * block, block)
            lanes = pl.ds(off, block)
            wide[:, lanes] += dot(gmean[...], counts[:, lanes].astype(bf16), NN)
            return carry

        lax.fori_loop(0, blocks, add, 0)
        wait_rows(outs, ins.at[x % 2], row_ssem.at[x + 1], row_rsem.at[x + 1])

    def returned(x, off):
        total = wide[:, pl.ds(off, block)]
        for rows in row_parts:
            total = total + dot(ins[x % 2, rows, :], picks(rows, off), TN)
        return total

    exchange_backward(2, lambda: start_first(1))
    start_second(1)

    def backward_two(i, carry):
        off = pl.multiple_of(i * block, block)
        lanes = pl.ds(off, block)
        ghid[...] = returned(2, off)
        joined = jnp.concatenate([table2[:, lanes], mean2[:, lanes]], axis=0)
        if before2.shape[1] < nodes:
            before[...] = dot(matrix(1), joined, NN)
        inverse = activate(1, True, kept_or_none(before2), off)
        backward_block(1, off, joined, inverse, True)
        return carry

    lax.fori_loop(0, blocks, backward_two, 0)

    def meanwhile():
        start_first(0)
        start_head()

    exchange_backward(3, meanwhile)
    square = start_third(1)
    start_second(0)
    share_head()

    def backward_one(i, carry):
        off = pl.multiple_of(i * block, block)
        lanes = pl.ds(off, block)
        ghid[...] = returned(3, off)
        joined = jnp.concatenate([table1[:, lanes], mean1[:, lanes]], axis=0)
        if before1.shape[1] < nodes:
            before[...] = dot(matrix(0), joined, NN)
        inverse = activate(0, True, kept_or_none(before1), off)
        backward_block(0, off, joined, inverse, False)
        return carry

    lax.fori_loop(0, blocks, backward_one, 0)
    start_first_layer()
    square = square + start_third(0) + wait_head()
    square = square + share_first_layer()

    lane_of = lax.broadcasted_iota(i32, (8, LANE), 1)
    mine = jnp.where(lane_of == 0, square, jnp.where(lane_of == 1, jnp.sum(loss), 0.0))
    scal_send[...] = mine

    def send_scalars(i, carry):
        peer = lax.rem(me + i, devices)
        pltpu.make_async_remote_copy(
            src_ref=scal_send.at[pl.ds(0, 1), :],
            dst_ref=scal_recv.at[pl.ds(me, 1), :],
            send_sem=s_ssem,
            recv_sem=s_rsem,
            device_id=target(lax.div(peer, n_shard), lax.rem(peer, n_shard)),
            device_id_type=MESH,
        ).start()
        return carry

    lax.fori_loop(1, devices, send_scalars, 0)
    scal_recv[pl.ds(me, 1), :] = mine[0:1, :]
    for seg in range(2):
        wait_third(seg)
    part_out[...] = recv3[...]
    wait_first_layer()
    wait_bytes(scal_recv.at[pl.ds(0, devices - 1), :], s_rsem)
    wait_bytes(scal_recv.at[pl.ds(0, devices - 1), :], s_ssem)
    totals = jnp.sum(scal_recv[...], axis=0, keepdims=True)
    scalar_out[...] = jnp.where(lane_of == 2, label_count[0:1, 0:1], totals)


def adamw(weight, grad, moment, square, rate, decay):
    moment_new = beta_one * moment + (1.0 - beta_one) * grad
    square_new = beta_two * square + (1.0 - beta_two) * grad * grad
    moment_hat = moment_new / (1.0 - beta_one**STEP)
    square_hat = square_new / (1.0 - beta_two**STEP)
    weight_new = weight - rate * (
        moment_hat / (jnp.sqrt(square_hat) + adam_epsilon) + decay * weight
    )
    return (weight_new, moment_new, square_new)


def update_kernel(fin, cls, part_ref, head_ref, first_ref, scalar_ref, *refs):
    states = [refs[3 * k : 3 * k + 3] for k in range(5)]
    outs = [refs[15 + 3 * k : 18 + 3 * k] for k in range(5)]
    copies = refs[30:33]
    loss_out, count_out, norm_out = refs[33:36]
    norm = jnp.sqrt(scalar_ref[0:1, 0:1])
    loss_out[...] = scalar_ref[0:1, 1:2]
    count_out[...] = scalar_ref[0:1, 2:3]
    norm_out[...] = norm
    factor = jnp.minimum(1.0, threshold / norm)
    small_last = head_ref[...].T
    small_first = first_ref[0].T
    bias = jnp.concatenate([small_first[fin : fin + 1], small_last[cls : cls + 2]], axis=0)
    gain = jnp.concatenate(
        [small_first[fin + 1 : fin + 2], small_last[cls + 2 : cls + 4]], axis=0
    )

    def update(k, grad, where, rate, decay):
        news = adamw(
            states[k][0][where], grad * factor, states[k][1][where], states[k][2][where], rate, decay
        )
        for out, new in zip(outs[k], news):
            out[where] = new
        if k < 3:
            copies[k][where] = news[0].astype(bf16)

    everything = (slice(None), slice(None))
    update(0, first_ref[0][:, 0:fin], (slice(None), slice(0, fin)), 0.05, 0.01)
    update(0, first_ref[1][:, 0:fin], (slice(None), slice(fin, 2 * fin)), 0.05, 0.01)
    n_group = part_ref.shape[1]
    for level in range(2):
        for piece in range(n_group):
            lanes = slice(piece * LANE, (piece + 1) * LANE)
            update(1, part_ref[level, piece], (level, slice(None), lanes), 0.05, 0.01)
    update(2, head_ref[:, 0:cls], everything, 0.05, 0.01)
    update(3, bias, everything, 0.3, 0.0)
    update(4, gain, everything, 0.3, 0.0)


def per_device(
    n_group,
    n_shard,
    features,
    node_counts,
    degrees,
    neighbours,
    send_rows,
    labels,
    train_mask,
    weight_first,
    weight_rest,
    weight_head,
    biases,
    gains,
    moment_first,
    square_first,
    moment_rest,
    square_rest,
    moment_head,
    square_head,
    moment_bias,
    square_bias,
    moment_gain,
    square_gain,
):
    nodes, fin = features.shape
    devices = n_group * n_shard
    hid = weight_rest.shape[1] // 2
    chunk = hid // n_shard
    cls = weight_head.shape[1]
    cap = send_rows.shape[1]
    slots = neighbours.shape[1]
    pad = round_up(cap + 2, 16)
    remote = devices * pad
    columns = nodes + remote
    block = 1024 if remote <= 512 else 512
    wire = bf16 if chunk % 16 == 0 else f32
    least = 16 if wire == bf16 else 8
    units = n_group if chunk * 2 // n_group >= least else 2
    unit_rows = chunk * 2 // units
    fin_pad = LANE
    cfg = dict(
        n_group=n_group,
        n_shard=n_shard,
        nodes=nodes,
        fin=fin,
        cls=cls,
        pad=pad,
        remote=remote,
        chunk=chunk,
        wire=wire,
        block=block,
        fin_pad=fin_pad,
        hid=hid,
        units=units,
        unit_rows=unit_rows,
    )

    away = neighbours - nodes
    source = away // cap
    moved = nodes + source * pad + (away - source * cap)
    mapped = jnp.where(away < 0, neighbours, moved)
    live = lax.broadcasted_iota(i32, mapped.shape, 1) < degrees[:, None]
    keys = jnp.where(live, mapped, -1).reshape(nodes // 16, 16 * slots)
    send_padded = jnp.pad(send_rows, ((0, 0), (0, pad - cap)), constant_values=-1)
    send_wide = jnp.broadcast_to(send_padded.reshape(remote, 1), (remote, LANE))

    vmem = pl.BlockSpec(memory_space=pltpu.VMEM)
    smem = pl.BlockSpec(memory_space=pltpu.SMEM)
    width = 4 * LANE + 4 * hid
    dma = pltpu.SemaphoreType.DMA
    stored = remote if remote <= 512 else 32
    kept_nodes = nodes if remote <= 512 else LANE
    scratch = [
        pltpu.VMEM((nodes, columns), narrow),
        pltpu.VMEM((stored, nodes), narrow),
        pltpu.VMEM((fin_pad, nodes), bf16),
        pltpu.VMEM((hid, columns), bf16),
        pltpu.VMEM((hid, columns), bf16),
        pltpu.VMEM((2 * fin_pad, nodes), narrow),
        pltpu.VMEM((2 * fin_pad, remote), narrow),
        pltpu.VMEM((fin_pad, nodes), bf16),
        pltpu.VMEM((hid, nodes), bf16),
        pltpu.VMEM((hid, kept_nodes), f32),
        pltpu.VMEM((hid, kept_nodes), f32),
        pltpu.VMEM((hid, nodes), bf16),
        pltpu.VMEM((hid, nodes), f32),
        pltpu.VMEM((remote, fin_pad), bf16),
        pltpu.VMEM((remote, fin_pad), bf16),
        pltpu.VMEM((remote, hid), bf16),
        pltpu.VMEM((2, remote, hid), bf16),
        pltpu.VMEM((8, nodes), f32),
        pltpu.VMEM((chunk, width), wire),
        pltpu.VMEM((hid, width), wire),
        pltpu.VMEM((hid, width), bf16),
        pltpu.VMEM((6, hid, LANE), f32),
        pltpu.VMEM((hid, block), f32),
        pltpu.VMEM((hid, block), f32),
        pltpu.VMEM((hid, block), f32),
        pltpu.VMEM((hid, block), f32),
        pltpu.VMEM((3, hid, LANE), f32),
        pltpu.VMEM((3, hid, LANE), f32),
        pltpu.VMEM((2, n_group, hid, LANE), f32),
        pltpu.VMEM((2, n_group, hid, LANE), wire),
        pltpu.VMEM((2, n_group, hid, LANE), wire),
        pltpu.VMEM((2, n_shard, chunk, LANE), wire),
        pltpu.VMEM((2, n_shard, chunk, LANE), wire),
        pltpu.VMEM((2, chunk, LANE), f32),
        pltpu.VMEM((2, n_group, chunk, LANE), f32),
        pltpu.VMEM((2, hid, LANE), f32),
        pltpu.VMEM((units, n_shard, unit_rows, LANE), wire),
        pltpu.VMEM((devices, unit_rows, LANE), wire),
        pltpu.VMEM((unit_rows, LANE), f32),
        pltpu.VMEM((n_group, unit_rows, LANE), f32),
        pltpu.VMEM((hid, LANE), f32),
        pltpu.VMEM((n_shard, chunk, LANE), wire),
        pltpu.VMEM((n_shard, chunk, LANE), wire),
        pltpu.VMEM((chunk, LANE), f32),
        pltpu.VMEM((n_group, chunk, LANE), f32),
        pltpu.VMEM((8, LANE), f32),
        pltpu.VMEM((devices, LANE), f32),
        dma((5,)),
        dma((5,)),
        dma((3,)),
        dma((3,)),
        dma((3, 2)),
        dma((3, 2)),
        dma((2,)),
        dma((2,)),
        dma((2,)),
        dma((2,)),
        dma,
        dma,
    ]
    sums = pl.pallas_call(
        functools.partial(step_kernel, cfg),
        out_shape=(
            jax.ShapeDtypeStruct((2, n_group, chunk, LANE), f32),
            jax.ShapeDtypeStruct((chunk, LANE), f32),
            jax.ShapeDtypeStruct((2, chunk, LANE), f32),
            jax.ShapeDtypeStruct((8, LANE), f32),
        ),
        in_specs=[vmem] * 5 + [smem] + [vmem] * 6,
        out_specs=(vmem,) * 4,
        scratch_shapes=scratch,
        compiler_params=pltpu.CompilerParams(
            collective_id=0, has_side_effects=True, vmem_limit_bytes=63 * 2**20
        ),
    )(
        features.T,
        keys,
        degrees.reshape(nodes // LANE, LANE),
        labels.reshape(nodes // LANE, LANE),
        train_mask.reshape(nodes // LANE, LANE),
        node_counts,
        send_wide,
        weight_first.T,
        weight_rest.transpose(0, 2, 1),
        weight_head,
        biases,
        gains,
    )
    turned = lambda value: value.T
    turned_rest = lambda value: value.transpose(0, 2, 1)
    same = lambda value: value
    turns = (turned, turned_rest, same, same, same)
    states = (
        (weight_first, moment_first, square_first),
        (weight_rest, moment_rest, square_rest),
        (weight_head, moment_head, square_head),
        (biases, moment_bias, square_bias),
        (gains, moment_gain, square_gain),
    )
    flat = [turn(value) for turn, three in zip(turns, states) for value in three]
    shapes = [jax.ShapeDtypeStruct(value.shape, f32) for value in flat]
    shapes += [jax.ShapeDtypeStruct(flat[3 * k].shape, bf16) for k in range(3)]
    shapes += [jax.ShapeDtypeStruct((1, 1), f32)] * 3
    updated = pl.pallas_call(
        functools.partial(update_kernel, fin, cls),
        out_shape=tuple(shapes),
        in_specs=[vmem] * (4 + len(flat)),
        out_specs=(vmem,) * len(shapes),
    )(*sums, *flat)
    news = tuple(turns[k // 3](updated[k]) for k in range(15))
    copies = tuple(turns[k](updated[15 + k]) for k in range(3))
    return tuple(value.reshape(()) for value in updated[18:]) + news + copies


def solution(mesh):
    nodes_split = P(("group", "shard"))
    nodes_rows = P(("group", "shard"), None)
    first = P(None, "shard")
    rest = P(None, None, "shard")
    head = P("shard", None)
    return jax.shard_map(
        functools.partial(per_device, mesh.shape["group"], mesh.shape["shard"]),
        mesh=mesh,
        in_specs=(
            nodes_rows,
            nodes_split,
            nodes_split,
            nodes_rows,
            nodes_rows,
            nodes_split,
            nodes_split,
            first,
            rest,
            head,
            first,
            first,
            first,
            first,
            rest,
            rest,
            head,
            head,
            first,
            first,
            first,
            first,
        ),
        out_specs=(P(), P(), P())
        + (first,) * 3
        + (rest,) * 3
        + (head,) * 3
        + (first,) * 6
        + (first, rest, head),
        check_vma=False,
    )
```

```python
import functools

import jax
import jax.numpy as jnp
from jax import lax
from jax.experimental import pallas as pl
from jax.experimental.pallas import tpu as pltpu
from jax.sharding import PartitionSpec as P

STEP = 10
MESH = pl.DeviceIdType.MESH
bf16 = jnp.bfloat16
f32 = jnp.float32
i32 = jnp.int32

norm_epsilon = 1e-05
threshold = 0.002
beta_one = 0.5
beta_two = 0.5
adam_epsilon = 1e-08

LANE = 128
LOW = 256
narrow = jnp.float8_e4m3fn
STRIP = 32

NN = (((1,), (0,)), ((), ()))
NT = (((1,), (1,)), ((), ()))
TN = (((0,), (0,)), ((), ()))


def dot(a, b, dims):
    return lax.dot_general(a, b, dims, preferred_element_type=f32)


def round_up(value, unit):
    return -(-value // unit) * unit


def twice(half, width):
    return jnp.concatenate([half] * (width // LANE), axis=1)


def step_kernel(
    cfg,
    feat_ref,
    neighbour_ref,
    deg_ref,
    label_ref,
    mask_ref,
    count_ref,
    send_ref,
    first_ref,
    rest_ref,
    head_ref,
    bias_ref,
    gain_ref,
    part_out,
    head_out,
    first_out,
    scalar_out,
    counts,
    picked,
    send_columns,
    slot_rows,
    key_high,
    key_low,
    table1,
    table2,
    table3,
    first_own,
    first_remote,
    mean1,
    mean2,
    before1,
    before2,
    gmean,
    wide,
    outs,
    ins,
    info,
    wsend,
    wwire,
    wfull,
    vectors,
    before,
    active,
    slope,
    ghid,
    gacc,
    bacc,
    gfull,
    gwire,
    recv1,
    send2,
    recv2,
    part3,
    recv3,
    gfirst,
    fwire,
    frecv,
    fpart,
    ffinal,
    ghead,
    hwire,
    hrecv,
    hpart,
    hfinal,
    scal_send,
    scal_recv,
    row_ssem,
    row_rsem,
    w_ssem,
    w_rsem,
    g_ssem,
    g_rsem,
    f_ssem,
    f_rsem,
    h_ssem,
    h_rsem,
    s_ssem,
    s_rsem,
):
    n_group, n_shard = cfg["n_group"], cfg["n_shard"]
    nodes, fin, cls = cfg["nodes"], cfg["fin"], cfg["cls"]
    pad, remote, chunk, wire = cfg["pad"], cfg["remote"], cfg["chunk"], cfg["wire"]
    block, fin_pad, hid = cfg["block"], cfg["fin_pad"], cfg["hid"]
    devices = n_group * n_shard
    columns = nodes + remote
    my_group, my_shard = lax.axis_index("group"), lax.axis_index("shard")
    me = my_group * n_shard + my_shard
    blocks = nodes // block

    def target(group, shard):
        return {"group": group, "shard": shard}

    out1, in1 = outs.at[:, pl.ds(0, fin_pad)], ins.at[1, :, pl.ds(0, fin_pad)]

    barrier = pltpu.get_barrier_semaphore()

    def greet(i, carry):
        peer = lax.rem(me + i, devices)
        pl.semaphore_signal(
            barrier,
            inc=1,
            device_id=target(lax.div(peer, n_shard), lax.rem(peer, n_shard)),
            device_id_type=MESH,
        )
        return carry

    lax.fori_loop(1, devices, greet, 0)

    def start_rows(source, landing, ssem, rsem):
        def start(i, carry):
            peer = lax.rem(me + i, devices)
            pltpu.make_async_remote_copy(
                src_ref=source.at[pl.ds(pl.multiple_of(peer * pad, pad), pad), :],
                dst_ref=landing.at[pl.ds(pl.multiple_of(me * pad, pad), pad), :],
                send_sem=ssem,
                recv_sem=rsem,
                device_id=target(lax.div(peer, n_shard), lax.rem(peer, n_shard)),
                device_id_type=MESH,
            ).start()
            return carry

        lax.fori_loop(1, devices, start, 0)
        own = pl.ds(pl.multiple_of(me * pad, pad), pad)
        landing[own, :] = source[own, :]

    def wait_bytes(ref, sem):
        pltpu.make_async_copy(ref, ref, sem).wait()

    def wait_rows(source, landing, ssem, rsem):
        rows = pl.ds(0, (devices - 1) * pad)
        wait_bytes(source.at[rows, :], ssem)
        wait_bytes(landing.at[rows, :], rsem)

    some = min(remote, 512)
    row_parts = [slice(r, r + some) for r in range(0, remote, some)]

    def make_picks(rows, off, width):
        lanes = lax.broadcasted_iota(i32, (some, LANE), 1) + off
        parts = [
            jnp.where(send_columns[rows, :] == lanes + LANE * j, 1.0, 0.0).astype(bf16)
            for j in range(width // LANE)
        ]
        return jnp.concatenate(parts, axis=1)

    def picks(rows, off):
        if picked.shape[0] == remote:
            return picked[rows, pl.ds(off, block)].astype(bf16)
        return make_picks(rows, off, block)

    def pick_rows(table, into):
        for rows in row_parts:
            if picked.shape[0] == remote:
                total = dot(picked[rows, :].astype(bf16), table[:, 0:nodes], NT)
            else:

                def add(i, total):
                    off = pl.multiple_of(i * block, block)
                    return total + dot(picks(rows, off), table[:, pl.ds(off, block)], NT)

                total = lax.fori_loop(0, blocks, add, jnp.zeros((some, table.shape[0]), f32))
            into[rows, :] = total.astype(bf16)

    total_counted = jnp.zeros((1, LANE), f32)
    lane_row = lax.broadcasted_iota(i32, (1, LANE), 1)
    for r in range(nodes // LANE):
        lanes = slice(r * LANE, (r + 1) * LANE)
        degree = deg_ref[r : r + 1, :].astype(f32)
        info[0:1, lanes] = 1.0 / degree
        info[3:4, lanes] = degree
        info[1:2, lanes] = label_ref[r : r + 1, :].astype(f32)
        counted = jnp.where(
            (lane_row + r * LANE < count_ref[0]) & (mask_ref[r : r + 1, :] > 0), 1.0, 0.0
        )
        info[2:3, lanes] = counted
        total_counted = total_counted + counted
    my_count = jnp.sum(total_counted, axis=1, keepdims=True)
    count_high = jnp.floor(my_count * (1.0 / 256.0))
    count_low = my_count - 256.0 * count_high

    table1[fin // 16 * 16 :, :] = jnp.zeros((fin_pad - fin // 16 * 16, nodes), bf16)
    table1[0:fin, :] = feat_ref[...]

    def split_in_two(value, into):
        value = value.astype(f32)
        largest = jnp.max(jnp.abs(value), axis=1, keepdims=True)
        scale = jnp.ones_like(largest)
        for power in (32, 16, 8, 4, 2, 1):
            larger = scale * 2.0**power
            scale = jnp.where(largest * larger <= 448.0, larger, scale)
        scaled = value * scale
        high = scaled.astype(narrow)
        into[0:fin_pad, :] = high
        into[fin_pad:, :] = ((scaled - high.astype(f32)) * 16.0).astype(narrow)
        return 1.0 / scale

    def joined_parts(both, unscale):
        return (both[0:fin_pad, :] + both[fin_pad:, :] * (1.0 / 16.0)) * unscale

    cap, slots = cfg["cap"], cfg["slots"]
    numbers = jnp.concatenate(
        [send_ref[...], jnp.full((pad - cap, devices), -256, i32)], axis=0
    )
    halves = jnp.concatenate([numbers >> 8, numbers & 255], axis=0).astype(f32).astype(bf16)
    for rows in row_parts:
        peers = lax.broadcasted_iota(i32, (some, devices), 1)
        row_numbers = lax.broadcasted_iota(i32, (some, devices), 0) + rows.start
        chosen = jnp.where(lax.div(row_numbers, pad) == peers, 1.0, 0.0).astype(bf16)
        found = dot(chosen, halves, NT)
        lanes = lax.broadcasted_iota(i32, (some, 2 * pad), 1)
        place = lax.rem(lax.broadcasted_iota(i32, (some, 2 * pad), 0), pad)
        found = jnp.where(lanes < pad, 256.0 * found, found)
        found = jnp.where(lax.rem(lanes, pad) == place, found, 0.0)
        column = jnp.sum(found, axis=1, keepdims=True).astype(i32)
        send_columns[rows, :] = jnp.broadcast_to(column, (some, LANE))

    wsend[...] = jnp.zeros(wsend.shape, wire)
    wsend[:, 0:fin] = first_ref[:, 0:fin].astype(bf16).astype(wire)
    wsend[:, LANE : LANE + fin] = first_ref[:, fin : 2 * fin].astype(bf16).astype(wire)
    wsend[:, 3 * LANE + 4 * hid : 3 * LANE + 4 * hid + cls] = head_ref[...].astype(bf16).astype(wire)
    small = jnp.concatenate(
        [bias_ref[...], gain_ref[...], jnp.zeros((2, chunk), f32)], axis=0
    )
    wsend[:, 2 * LANE : 2 * LANE + 8] = small.T.astype(bf16).astype(wire)
    for level in range(2):
        lanes = slice(3 * LANE + level * 2 * hid, 3 * LANE + (level + 1) * 2 * hid)
        wsend[:, lanes] = rest_ref[level].astype(bf16).astype(wire)

    if picked.shape[0] == remote:

        def store_picks(i, carry):
            off = pl.multiple_of(i * 512, 512)
            picked[:, pl.ds(off, 512)] = make_picks(row_parts[0], off, 512).astype(narrow)
            return carry

        lax.fori_loop(0, nodes // 512, store_picks, 0)

    pick_rows(table1, out1)
    spare = lax.rem(lax.broadcasted_iota(i32, (remote, fin_pad), 0), pad)
    sent = out1[...].astype(f32)
    sent = jnp.where(spare == pad - 2, count_high, sent)
    sent = jnp.where(spare == pad - 1, count_low, sent)
    out1[...] = sent.astype(bf16)

    own_chunk = pl.ds(pl.multiple_of(my_shard * chunk, chunk), chunk)
    weight_parts = (
        slice(0, 3 * LANE),
        slice(3 * LANE, 3 * LANE + 2 * hid),
        slice(3 * LANE + 2 * hid, 4 * LANE + 4 * hid),
    )

    def send_weights(part):
        lanes = weight_parts[part]

        def start(i, carry):
            shard = lax.rem(my_shard + i, n_shard)
            pltpu.make_async_remote_copy(
                src_ref=wsend.at[:, lanes],
                dst_ref=wwire.at[own_chunk, lanes],
                send_sem=w_ssem.at[part],
                recv_sem=w_rsem.at[part],
                device_id=target(my_group, shard),
                device_id_type=MESH,
            ).start()
            return carry

        lax.fori_loop(1, n_shard, start, 0)

    def wait_weights(part):
        lanes = weight_parts[part]
        rows = pl.ds(0, (n_shard - 1) * chunk)
        wait_bytes(wwire.at[rows, lanes], w_rsem.at[part])
        wait_bytes(wwire.at[rows, lanes], w_ssem.at[part])
        wfull[:, lanes] = wwire[:, lanes].astype(bf16)

    pl.semaphore_wait(barrier, devices - 1)
    start_rows(out1, in1, row_ssem.at[0], row_rsem.at[0])
    wwire[own_chunk, :] = wsend[...]
    send_weights(0)

    tiles = nodes // LANE
    for g in range(tiles):
        lanes = slice(g * LANE, (g + 1) * LANE)
        column = neighbour_ref[:, lanes]
        away = column - nodes
        source = ((away.astype(f32) + 0.5) * (1.0 / cap)).astype(i32)
        moved = jnp.where(away < 0, column, column + source * (pad - cap))
        live = lax.broadcasted_iota(i32, (slots, LANE), 0).astype(f32) < info[3:4, lanes]
        slot_rows[g * slots : (g + 1) * slots, :] = jnp.where(live, moved, -256)
    per_half = LANE // 16
    sixteenth = lax.div(lax.broadcasted_iota(i32, (tiles, LANE), 1), 16)
    for half in range(slots // per_half):
        made = [jnp.zeros((tiles, LANE), i32)] * per_half
        for j in range(per_half):
            rows = slot_rows[pl.ds(half * per_half + j, tiles, stride=slots), :]
            here = sixteenth == j
            for b in range(per_half):
                turned = pltpu.roll(rows, 16 * ((j - b) % per_half), 1) if j != b else rows
                made[b] = jnp.where(here, turned, made[b])
        lanes = slice(half * LANE, (half + 1) * LANE)
        for b in range(per_half):
            key_high[b, :, lanes] = (made[b] >> 8).astype(f32)
            key_low[b, :, lanes] = (made[b] & 255).astype(f32)

    high_rows = columns // LOW
    low_iota = lax.broadcasted_iota(i32, (LOW, LOW), 0).astype(f32).astype(bf16)
    same_node = (
        lax.rem(lax.broadcasted_iota(i32, (16, LOW), 1), 16)
        == lax.broadcasted_iota(i32, (16, LOW), 0)
    ).astype(f32).astype(bf16)
    zero_tile = jnp.zeros((16, LOW), bf16)
    one_low = jnp.ones((LOW, LOW), bf16)
    zero_low = jnp.zeros((LOW, LOW), bf16)
    group_rows = 32
    fold = group_rows // 16

    def build(it, carry):
        for k in range(0, 8, fold):
            made = []
            for kk in range(k, k + fold):
                high_row = jnp.broadcast_to(key_high[kk, pl.ds(it, 1), :], (16, LOW)).astype(bf16)
                low_row = jnp.broadcast_to(key_low[kk, pl.ds(it, 1), :], (16, LOW)).astype(bf16)
                left = jnp.concatenate(
                    [
                        jnp.where(high_row == jnp.asarray(h, bf16), same_node, zero_tile)
                        for h in range(high_rows)
                    ],
                    axis=0,
                ).astype(narrow)
                right = jnp.where(
                    low_iota == jnp.concatenate([low_row] * (LOW // 16), axis=0),
                    one_low,
                    zero_low,
                ).astype(narrow)
                made.append(dot(left, right, NT))
            row = pl.multiple_of(it * 128 + k * 16, group_rows)
            for h in range(high_rows):
                tile = jnp.concatenate([m[h * 16 : h * 16 + 16, :] for m in made], axis=0)
                counts[pl.ds(row, group_rows), h * LOW : (h + 1) * LOW] = tile.astype(
                    counts.dtype
                )
        return carry

    unscale_own = split_in_two(table1[...], first_own)
    lax.fori_loop(0, nodes // 128, build, 0)

    wait_weights(0)
    weight_lanes = (
        slice(0, 2 * LANE),
        weight_parts[1],
        slice(3 * LANE + 2 * hid, 3 * LANE + 4 * hid),
    )
    small_full = wfull[:, 2 * LANE : 3 * LANE].astype(f32)
    for v in range(6):
        vectors[v] = jnp.broadcast_to(small_full[:, v : v + 1], (hid, LANE))

    def matrix(level):
        return wfull[:, weight_lanes[level]]

    wait_rows(out1, in1, row_ssem.at[0], row_rsem.at[0])
    received = in1[...].astype(f32)
    scale = jnp.where(spare == pad - 2, 256.0, jnp.where(spare == pad - 1, 1.0, 0.0))
    label_count = jnp.sum(received * scale, axis=0, keepdims=True)
    unscale_remote = split_in_two(
        jnp.where(spare < pad - 2, received, 0.0).T, first_remote
    )

    def c_block(off, lanes):
        return counts[pl.ds(off, block), lanes].astype(bf16)

    strips = [slice(r, r + STRIP) for r in range(0, hid, STRIP)]

    def fold_rows(value):
        return jnp.sum(value.reshape(STRIP // 8, 8, value.shape[1]), axis=0)

    def activate(level, keep_slope, kept, off):
        squares = jnp.zeros((8, block), f32)
        for st in strips:
            if kept is not None and keep_slope:
                b = kept[st, pl.ds(off, block)]
            else:
                b = before[st, :] + twice(vectors[level, st, :], block)
            if kept is not None and not keep_slope:
                kept[st, pl.ds(off, block)] = b
            s = 0.5 + 0.5 * jnp.tanh(0.5 * b)
            a = b * s
            active[st, :] = a
            if keep_slope:
                slope[st, :] = s + a * (1.0 - s)
            squares = squares + fold_rows(a * a)
        mean_square = jnp.sum(squares, axis=0, keepdims=True) * (1.0 / hid)
        return lax.rsqrt(mean_square + norm_epsilon)

    def hidden_strip(level, st, inverse):
        return (twice(vectors[3 + level, st, :], block) * (active[st, :] * inverse)).astype(bf16)

    def kept_or_none(kept):
        return kept if kept is not None and kept.shape[1] == nodes else None

    def forward_block(level, off, summed, table, mean, kept, keep_slope):
        lanes = pl.ds(off, block)
        mean_low = (summed * info[0:1, lanes]).astype(bf16)
        if mean is not None:
            mean[:, lanes] = mean_low
        joined = jnp.concatenate([table[:, lanes], mean_low], axis=0)
        before[...] = dot(matrix(level), joined, NN)
        return joined, activate(level, keep_slope, kept_or_none(kept), off)

    send_weights(1)
    def layer_one(i, carry):
        off = pl.multiple_of(i * block, block)
        own = dot(first_own[...], counts[pl.ds(off, block), 0:nodes], NT)
        away = dot(first_remote[...], counts[pl.ds(off, block), nodes:], NT)
        summed = joined_parts(own, unscale_own) + joined_parts(away, unscale_remote)
        _, inverse = forward_block(0, off, summed, table1, mean1, before1, False)
        for st in strips:
            table2[st, pl.ds(off, block)] = hidden_strip(0, st, inverse)
        return carry

    lax.fori_loop(0, blocks, layer_one, 0)

    def own_sums(table):
        def add(i, carry):
            off = pl.multiple_of(i * block, block)
            wide[:, pl.ds(off, block)] = dot(
                table[:, 0:nodes], c_block(off, slice(0, nodes)), NT
            )
            return carry

        lax.fori_loop(0, blocks, add, 0)

    def exchange_forward(table, x):
        pick_rows(table, outs)
        start_rows(outs, ins.at[x % 2], row_ssem.at[x + 1], row_rsem.at[x + 1])
        if x == 0:
            send_weights(2)
        own_sums(table)
        wait_rows(outs, ins.at[x % 2], row_ssem.at[x + 1], row_rsem.at[x + 1])
        table[:, nodes:] = ins[x % 2].T

    def all_sums(table, off):
        return wide[:, pl.ds(off, block)] + dot(
            table[:, nodes:], c_block(off, slice(nodes, columns)), NT
        )

    exchange_forward(table2, 0)
    wait_weights(1)

    def layer_two(i, carry):
        off = pl.multiple_of(i * block, block)
        _, inverse = forward_block(1, off, all_sums(table2, off), table2, mean2, before2, False)
        for st in strips:
            table3[st, pl.ds(off, block)] = hidden_strip(1, st, inverse)
        return carry

    lax.fori_loop(0, blocks, layer_two, 0)

    exchange_forward(table3, 1)
    wait_weights(2)
    gfirst[...] = jnp.zeros(gfirst.shape, f32)
    ghead[...] = jnp.zeros(ghead.shape, f32)
    gfull[...] = jnp.zeros(gfull.shape, f32)
    gacc[...] = jnp.zeros(gacc.shape, f32)
    bacc[...] = jnp.zeros(bacc.shape, f32)
    head_low = wfull[:, 3 * LANE + 4 * hid :]
    cls_pad = round_up(cls, 16)
    one_over_count = 1.0 / label_count[0:1, 0:1]
    class_iota = lax.broadcasted_iota(i32, (cls_pad, block), 0)

    def backward_block(level, off, joined, inverse, need_input):
        lanes = pl.ds(off, block)
        crossed = jnp.zeros((8, block), f32)
        for st in strips:
            u = ghid[st, :] * twice(vectors[3 + level, st, :], block)
            crossed = crossed + fold_rows(u * active[st, :])
        factor = jnp.sum(crossed, axis=0, keepdims=True) * (1.0 / hid) * inverse
        factor = factor * inverse * inverse
        low_parts = []
        for st in strips:
            g = ghid[st, :]
            a = active[st, :]
            u = g * twice(vectors[3 + level, st, :], block)
            low = ((inverse * u - a * factor) * slope[st, :]).astype(bf16)
            low_parts.append(low)
            gain_term = g * (a * inverse)
            bias_term = low.astype(f32)
            gain_sum = gain_term[:, 0:LANE]
            bias_sum = bias_term[:, 0:LANE]
            for j in range(1, block // LANE):
                gain_sum = gain_sum + gain_term[:, j * LANE : (j + 1) * LANE]
                bias_sum = bias_sum + bias_term[:, j * LANE : (j + 1) * LANE]
            gacc[level, st, :] += gain_sum
            bacc[level, st, :] += bias_sum
        low = jnp.concatenate(low_parts, axis=0)
        into = gfirst if level == 0 else gfull.at[level - 1]
        added = dot(low, joined, NT)
        for j in range(joined.shape[0] // LANE):
            into[j] += added[:, j * LANE : (j + 1) * LANE]
        if need_input:
            back = dot(matrix(level), low, TN)
            wide[:, lanes] = back[0:hid, :]
            gmean[:, lanes] = (back[hid:, :] * info[0:1, lanes]).astype(bf16)

    def layer_three(i, loss):
        off = pl.multiple_of(i * block, block)
        lanes = pl.ds(off, block)
        joined, inverse = forward_block(2, off, all_sums(table3, off), table3, None, None, True)
        last = jnp.concatenate([hidden_strip(2, st, inverse) for st in strips], axis=0)
        logits = dot(head_low, last, TN)[0:cls_pad, :]
        logits = jnp.where(class_iota < cls, logits, -jnp.inf)
        highest = jnp.max(logits, axis=0, keepdims=True)
        shifted = logits - highest
        grown = jnp.exp(shifted)
        total = jnp.sum(grown, axis=0, keepdims=True)
        hot = class_iota == info[1:2, lanes].astype(i32)
        counted = info[2:3, lanes]
        chosen = jnp.sum(jnp.where(hot, shifted, 0.0), axis=0, keepdims=True)
        loss = loss + (jnp.log(total) - chosen) * counted
        g_logits = (grown / total - jnp.where(hot, 1.0, 0.0)) * (counted * one_over_count)
        g_low = jnp.concatenate(
            [g_logits, jnp.zeros((LANE - cls_pad, block), f32)], axis=0
        ).astype(bf16)
        ghead[...] += dot(last, g_low, NT)
        ghid[...] = dot(head_low, g_low, NN)
        backward_block(2, off, joined, inverse, True)
        return loss

    loss = lax.fori_loop(0, blocks, layer_three, jnp.zeros((1, block), f32))

    def start_first(seg):
        for piece in range(n_group):
            gwire[seg, piece] = gfull[seg, piece].astype(wire)

        def start(i, carry):
            group = lax.rem(my_group + i, n_group)
            pltpu.make_async_remote_copy(
                src_ref=gwire.at[seg, group],
                dst_ref=recv1.at[seg, my_group],
                send_sem=g_ssem.at[0, seg],
                recv_sem=g_rsem.at[0, seg],
                device_id=target(group, my_shard),
                device_id_type=MESH,
            ).start()
            return carry

        lax.fori_loop(1, n_group, start, 0)
        recv1[seg, my_group] = jnp.zeros(recv1.shape[2:], wire)

    def start_second(seg):
        wait_bytes(gwire.at[seg, pl.ds(0, n_group - 1)], g_ssem.at[0, seg])
        wait_bytes(recv1.at[seg, pl.ds(0, n_group - 1)], g_rsem.at[0, seg])
        total = gfull[seg, my_group]
        for group in range(n_group):
            total = total + recv1[seg, group].astype(f32)
        gfull[seg, my_group] = total
        send2[seg] = total.astype(wire).reshape(n_shard, chunk, LANE)

        def start(i, carry):
            shard = lax.rem(my_shard + i, n_shard)
            pltpu.make_async_remote_copy(
                src_ref=send2.at[seg, shard],
                dst_ref=recv2.at[seg, my_shard],
                send_sem=g_ssem.at[1, seg],
                recv_sem=g_rsem.at[1, seg],
                device_id=target(my_group, shard),
                device_id_type=MESH,
            ).start()
            return carry

        lax.fori_loop(1, n_shard, start, 0)
        recv2[seg, my_shard] = jnp.zeros(recv2.shape[2:], wire)

    def start_third(seg):
        wait_bytes(send2.at[seg, pl.ds(0, n_shard - 1)], g_ssem.at[1, seg])
        wait_bytes(recv2.at[seg, pl.ds(0, n_shard - 1)], g_rsem.at[1, seg])
        total = gfull[seg, my_group, own_chunk, :]
        for shard in range(n_shard):
            total = total + recv2[seg, shard].astype(f32)
        part3[seg] = total

        def start(i, carry):
            group = lax.rem(my_group + i, n_group)
            pltpu.make_async_remote_copy(
                src_ref=part3.at[seg],
                dst_ref=recv3.at[seg, my_group],
                send_sem=g_ssem.at[2, seg],
                recv_sem=g_rsem.at[2, seg],
                device_id=target(group, my_shard),
                device_id_type=MESH,
            ).start()
            return carry

        lax.fori_loop(1, n_group, start, 0)
        recv3[seg, my_group] = total
        return jnp.sum(total * total)

    def wait_third(seg):
        for _ in range(n_group - 1):
            wait_bytes(part3.at[seg], g_ssem.at[2, seg])
        wait_bytes(recv3.at[seg, pl.ds(0, n_group - 1)], g_rsem.at[2, seg])

    def bias_and_gain(levels, first_lane):
        lane_wide = lax.broadcasted_iota(i32, (hid, LANE), 1)
        total = jnp.zeros((hid, LANE), f32)
        for n, level in enumerate(levels):
            for acc, shift in ((bacc, 0), (gacc, len(levels))):
                total = jnp.where(
                    lane_wide == first_lane + shift + n,
                    jnp.sum(acc[level], axis=1, keepdims=True),
                    total,
                )
        return total

    def start_head():
        total = ghead[...] + bias_and_gain((1, 2), cls)
        ghead[...] = total
        hwire[...] = total.astype(wire).reshape(n_shard, chunk, LANE)

        def start(i, carry):
            shard = lax.rem(my_shard + i, n_shard)
            pltpu.make_async_remote_copy(
                src_ref=hwire.at[shard],
                dst_ref=hrecv.at[my_shard],
                send_sem=h_ssem.at[0],
                recv_sem=h_rsem.at[0],
                device_id=target(my_group, shard),
                device_id_type=MESH,
            ).start()
            return carry

        lax.fori_loop(1, n_shard, start, 0)
        hrecv[my_shard] = jnp.zeros(hrecv.shape[1:], wire)

    def share_head():
        wait_bytes(hwire.at[pl.ds(0, n_shard - 1)], h_ssem.at[0])
        wait_bytes(hrecv.at[pl.ds(0, n_shard - 1)], h_rsem.at[0])
        total = ghead[own_chunk, :]
        for shard in range(n_shard):
            total = total + hrecv[shard].astype(f32)
        hpart[...] = total

        def start(i, carry):
            group = lax.rem(my_group + i, n_group)
            pltpu.make_async_remote_copy(
                src_ref=hpart,
                dst_ref=hfinal.at[my_group],
                send_sem=h_ssem.at[1],
                recv_sem=h_rsem.at[1],
                device_id=target(group, my_shard),
                device_id_type=MESH,
            ).start()
            return carry

        lax.fori_loop(1, n_group, start, 0)
        hfinal[my_group] = total

    def wait_head():
        wait_bytes(hfinal.at[pl.ds(0, n_group - 1)], h_ssem.at[1])
        wait_bytes(hfinal.at[pl.ds(0, n_group - 1)], h_rsem.at[1])
        total = hfinal[0]
        for group in range(1, n_group):
            total = total + hfinal[group]
        head_out[...] = total
        return jnp.sum(total * total) * (1.0 / n_group)

    units, unit_rows, row_parts_first = cfg["units"], cfg["unit_rows"], cfg["units"] // 2

    def start_first_layer():
        gfirst[0] += bias_and_gain((0,), fin)
        for unit in range(units):
            tile, part = unit // row_parts_first, unit % row_parts_first
            whole = gfirst[tile].reshape(n_shard, chunk, LANE)
            fwire[unit] = whole[:, part * unit_rows : (part + 1) * unit_rows, :].astype(wire)

        def start(i, carry):
            peer = lax.rem(me + i, devices)
            group, shard = lax.div(peer, n_shard), lax.rem(peer, n_shard)
            pltpu.make_async_remote_copy(
                src_ref=fwire.at[lax.rem(group, units), shard],
                dst_ref=frecv.at[me],
                send_sem=f_ssem.at[0],
                recv_sem=f_rsem.at[0],
                device_id=target(group, shard),
                device_id_type=MESH,
            ).start()
            return carry

        lax.fori_loop(1, devices, start, 0)
        frecv[me] = fwire[lax.rem(my_group, units), my_shard]

    def share_first_layer():
        wait_bytes(frecv.at[pl.ds(0, devices - 1)], f_ssem.at[0])
        wait_bytes(frecv.at[pl.ds(0, devices - 1)], f_rsem.at[0])
        total = jnp.sum(frecv[...].astype(f32), axis=0)
        fpart[...] = total

        def start(i, carry):
            group = lax.rem(my_group + i, n_group)
            pltpu.make_async_remote_copy(
                src_ref=fpart,
                dst_ref=ffinal.at[my_group],
                send_sem=f_ssem.at[1],
                recv_sem=f_rsem.at[1],
                device_id=target(group, my_shard),
                device_id_type=MESH,
            ).start()
            return carry

        lax.fori_loop(1, n_group, start, 0)
        ffinal[my_group] = total
        return jnp.sum(total * total) * (units / n_group)

    def wait_first_layer():
        wait_bytes(ffinal.at[pl.ds(0, n_group - 1)], f_ssem.at[1])
        wait_bytes(ffinal.at[pl.ds(0, n_group - 1)], f_rsem.at[1])
        for unit in range(units):
            tile, part = unit // row_parts_first, unit % row_parts_first
            first_out[tile, part * unit_rows : (part + 1) * unit_rows, :] = ffinal[unit]

    def exchange_backward(x, meanwhile):
        for rows in row_parts:
            lanes = slice(nodes + rows.start, nodes + rows.stop)
            back = dot(gmean[...], counts[:, lanes].astype(bf16), NN)
            outs[rows, :] = back.astype(bf16).T
        start_rows(outs, ins.at[x % 2], row_ssem.at[x + 1], row_rsem.at[x + 1])
        meanwhile()

        def add(i, carry):
            off = pl.multiple_of(i * block, block)
            lanes = pl.ds(off, block)
            wide[:, lanes] += dot(gmean[...], counts[:, lanes].astype(bf16), NN)
            return carry

        lax.fori_loop(0, blocks, add, 0)
        wait_rows(outs, ins.at[x % 2], row_ssem.at[x + 1], row_rsem.at[x + 1])

    def returned(x, off):
        total = wide[:, pl.ds(off, block)]
        for rows in row_parts:
            total = total + dot(ins[x % 2, rows, :], picks(rows, off), TN)
        return total

    exchange_backward(2, lambda: start_first(1))
    start_second(1)

    def backward_two(i, carry):
        off = pl.multiple_of(i * block, block)
        lanes = pl.ds(off, block)
        ghid[...] = returned(2, off)
        joined = jnp.concatenate([table2[:, lanes], mean2[:, lanes]], axis=0)
        if before2.shape[1] < nodes:
            before[...] = dot(matrix(1), joined, NN)
        inverse = activate(1, True, kept_or_none(before2), off)
        backward_block(1, off, joined, inverse, True)
        return carry

    lax.fori_loop(0, blocks, backward_two, 0)

    def meanwhile():
        start_first(0)
        start_head()

    exchange_backward(3, meanwhile)
    square = start_third(1)
    start_second(0)
    share_head()

    def backward_one(i, carry):
        off = pl.multiple_of(i * block, block)
        lanes = pl.ds(off, block)
        ghid[...] = returned(3, off)
        joined = jnp.concatenate([table1[:, lanes], mean1[:, lanes]], axis=0)
        if before1.shape[1] < nodes:
            before[...] = dot(matrix(0), joined, NN)
        inverse = activate(0, True, kept_or_none(before1), off)
        backward_block(0, off, joined, inverse, False)
        return carry

    lax.fori_loop(0, blocks, backward_one, 0)
    start_first_layer()
    square = square + start_third(0) + wait_head()
    square = square + share_first_layer()

    lane_of = lax.broadcasted_iota(i32, (8, LANE), 1)
    mine = jnp.where(lane_of == 0, square, jnp.where(lane_of == 1, jnp.sum(loss), 0.0))
    scal_send[...] = mine

    def send_scalars(i, carry):
        peer = lax.rem(me + i, devices)
        pltpu.make_async_remote_copy(
            src_ref=scal_send.at[pl.ds(0, 1), :],
            dst_ref=scal_recv.at[pl.ds(me, 1), :],
            send_sem=s_ssem,
            recv_sem=s_rsem,
            device_id=target(lax.div(peer, n_shard), lax.rem(peer, n_shard)),
            device_id_type=MESH,
        ).start()
        return carry

    lax.fori_loop(1, devices, send_scalars, 0)
    scal_recv[pl.ds(me, 1), :] = mine[0:1, :]
    for seg in range(2):
        wait_third(seg)
    part_out[...] = recv3[...]
    wait_first_layer()
    wait_bytes(scal_recv.at[pl.ds(0, devices - 1), :], s_rsem)
    wait_bytes(scal_recv.at[pl.ds(0, devices - 1), :], s_ssem)
    totals = jnp.sum(scal_recv[...], axis=0, keepdims=True)
    scalar_out[...] = jnp.where(lane_of == 2, label_count[0:1, 0:1], totals)


def adamw(weight, grad, moment, square, rate, decay):
    moment_new = beta_one * moment + (1.0 - beta_one) * grad
    square_new = beta_two * square + (1.0 - beta_two) * grad * grad
    moment_hat = moment_new / (1.0 - beta_one**STEP)
    square_hat = square_new / (1.0 - beta_two**STEP)
    weight_new = weight - rate * (
        moment_hat / (jnp.sqrt(square_hat) + adam_epsilon) + decay * weight
    )
    return (weight_new, moment_new, square_new)


def update_kernel(fin, cls, part_ref, head_ref, first_ref, scalar_ref, *refs):
    states = [refs[3 * k : 3 * k + 3] for k in range(5)]
    outs = [refs[15 + 3 * k : 18 + 3 * k] for k in range(5)]
    copies = refs[30:33]
    loss_out, count_out, norm_out = refs[33:36]
    norm = jnp.sqrt(scalar_ref[0:1, 0:1])
    loss_out[...] = scalar_ref[0:1, 1:2]
    count_out[...] = scalar_ref[0:1, 2:3]
    norm_out[...] = norm
    factor = jnp.minimum(1.0, threshold / norm)
    small_last = head_ref[...].T
    small_first = first_ref[0].T
    bias = jnp.concatenate([small_first[fin : fin + 1], small_last[cls : cls + 2]], axis=0)
    gain = jnp.concatenate(
        [small_first[fin + 1 : fin + 2], small_last[cls + 2 : cls + 4]], axis=0
    )

    def update(k, grad, where, rate, decay):
        news = adamw(
            states[k][0][where], grad * factor, states[k][1][where], states[k][2][where], rate, decay
        )
        for out, new in zip(outs[k], news):
            out[where] = new
        if k < 3:
            copies[k][where] = news[0].astype(bf16)

    everything = (slice(None), slice(None))
    update(0, first_ref[0][:, 0:fin], (slice(None), slice(0, fin)), 0.05, 0.01)
    update(0, first_ref[1][:, 0:fin], (slice(None), slice(fin, 2 * fin)), 0.05, 0.01)
    n_group = part_ref.shape[1]
    for level in range(2):
        for piece in range(n_group):
            lanes = slice(piece * LANE, (piece + 1) * LANE)
            update(1, part_ref[level, piece], (level, slice(None), lanes), 0.05, 0.01)
    update(2, head_ref[:, 0:cls], everything, 0.05, 0.01)
    update(3, bias, everything, 0.3, 0.0)
    update(4, gain, everything, 0.3, 0.0)


def per_device(
    n_group,
    n_shard,
    features,
    node_counts,
    degrees,
    neighbours,
    send_rows,
    labels,
    train_mask,
    weight_first,
    weight_rest,
    weight_head,
    biases,
    gains,
    moment_first,
    square_first,
    moment_rest,
    square_rest,
    moment_head,
    square_head,
    moment_bias,
    square_bias,
    moment_gain,
    square_gain,
):
    nodes, fin = features.shape
    devices = n_group * n_shard
    hid = weight_rest.shape[1] // 2
    chunk = hid // n_shard
    cls = weight_head.shape[1]
    cap = send_rows.shape[1]
    slots = neighbours.shape[1]
    pad = round_up(cap + 2, 16)
    remote = devices * pad
    columns = nodes + remote
    block = 1024 if remote <= 512 else 512
    wire = bf16 if chunk % 16 == 0 else f32
    least = 16 if wire == bf16 else 8
    units = n_group if chunk * 2 // n_group >= least else 2
    unit_rows = chunk * 2 // units
    fin_pad = LANE
    cfg = dict(
        n_group=n_group,
        n_shard=n_shard,
        nodes=nodes,
        fin=fin,
        cls=cls,
        pad=pad,
        remote=remote,
        chunk=chunk,
        wire=wire,
        block=block,
        fin_pad=fin_pad,
        hid=hid,
        cap=cap,
        slots=slots,
        units=units,
        unit_rows=unit_rows,
    )

    vmem = pl.BlockSpec(memory_space=pltpu.VMEM)
    smem = pl.BlockSpec(memory_space=pltpu.SMEM)
    width = 4 * LANE + 4 * hid
    dma = pltpu.SemaphoreType.DMA
    stored = remote if remote <= 512 else 32
    kept_nodes = nodes if remote <= 512 else LANE
    scratch = [
        pltpu.VMEM((nodes, columns), narrow),
        pltpu.VMEM((stored, nodes), narrow),
        pltpu.VMEM((remote, LANE), i32),
        pltpu.VMEM((nodes // LANE * slots, LANE), i32),
        pltpu.VMEM((8, nodes // LANE, LOW), f32),
        pltpu.VMEM((8, nodes // LANE, LOW), f32),
        pltpu.VMEM((fin_pad, nodes), bf16),
        pltpu.VMEM((hid, columns), bf16),
        pltpu.VMEM((hid, columns), bf16),
        pltpu.VMEM((2 * fin_pad, nodes), narrow),
        pltpu.VMEM((2 * fin_pad, remote), narrow),
        pltpu.VMEM((fin_pad, nodes), bf16),
        pltpu.VMEM((hid, nodes), bf16),
        pltpu.VMEM((hid, kept_nodes), f32),
        pltpu.VMEM((hid, kept_nodes), f32),
        pltpu.VMEM((hid, nodes), bf16),
        pltpu.VMEM((hid, nodes), f32),
        pltpu.VMEM((remote, hid), bf16),
        pltpu.VMEM((2, remote, hid), bf16),
        pltpu.VMEM((8, nodes), f32),
        pltpu.VMEM((chunk, width), wire),
        pltpu.VMEM((hid, width), wire),
        pltpu.VMEM((hid, width), bf16),
        pltpu.VMEM((6, hid, LANE), f32),
        pltpu.VMEM((hid, block), f32),
        pltpu.VMEM((hid, block), f32),
        pltpu.VMEM((hid, block), f32),
        pltpu.VMEM((hid, block), f32),
        pltpu.VMEM((3, hid, LANE), f32),
        pltpu.VMEM((3, hid, LANE), f32),
        pltpu.VMEM((2, n_group, hid, LANE), f32),
        pltpu.VMEM((2, n_group, hid, LANE), wire),
        pltpu.VMEM((2, n_group, hid, LANE), wire),
        pltpu.VMEM((2, n_shard, chunk, LANE), wire),
        pltpu.VMEM((2, n_shard, chunk, LANE), wire),
        pltpu.VMEM((2, chunk, LANE), f32),
        pltpu.VMEM((2, n_group, chunk, LANE), f32),
        pltpu.VMEM((2, hid, LANE), f32),
        pltpu.VMEM((units, n_shard, unit_rows, LANE), wire),
        pltpu.VMEM((devices, unit_rows, LANE), wire),
        pltpu.VMEM((unit_rows, LANE), f32),
        pltpu.VMEM((n_group, unit_rows, LANE), f32),
        pltpu.VMEM((hid, LANE), f32),
        pltpu.VMEM((n_shard, chunk, LANE), wire),
        pltpu.VMEM((n_shard, chunk, LANE), wire),
        pltpu.VMEM((chunk, LANE), f32),
        pltpu.VMEM((n_group, chunk, LANE), f32),
        pltpu.VMEM((8, LANE), f32),
        pltpu.VMEM((devices, LANE), f32),
        dma((5,)),
        dma((5,)),
        dma((3,)),
        dma((3,)),
        dma((3, 2)),
        dma((3, 2)),
        dma((2,)),
        dma((2,)),
        dma((2,)),
        dma((2,)),
        dma,
        dma,
    ]
    sums = pl.pallas_call(
        functools.partial(step_kernel, cfg),
        out_shape=(
            jax.ShapeDtypeStruct((2, n_group, chunk, LANE), f32),
            jax.ShapeDtypeStruct((chunk, LANE), f32),
            jax.ShapeDtypeStruct((2, chunk, LANE), f32),
            jax.ShapeDtypeStruct((8, LANE), f32),
        ),
        in_specs=[vmem] * 5 + [smem] + [vmem] * 6,
        out_specs=(vmem,) * 4,
        scratch_shapes=scratch,
        compiler_params=pltpu.CompilerParams(
            collective_id=0, has_side_effects=True, vmem_limit_bytes=63 * 2**20
        ),
    )(
        features.T,
        neighbours.T,
        degrees.reshape(nodes // LANE, LANE),
        labels.reshape(nodes // LANE, LANE),
        train_mask.reshape(nodes // LANE, LANE),
        node_counts,
        send_rows.T,
        weight_first.T,
        weight_rest.transpose(0, 2, 1),
        weight_head,
        biases,
        gains,
    )
    turned = lambda value: value.T
    turned_rest = lambda value: value.transpose(0, 2, 1)
    same = lambda value: value
    turns = (turned, turned_rest, same, same, same)
    states = (
        (weight_first, moment_first, square_first),
        (weight_rest, moment_rest, square_rest),
        (weight_head, moment_head, square_head),
        (biases, moment_bias, square_bias),
        (gains, moment_gain, square_gain),
    )
    flat = [turn(value) for turn, three in zip(turns, states) for value in three]
    shapes = [jax.ShapeDtypeStruct(value.shape, f32) for value in flat]
    shapes += [jax.ShapeDtypeStruct(flat[3 * k].shape, bf16) for k in range(3)]
    shapes += [jax.ShapeDtypeStruct((1, 1), f32)] * 3
    updated = pl.pallas_call(
        functools.partial(update_kernel, fin, cls),
        out_shape=tuple(shapes),
        in_specs=[vmem] * (4 + len(flat)),
        out_specs=(vmem,) * len(shapes),
    )(*sums, *flat)
    news = tuple(turns[k // 3](updated[k]) for k in range(15))
    copies = tuple(turns[k](updated[15 + k]) for k in range(3))
    return tuple(value.reshape(()) for value in updated[18:]) + news + copies


def solution(mesh):
    nodes_split = P(("group", "shard"))
    nodes_rows = P(("group", "shard"), None)
    first = P(None, "shard")
    rest = P(None, None, "shard")
    head = P("shard", None)
    return jax.shard_map(
        functools.partial(per_device, mesh.shape["group"], mesh.shape["shard"]),
        mesh=mesh,
        in_specs=(
            nodes_rows,
            nodes_split,
            nodes_split,
            nodes_rows,
            nodes_rows,
            nodes_split,
            nodes_split,
            first,
            rest,
            head,
            first,
            first,
            first,
            first,
            rest,
            rest,
            head,
            head,
            first,
            first,
            first,
            first,
        ),
        out_specs=(P(), P(), P())
        + (first,) * 3
        + (rest,) * 3
        + (head,) * 3
        + (first,) * 6
        + (first, rest, head),
        check_vma=False,
    )
```

```python
import functools

import jax
import jax.numpy as jnp
from jax import lax
from jax.experimental import pallas as pl
from jax.experimental.pallas import tpu as pltpu
from jax.sharding import PartitionSpec as P

STEP = 10
MESH = pl.DeviceIdType.MESH
bf16 = jnp.bfloat16
f32 = jnp.float32
i32 = jnp.int32

norm_epsilon = 1e-05
threshold = 0.002
beta_one = 0.5
beta_two = 0.5
adam_epsilon = 1e-08

LANE = 128
LOW = 256
narrow = jnp.float8_e4m3fn
STRIP = 32

NN = (((1,), (0,)), ((), ()))
NT = (((1,), (1,)), ((), ()))
TN = (((0,), (0,)), ((), ()))


def dot(a, b, dims):
    return lax.dot_general(a, b, dims, preferred_element_type=f32)


def round_up(value, unit):
    return -(-value // unit) * unit


def twice(half, width):
    return jnp.concatenate([half] * (width // LANE), axis=1)


def step_kernel(
    cfg,
    feat_ref,
    neighbour_ref,
    deg_ref,
    label_ref,
    mask_ref,
    count_ref,
    send_ref,
    first_ref,
    rest_ref,
    head_ref,
    bias_ref,
    gain_ref,
    part_out,
    head_out,
    first_out,
    scalar_out,
    counts,
    picked,
    send_columns,
    slot_rows,
    key_high,
    key_low,
    table1,
    table2,
    table3,
    first_own,
    first_remote,
    mean1,
    mean2,
    before1,
    before2,
    gmean,
    wide,
    outs,
    ins,
    info,
    wsend,
    wwire,
    wfull,
    vectors,
    before,
    slope,
    ghid,
    losses,
    gacc,
    bacc,
    gfull,
    gwire,
    recv1,
    send2,
    recv2,
    part3,
    recv3,
    gfirst,
    fwire,
    frecv,
    fpart,
    ffinal,
    ghead,
    hwire,
    hrecv,
    hpart,
    hfinal,
    scal_send,
    scal_recv,
    row_ssem,
    row_rsem,
    w_ssem,
    w_rsem,
    g_ssem,
    g_rsem,
    f_ssem,
    f_rsem,
    h_ssem,
    h_rsem,
    s_ssem,
    s_rsem,
):
    n_group, n_shard = cfg["n_group"], cfg["n_shard"]
    nodes, fin, cls = cfg["nodes"], cfg["fin"], cfg["cls"]
    pad, remote, chunk, wire = cfg["pad"], cfg["remote"], cfg["chunk"], cfg["wire"]
    block, fin_pad, hid = cfg["block"], cfg["fin_pad"], cfg["hid"]
    devices = n_group * n_shard
    columns = nodes + remote
    my_group, my_shard = lax.axis_index("group"), lax.axis_index("shard")
    me = my_group * n_shard + my_shard
    blocks = nodes // block
    streams, large = cfg["streams"], cfg["large"]

    def target(group, shard):
        return {"group": group, "shard": shard}

    out1, in1 = outs.at[:, pl.ds(0, fin_pad)], ins.at[1, :, pl.ds(0, fin_pad)]

    barrier = pltpu.get_barrier_semaphore()

    def greet(group, shard):
        pl.semaphore_signal(
            barrier, inc=1, device_id=target(group, shard), device_id_type=MESH
        )

    def each_shard(action, group, first):
        if n_shard <= 8:
            for i in range(first, n_shard):
                action(group, lax.rem(my_shard + i, n_shard))
        else:

            def run(i, carry):
                action(group, lax.rem(my_shard + i, n_shard))
                return carry

            lax.fori_loop(first, n_shard, run, 0)

    def each_group(action):
        for i in range(1, n_group):
            action(lax.rem(my_group + i, n_group), my_shard)

    def each_device(action):
        for i in range(n_group):
            each_shard(action, lax.rem(my_group + i, n_group), 1 if i == 0 else 0)

    each_device(greet)

    def start_rows(source, landing, ssem, rsem):
        def start(group, shard):
            peer = group * n_shard + shard
            pltpu.make_async_remote_copy(
                src_ref=source.at[pl.ds(pl.multiple_of(peer * pad, pad), pad), :],
                dst_ref=landing.at[pl.ds(pl.multiple_of(me * pad, pad), pad), :],
                send_sem=ssem,
                recv_sem=rsem,
                device_id=target(group, shard),
                device_id_type=MESH,
            ).start()

        each_device(start)
        own = pl.ds(pl.multiple_of(me * pad, pad), pad)
        landing[own, :] = source[own, :]

    def wait_bytes(ref, sem):
        pltpu.make_async_copy(ref, ref, sem).wait()

    def wait_rows(source, landing, ssem, rsem):
        rows = pl.ds(0, (devices - 1) * pad)
        wait_bytes(source.at[rows, :], ssem)
        wait_bytes(landing.at[rows, :], rsem)

    some = min(remote, 512)
    row_parts = [slice(r, r + some) for r in range(0, remote, some)]

    def make_picks(rows, off, width):
        lanes = lax.broadcasted_iota(i32, (some, LANE), 1) + off
        parts = [
            jnp.where(send_columns[rows, :] == lanes + LANE * j, 1.0, 0.0).astype(bf16)
            for j in range(width // LANE)
        ]
        return jnp.concatenate(parts, axis=1)

    def picks(rows, off):
        if picked.shape[0] == remote:
            return picked[rows, pl.ds(off, block)].astype(bf16)
        return make_picks(rows, off, block)

    def pick_rows(table, into):
        for rows in row_parts:
            if picked.shape[0] == remote:
                total = dot(picked[rows, :].astype(bf16), table[:, 0:nodes], NT)
            else:

                def add(i, total):
                    off = pl.multiple_of(i * block, block)
                    return total + dot(picks(rows, off), table[:, pl.ds(off, block)], NT)

                total = lax.fori_loop(0, blocks, add, jnp.zeros((some, table.shape[0]), f32))
            into[rows, :] = total.astype(bf16)

    total_counted = jnp.zeros((1, LANE), f32)
    lane_row = lax.broadcasted_iota(i32, (1, LANE), 1)
    for r in range(nodes // LANE):
        lanes = slice(r * LANE, (r + 1) * LANE)
        degree = deg_ref[r : r + 1, :].astype(f32)
        info[0:1, lanes] = 1.0 / degree
        info[3:4, lanes] = degree
        info[1:2, lanes] = label_ref[r : r + 1, :].astype(f32)
        counted = jnp.where(
            (lane_row + r * LANE < count_ref[0]) & (mask_ref[r : r + 1, :] > 0), 1.0, 0.0
        )
        info[2:3, lanes] = counted
        total_counted = total_counted + counted
    my_count = jnp.sum(total_counted, axis=1, keepdims=True)
    count_high = jnp.floor(my_count * (1.0 / 256.0))
    count_low = my_count - 256.0 * count_high

    table1[fin // 16 * 16 :, :] = jnp.zeros((fin_pad - fin // 16 * 16, nodes), bf16)
    table1[0:fin, :] = feat_ref[...]

    def split_in_two(value, into):
        value = value.astype(f32)
        largest = jnp.max(jnp.abs(value), axis=1, keepdims=True)
        scale = jnp.ones_like(largest)
        for power in (32, 16, 8, 4, 2, 1):
            larger = scale * 2.0**power
            scale = jnp.where(largest * larger <= 448.0, larger, scale)
        scaled = value * scale
        high = scaled.astype(narrow)
        into[0:fin_pad, :] = high
        into[fin_pad:, :] = ((scaled - high.astype(f32)) * 16.0).astype(narrow)
        return 1.0 / scale

    def joined_parts(both, unscale):
        return (both[0:fin_pad, :] + both[fin_pad:, :] * (1.0 / 16.0)) * unscale

    cap, slots = cfg["cap"], cfg["slots"]
    numbers = jnp.concatenate(
        [send_ref[...], jnp.full((pad - cap, devices), -256, i32)], axis=0
    )
    halves = jnp.concatenate([numbers >> 8, numbers & 255], axis=0).astype(f32).astype(bf16)
    for rows in row_parts:
        peers = lax.broadcasted_iota(i32, (some, devices), 1)
        row_numbers = lax.broadcasted_iota(i32, (some, devices), 0) + rows.start
        chosen = jnp.where(lax.div(row_numbers, pad) == peers, 1.0, 0.0).astype(bf16)
        found = dot(chosen, halves, NT)
        lanes = lax.broadcasted_iota(i32, (some, 2 * pad), 1)
        place = lax.rem(lax.broadcasted_iota(i32, (some, 2 * pad), 0), pad)
        found = jnp.where(lanes < pad, 256.0 * found, found)
        found = jnp.where(lax.rem(lanes, pad) == place, found, 0.0)
        column = jnp.sum(found, axis=1, keepdims=True).astype(i32)
        send_columns[rows, :] = jnp.broadcast_to(column, (some, LANE))

    wsend[...] = jnp.zeros(wsend.shape, wire)
    wsend[:, 0:fin] = first_ref[:, 0:fin].astype(bf16).astype(wire)
    wsend[:, LANE : LANE + fin] = first_ref[:, fin : 2 * fin].astype(bf16).astype(wire)
    wsend[:, 3 * LANE + 4 * hid : 3 * LANE + 4 * hid + cls] = head_ref[...].astype(bf16).astype(wire)
    small = jnp.concatenate(
        [bias_ref[...], gain_ref[...], jnp.zeros((2, chunk), f32)], axis=0
    )
    wsend[:, 2 * LANE : 2 * LANE + 8] = small.T.astype(bf16).astype(wire)
    for level in range(2):
        lanes = slice(3 * LANE + level * 2 * hid, 3 * LANE + (level + 1) * 2 * hid)
        wsend[:, lanes] = rest_ref[level].astype(bf16).astype(wire)

    if picked.shape[0] == remote:

        def store_picks(i, carry):
            off = pl.multiple_of(i * 512, 512)
            picked[:, pl.ds(off, 512)] = make_picks(row_parts[0], off, 512).astype(narrow)
            return carry

        lax.fori_loop(0, nodes // 512, store_picks, 0)

    pick_rows(table1, out1)
    spare = lax.rem(lax.broadcasted_iota(i32, (remote, fin_pad), 0), pad)
    sent = out1[...].astype(f32)
    sent = jnp.where(spare == pad - 2, count_high, sent)
    sent = jnp.where(spare == pad - 1, count_low, sent)
    out1[...] = sent.astype(bf16)

    own_chunk = pl.ds(pl.multiple_of(my_shard * chunk, chunk), chunk)
    weight_parts = (
        slice(0, 3 * LANE),
        slice(3 * LANE, 3 * LANE + 2 * hid),
        slice(3 * LANE + 2 * hid, 4 * LANE + 4 * hid),
    )

    def send_weights(part):
        lanes = weight_parts[part]

        def start(group, shard):
            pltpu.make_async_remote_copy(
                src_ref=wsend.at[:, lanes],
                dst_ref=wwire.at[own_chunk, lanes],
                send_sem=w_ssem.at[part],
                recv_sem=w_rsem.at[part],
                device_id=target(group, shard),
                device_id_type=MESH,
            ).start()

        each_shard(start, my_group, 1)

    def wait_weights(part):
        lanes = weight_parts[part]
        rows = pl.ds(0, (n_shard - 1) * chunk)
        wait_bytes(wwire.at[rows, lanes], w_rsem.at[part])
        wait_bytes(wwire.at[rows, lanes], w_ssem.at[part])
        wfull[:, lanes] = wwire[:, lanes].astype(bf16)

    pl.semaphore_wait(barrier, devices - 1)
    start_rows(out1, in1, row_ssem.at[0], row_rsem.at[0])
    wwire[own_chunk, :] = wsend[...]
    send_weights(0)

    tiles = nodes // LANE
    for g in range(tiles):
        lanes = slice(g * LANE, (g + 1) * LANE)
        column = neighbour_ref[:, lanes]
        away = column - nodes
        source = ((away.astype(f32) + 0.5) * (1.0 / cap)).astype(i32)
        moved = jnp.where(away < 0, column, column + source * (pad - cap))
        live = lax.broadcasted_iota(i32, (slots, LANE), 0).astype(f32) < info[3:4, lanes]
        slot_rows[g * slots : (g + 1) * slots, :] = jnp.where(live, moved, -256)
    per_half = LANE // 16
    sixteenth = lax.div(lax.broadcasted_iota(i32, (tiles, LANE), 1), 16)
    for half in range(slots // per_half):
        made = [jnp.zeros((tiles, LANE), i32)] * per_half
        for j in range(per_half):
            rows = slot_rows[pl.ds(half * per_half + j, tiles, stride=slots), :]
            here = sixteenth == j
            for b in range(per_half):
                turned = pltpu.roll(rows, 16 * ((j - b) % per_half), 1) if j != b else rows
                made[b] = jnp.where(here, turned, made[b])
        lanes = slice(half * LANE, (half + 1) * LANE)
        for b in range(per_half):
            key_high[b, :, lanes] = (made[b] >> 8).astype(f32)
            key_low[b, :, lanes] = (made[b] & 255).astype(f32)

    high_rows = columns // LOW
    low_iota = lax.broadcasted_iota(i32, (LOW, LOW), 0).astype(f32).astype(bf16)
    same_node = (
        lax.rem(lax.broadcasted_iota(i32, (16, LOW), 1), 16)
        == lax.broadcasted_iota(i32, (16, LOW), 0)
    ).astype(f32).astype(bf16)
    zero_tile = jnp.zeros((16, LOW), bf16)
    one_low = jnp.ones((LOW, LOW), bf16)
    zero_low = jnp.zeros((LOW, LOW), bf16)
    group_rows = 32
    fold = group_rows // 16

    def build(it, carry):
        for k in range(0, 8, fold):
            made = []
            for kk in range(k, k + fold):
                high_row = jnp.broadcast_to(key_high[kk, pl.ds(it, 1), :], (16, LOW)).astype(bf16)
                low_row = jnp.broadcast_to(key_low[kk, pl.ds(it, 1), :], (16, LOW)).astype(bf16)
                left = jnp.concatenate(
                    [
                        jnp.where(high_row == jnp.asarray(h, bf16), same_node, zero_tile)
                        for h in range(high_rows)
                    ],
                    axis=0,
                ).astype(narrow)
                right = jnp.where(
                    low_iota == jnp.concatenate([low_row] * (LOW // 16), axis=0),
                    one_low,
                    zero_low,
                ).astype(narrow)
                made.append(dot(left, right, NT))
            row = pl.multiple_of(it * 128 + k * 16, group_rows)
            for h in range(high_rows):
                tile = jnp.concatenate([m[h * 16 : h * 16 + 16, :] for m in made], axis=0)
                counts[pl.ds(row, group_rows), h * LOW : (h + 1) * LOW] = tile.astype(
                    counts.dtype
                )
        return carry

    unscale_own = split_in_two(table1[...], first_own)
    lax.fori_loop(0, nodes // 256, build, 0)
    send_weights(1)
    lax.fori_loop(nodes // 256, nodes // 128, build, 0)

    wait_weights(0)
    weight_lanes = (
        slice(0, 2 * LANE),
        weight_parts[1],
        slice(3 * LANE + 2 * hid, 3 * LANE + 4 * hid),
    )
    small_full = wfull[:, 2 * LANE : 3 * LANE].astype(f32)
    for v in range(6):
        vectors[v] = jnp.broadcast_to(small_full[:, v : v + 1], (hid, LANE))

    def matrix(level):
        return wfull[:, weight_lanes[level]]

    wait_rows(out1, in1, row_ssem.at[0], row_rsem.at[0])
    received = in1[...].astype(f32)
    scale = jnp.where(spare == pad - 2, 256.0, jnp.where(spare == pad - 1, 1.0, 0.0))
    label_count = jnp.sum(received * scale, axis=0, keepdims=True)
    unscale_remote = split_in_two(
        jnp.where(spare < pad - 2, received, 0.0).T, first_remote
    )

    def c_block(off, lanes):
        return counts[pl.ds(off, block), lanes].astype(bf16)

    strips = [slice(r, r + STRIP) for r in range(0, hid, STRIP)]

    def fold_rows(value):
        return jnp.sum(value.reshape(STRIP // 8, 8, value.shape[1]), axis=0)

    def activate(level, keep_slope, kept, off, w):
        squares = jnp.zeros((8, block), f32)
        for st in strips:
            if kept is not None and keep_slope:
                b = kept[st, pl.ds(off, block)]
            else:
                b = before[w, st, :] + twice(vectors[level, st, :], block)
            if kept is not None and not keep_slope:
                kept[st, pl.ds(off, block)] = b
            s = 0.5 + 0.5 * jnp.tanh(0.5 * b)
            a = b * s
            before[w, st, :] = a
            if keep_slope:
                slope[w, st, :] = s + a * (1.0 - s)
            squares = squares + fold_rows(a * a)
        mean_square = jnp.sum(squares, axis=0, keepdims=True) * (1.0 / hid)
        return lax.rsqrt(mean_square + norm_epsilon)

    def hidden_strip(level, st, inverse, w):
        scaled = before[w, st, :] * inverse
        return (twice(vectors[3 + level, st, :], block) * scaled).astype(bf16)

    def kept_or_none(kept):
        return kept if kept is not None and kept.shape[1] == nodes else None

    def forward_block(level, off, summed, table, mean, kept, keep_slope, w):
        lanes = pl.ds(off, block)
        mean_low = (summed * info[0:1, lanes]).astype(bf16)
        if mean is not None:
            mean[:, lanes] = mean_low
        joined = jnp.concatenate([table[:, lanes], mean_low], axis=0)
        before[w] = dot(matrix(level), joined, NN)
        yield
        return joined, activate(level, keep_slope, kept_or_none(kept), off, w)

    def run_blocks(make):
        def body(k, carry):
            live = [
                make(pl.multiple_of((k * streams + w) * block, block), w)
                for w in range(streams)
            ]
            ended, tick = set(), 0
            while len(ended) < streams:
                for w in range(streams):
                    if tick >= w and w not in ended:
                        if next(live[w], "end") == "end":
                            ended.add(w)
                tick += 1
            return carry

        lax.fori_loop(0, blocks // streams, body, 0)

    send_weights(2)
    def layer_one(off, w):
        rows = pl.ds(off, block)
        own = dot(first_own[...], counts[rows, 0:nodes], NT)
        away = dot(first_remote[...], counts[rows, nodes:], NT)
        yield
        summed = joined_parts(own, unscale_own) + joined_parts(away, unscale_remote)
        _, inverse = yield from forward_block(0, off, summed, table1, mean1, before1, False, w)
        yield
        for st in strips:
            table2[st, rows] = hidden_strip(0, st, inverse, w)

    run_blocks(layer_one)

    def own_sums(table):
        def add(i, carry):
            rows = pl.ds(pl.multiple_of(i * large, large), large)
            wide[:, rows] = dot(table[:, 0:nodes], counts[rows, 0:nodes].astype(bf16), NT)
            return carry

        lax.fori_loop(0, nodes // large, add, 0)

    def exchange_forward(table, x):
        pick_rows(table, outs)
        start_rows(outs, ins.at[x % 2], row_ssem.at[x + 1], row_rsem.at[x + 1])
        own_sums(table)
        wait_rows(outs, ins.at[x % 2], row_ssem.at[x + 1], row_rsem.at[x + 1])
        table[:, nodes:] = ins[x % 2].T

    def all_sums(table, off):
        return wide[:, pl.ds(off, block)] + dot(
            table[:, nodes:], c_block(off, slice(nodes, columns)), NT
        )

    exchange_forward(table2, 0)
    wait_weights(1)

    def layer_two(off, w):
        summed = all_sums(table2, off)
        yield
        _, inverse = yield from forward_block(1, off, summed, table2, mean2, before2, False, w)
        yield
        for st in strips:
            table3[st, pl.ds(off, block)] = hidden_strip(1, st, inverse, w)

    run_blocks(layer_two)

    exchange_forward(table3, 1)
    wait_weights(2)
    gfirst[...] = jnp.zeros(gfirst.shape, f32)
    ghead[...] = jnp.zeros(ghead.shape, f32)
    gfull[...] = jnp.zeros(gfull.shape, f32)
    gacc[...] = jnp.zeros(gacc.shape, f32)
    bacc[...] = jnp.zeros(bacc.shape, f32)
    head_low = wfull[:, 3 * LANE + 4 * hid :]
    cls_pad = round_up(cls, 16)
    one_over_count = 1.0 / label_count[0:1, 0:1]
    class_iota = lax.broadcasted_iota(i32, (cls_pad, block), 0)

    def backward_block(level, off, joined, inverse, need_input, w):
        lanes = pl.ds(off, block)
        crossed = jnp.zeros((8, block), f32)
        for st in strips:
            u = ghid[w, st, :] * twice(vectors[3 + level, st, :], block)
            crossed = crossed + fold_rows(u * before[w, st, :])
        factor = jnp.sum(crossed, axis=0, keepdims=True) * (1.0 / hid) * inverse
        factor = factor * inverse * inverse
        low_parts = []
        for st in strips:
            g = ghid[w, st, :]
            a = before[w, st, :]
            u = g * twice(vectors[3 + level, st, :], block)
            low = ((inverse * u - a * factor) * slope[w, st, :]).astype(bf16)
            low_parts.append(low)
            gain_term = g * (a * inverse)
            bias_term = low.astype(f32)
            gain_sum = gain_term[:, 0:LANE]
            bias_sum = bias_term[:, 0:LANE]
            for j in range(1, block // LANE):
                gain_sum = gain_sum + gain_term[:, j * LANE : (j + 1) * LANE]
                bias_sum = bias_sum + bias_term[:, j * LANE : (j + 1) * LANE]
            gacc[level, st, :] += gain_sum
            bacc[level, st, :] += bias_sum
        low = jnp.concatenate(low_parts, axis=0)
        yield
        into = gfirst if level == 0 else gfull.at[level - 1]
        added = dot(low, joined, NT)
        for j in range(joined.shape[0] // LANE):
            into[j] += added[:, j * LANE : (j + 1) * LANE]
        if need_input:
            back = dot(matrix(level), low, TN)
            wide[:, lanes] = back[0:hid, :]
            gmean[:, lanes] = (back[hid:, :] * info[0:1, lanes]).astype(bf16)

    def layer_three(off, w):
        lanes = pl.ds(off, block)
        summed = all_sums(table3, off)
        yield
        joined, inverse = yield from forward_block(
            2, off, summed, table3, None, None, True, w
        )
        last = jnp.concatenate([hidden_strip(2, st, inverse, w) for st in strips], axis=0)
        yield
        logits = dot(head_low, last, TN)[0:cls_pad, :]
        yield
        logits = jnp.where(class_iota < cls, logits, -jnp.inf)
        highest = jnp.max(logits, axis=0, keepdims=True)
        shifted = logits - highest
        grown = jnp.exp(shifted)
        total = jnp.sum(grown, axis=0, keepdims=True)
        hot = class_iota == info[1:2, lanes].astype(i32)
        counted = info[2:3, lanes]
        chosen = jnp.sum(jnp.where(hot, shifted, 0.0), axis=0, keepdims=True)
        losses[w : w + 1, :] += (jnp.log(total) - chosen) * counted
        g_logits = (grown * (1.0 / total) - jnp.where(hot, 1.0, 0.0)) * (counted * one_over_count)
        g_low = jnp.concatenate(
            [g_logits, jnp.zeros((LANE - cls_pad, block), f32)], axis=0
        ).astype(bf16)
        yield
        ghead[...] += dot(last, g_low, NT)
        ghid[w] = dot(head_low, g_low, NN)
        yield
        yield from backward_block(2, off, joined, inverse, True, w)

    losses[...] = jnp.zeros(losses.shape, f32)
    run_blocks(layer_three)

    def start_first(seg):
        for piece in range(n_group):
            gwire[seg, piece] = gfull[seg, piece].astype(wire)

        def start(group, shard):
            pltpu.make_async_remote_copy(
                src_ref=gwire.at[seg, group],
                dst_ref=recv1.at[seg, my_group],
                send_sem=g_ssem.at[0, seg],
                recv_sem=g_rsem.at[0, seg],
                device_id=target(group, shard),
                device_id_type=MESH,
            ).start()

        each_group(start)
        recv1[seg, my_group] = jnp.zeros(recv1.shape[2:], wire)

    def start_second(seg):
        wait_bytes(gwire.at[seg, pl.ds(0, n_group - 1)], g_ssem.at[0, seg])
        wait_bytes(recv1.at[seg, pl.ds(0, n_group - 1)], g_rsem.at[0, seg])
        total = gfull[seg, my_group]
        for group in range(n_group):
            total = total + recv1[seg, group].astype(f32)
        gfull[seg, my_group] = total
        send2[seg] = total.astype(wire).reshape(n_shard, chunk, LANE)

        def start(group, shard):
            pltpu.make_async_remote_copy(
                src_ref=send2.at[seg, shard],
                dst_ref=recv2.at[seg, my_shard],
                send_sem=g_ssem.at[1, seg],
                recv_sem=g_rsem.at[1, seg],
                device_id=target(group, shard),
                device_id_type=MESH,
            ).start()

        each_shard(start, my_group, 1)
        recv2[seg, my_shard] = jnp.zeros(recv2.shape[2:], wire)

    def start_third(seg):
        wait_bytes(send2.at[seg, pl.ds(0, n_shard - 1)], g_ssem.at[1, seg])
        wait_bytes(recv2.at[seg, pl.ds(0, n_shard - 1)], g_rsem.at[1, seg])
        total = gfull[seg, my_group, own_chunk, :]
        for shard in range(n_shard):
            total = total + recv2[seg, shard].astype(f32)
        part3[seg] = total

        def start(group, shard):
            pltpu.make_async_remote_copy(
                src_ref=part3.at[seg],
                dst_ref=recv3.at[seg, my_group],
                send_sem=g_ssem.at[2, seg],
                recv_sem=g_rsem.at[2, seg],
                device_id=target(group, shard),
                device_id_type=MESH,
            ).start()

        each_group(start)
        recv3[seg, my_group] = total
        return jnp.sum(total * total)

    def wait_third(seg):
        for _ in range(n_group - 1):
            wait_bytes(part3.at[seg], g_ssem.at[2, seg])
        wait_bytes(recv3.at[seg, pl.ds(0, n_group - 1)], g_rsem.at[2, seg])

    def bias_and_gain(levels, first_lane):
        lane_wide = lax.broadcasted_iota(i32, (hid, LANE), 1)
        total = jnp.zeros((hid, LANE), f32)
        for n, level in enumerate(levels):
            for acc, shift in ((bacc, 0), (gacc, len(levels))):
                total = jnp.where(
                    lane_wide == first_lane + shift + n,
                    jnp.sum(acc[level], axis=1, keepdims=True),
                    total,
                )
        return total

    def start_head():
        total = ghead[...] + bias_and_gain((1, 2), cls)
        ghead[...] = total
        hwire[...] = total.astype(wire).reshape(n_shard, chunk, LANE)

        def start(group, shard):
            pltpu.make_async_remote_copy(
                src_ref=hwire.at[shard],
                dst_ref=hrecv.at[my_shard],
                send_sem=h_ssem.at[0],
                recv_sem=h_rsem.at[0],
                device_id=target(group, shard),
                device_id_type=MESH,
            ).start()

        each_shard(start, my_group, 1)
        hrecv[my_shard] = jnp.zeros(hrecv.shape[1:], wire)

    def share_head():
        wait_bytes(hwire.at[pl.ds(0, n_shard - 1)], h_ssem.at[0])
        wait_bytes(hrecv.at[pl.ds(0, n_shard - 1)], h_rsem.at[0])
        total = ghead[own_chunk, :]
        for shard in range(n_shard):
            total = total + hrecv[shard].astype(f32)
        hpart[...] = total

        def start(group, shard):
            pltpu.make_async_remote_copy(
                src_ref=hpart,
                dst_ref=hfinal.at[my_group],
                send_sem=h_ssem.at[1],
                recv_sem=h_rsem.at[1],
                device_id=target(group, shard),
                device_id_type=MESH,
            ).start()

        each_group(start)
        hfinal[my_group] = total

    def wait_head():
        wait_bytes(hfinal.at[pl.ds(0, n_group - 1)], h_ssem.at[1])
        wait_bytes(hfinal.at[pl.ds(0, n_group - 1)], h_rsem.at[1])
        total = hfinal[0]
        for group in range(1, n_group):
            total = total + hfinal[group]
        head_out[...] = total
        return jnp.sum(total * total) * (1.0 / n_group)

    units, unit_rows, row_parts_first = cfg["units"], cfg["unit_rows"], cfg["units"] // 2

    def start_first_layer():
        gfirst[0] += bias_and_gain((0,), fin)
        for unit in range(units):
            tile, part = unit // row_parts_first, unit % row_parts_first
            whole = gfirst[tile].reshape(n_shard, chunk, LANE)
            fwire[unit] = whole[:, part * unit_rows : (part + 1) * unit_rows, :].astype(wire)

        def start(group, shard):
            pltpu.make_async_remote_copy(
                src_ref=fwire.at[lax.rem(group, units), shard],
                dst_ref=frecv.at[me],
                send_sem=f_ssem.at[0],
                recv_sem=f_rsem.at[0],
                device_id=target(group, shard),
                device_id_type=MESH,
            ).start()

        each_device(start)
        frecv[me] = fwire[lax.rem(my_group, units), my_shard]

    def share_first_layer():
        wait_bytes(frecv.at[pl.ds(0, devices - 1)], f_ssem.at[0])
        wait_bytes(frecv.at[pl.ds(0, devices - 1)], f_rsem.at[0])
        total = jnp.sum(frecv[...].astype(f32), axis=0)
        fpart[...] = total

        def start(group, shard):
            pltpu.make_async_remote_copy(
                src_ref=fpart,
                dst_ref=ffinal.at[my_group],
                send_sem=f_ssem.at[1],
                recv_sem=f_rsem.at[1],
                device_id=target(group, shard),
                device_id_type=MESH,
            ).start()

        each_group(start)
        ffinal[my_group] = total
        return jnp.sum(total * total) * (units / n_group)

    def wait_first_layer():
        wait_bytes(ffinal.at[pl.ds(0, n_group - 1)], f_ssem.at[1])
        wait_bytes(ffinal.at[pl.ds(0, n_group - 1)], f_rsem.at[1])
        for unit in range(units):
            tile, part = unit // row_parts_first, unit % row_parts_first
            first_out[tile, part * unit_rows : (part + 1) * unit_rows, :] = ffinal[unit]

    def exchange_backward(x, meanwhile):
        for rows in row_parts:
            lanes = slice(nodes + rows.start, nodes + rows.stop)
            back = dot(gmean[...], counts[:, lanes].astype(bf16), NN)
            outs[rows, :] = back.astype(bf16).T
        start_rows(outs, ins.at[x % 2], row_ssem.at[x + 1], row_rsem.at[x + 1])
        meanwhile()

        def add(i, carry):
            lanes = pl.ds(pl.multiple_of(i * large, large), large)
            wide[:, lanes] += dot(gmean[...], counts[:, lanes].astype(bf16), NN)
            return carry

        lax.fori_loop(0, nodes // large, add, 0)
        wait_rows(outs, ins.at[x % 2], row_ssem.at[x + 1], row_rsem.at[x + 1])

    def returned(x, off):
        total = wide[:, pl.ds(off, block)]
        for rows in row_parts:
            total = total + dot(ins[x % 2, rows, :], picks(rows, off), TN)
        return total

    exchange_backward(2, lambda: start_first(1))
    start_second(1)

    def backward_two(off, w):
        lanes = pl.ds(off, block)
        ghid[w] = returned(2, off)
        joined = jnp.concatenate([table2[:, lanes], mean2[:, lanes]], axis=0)
        if before2.shape[1] < nodes:
            before[w] = dot(matrix(1), joined, NN)
        yield
        inverse = activate(1, True, kept_or_none(before2), off, w)
        yield from backward_block(1, off, joined, inverse, True, w)

    run_blocks(backward_two)

    def meanwhile():
        start_first(0)
        start_head()

    exchange_backward(3, meanwhile)
    square = start_third(1)
    start_second(0)
    share_head()

    def backward_one(off, w):
        lanes = pl.ds(off, block)
        ghid[w] = returned(3, off)
        joined = jnp.concatenate([table1[:, lanes], mean1[:, lanes]], axis=0)
        if before1.shape[1] < nodes:
            before[w] = dot(matrix(0), joined, NN)
        yield
        inverse = activate(0, True, kept_or_none(before1), off, w)
        yield from backward_block(0, off, joined, inverse, False, w)

    run_blocks(backward_one)
    start_first_layer()
    square = square + start_third(0) + wait_head()
    square = square + share_first_layer()

    lane_of = lax.broadcasted_iota(i32, (8, LANE), 1)
    mine = jnp.where(lane_of == 0, square, jnp.where(lane_of == 1, jnp.sum(losses[...]), 0.0))
    scal_send[...] = mine

    def send_scalars(group, shard):
        pltpu.make_async_remote_copy(
            src_ref=scal_send.at[pl.ds(0, 1), :],
            dst_ref=scal_recv.at[pl.ds(me, 1), :],
            send_sem=s_ssem,
            recv_sem=s_rsem,
            device_id=target(group, shard),
            device_id_type=MESH,
        ).start()

    each_device(send_scalars)
    scal_recv[pl.ds(me, 1), :] = mine[0:1, :]
    for seg in range(2):
        wait_third(seg)
    part_out[...] = recv3[...]
    wait_first_layer()
    wait_bytes(scal_recv.at[pl.ds(0, devices - 1), :], s_rsem)
    wait_bytes(scal_recv.at[pl.ds(0, devices - 1), :], s_ssem)
    totals = jnp.sum(scal_recv[...], axis=0, keepdims=True)
    scalar_out[...] = jnp.where(lane_of == 2, label_count[0:1, 0:1], totals)


def adamw(weight, grad, moment, square, rate, decay):
    moment_new = beta_one * moment + (1.0 - beta_one) * grad
    square_new = beta_two * square + (1.0 - beta_two) * grad * grad
    moment_hat = moment_new / (1.0 - beta_one**STEP)
    square_hat = square_new / (1.0 - beta_two**STEP)
    weight_new = weight - rate * (
        moment_hat / (jnp.sqrt(square_hat) + adam_epsilon) + decay * weight
    )
    return (weight_new, moment_new, square_new)


def update_kernel(fin, cls, part_ref, head_ref, first_ref, scalar_ref, *refs):
    states = [refs[3 * k : 3 * k + 3] for k in range(5)]
    outs = [refs[15 + 3 * k : 18 + 3 * k] for k in range(5)]
    copies = refs[30:33]
    loss_out, count_out, norm_out = refs[33:36]
    norm = jnp.sqrt(scalar_ref[0:1, 0:1])
    loss_out[...] = scalar_ref[0:1, 1:2]
    count_out[...] = scalar_ref[0:1, 2:3]
    norm_out[...] = norm
    factor = jnp.minimum(1.0, threshold / norm)
    small_last = head_ref[...].T
    small_first = first_ref[0].T
    bias = jnp.concatenate([small_first[fin : fin + 1], small_last[cls : cls + 2]], axis=0)
    gain = jnp.concatenate(
        [small_first[fin + 1 : fin + 2], small_last[cls + 2 : cls + 4]], axis=0
    )

    def update(k, grad, where, rate, decay):
        news = adamw(
            states[k][0][where], grad * factor, states[k][1][where], states[k][2][where], rate, decay
        )
        for out, new in zip(outs[k], news):
            out[where] = new
        if k < 3:
            copies[k][where] = news[0].astype(bf16)

    everything = (slice(None), slice(None))
    update(0, first_ref[0][:, 0:fin], (slice(None), slice(0, fin)), 0.05, 0.01)
    update(0, first_ref[1][:, 0:fin], (slice(None), slice(fin, 2 * fin)), 0.05, 0.01)
    n_group = part_ref.shape[1]
    for level in range(2):
        for piece in range(n_group):
            lanes = slice(piece * LANE, (piece + 1) * LANE)
            update(1, part_ref[level, piece], (level, slice(None), lanes), 0.05, 0.01)
    update(2, head_ref[:, 0:cls], everything, 0.05, 0.01)
    update(3, bias, everything, 0.3, 0.0)
    update(4, gain, everything, 0.3, 0.0)


def per_device(
    n_group,
    n_shard,
    features,
    node_counts,
    degrees,
    neighbours,
    send_rows,
    labels,
    train_mask,
    weight_first,
    weight_rest,
    weight_head,
    biases,
    gains,
    moment_first,
    square_first,
    moment_rest,
    square_rest,
    moment_head,
    square_head,
    moment_bias,
    square_bias,
    moment_gain,
    square_gain,
):
    nodes, fin = features.shape
    devices = n_group * n_shard
    hid = weight_rest.shape[1] // 2
    chunk = hid // n_shard
    cls = weight_head.shape[1]
    cap = send_rows.shape[1]
    slots = neighbours.shape[1]
    pad = round_up(cap + 2, 16)
    remote = devices * pad
    columns = nodes + remote
    roomy = remote <= 512
    block, streams, large = (1024, 2, 2048) if roomy else (512, 1, 512)
    wire = bf16 if chunk % 16 == 0 else f32
    least = 16 if wire == bf16 else 8
    units = n_group if chunk * 2 // n_group >= least else 2
    unit_rows = chunk * 2 // units
    fin_pad = LANE
    cfg = dict(
        n_group=n_group,
        n_shard=n_shard,
        nodes=nodes,
        fin=fin,
        cls=cls,
        pad=pad,
        remote=remote,
        chunk=chunk,
        wire=wire,
        block=block,
        streams=streams,
        large=large,
        fin_pad=fin_pad,
        hid=hid,
        cap=cap,
        slots=slots,
        units=units,
        unit_rows=unit_rows,
    )

    vmem = pl.BlockSpec(memory_space=pltpu.VMEM)
    smem = pl.BlockSpec(memory_space=pltpu.SMEM)
    width = 4 * LANE + 4 * hid
    dma = pltpu.SemaphoreType.DMA
    stored = remote if remote <= 512 else 32
    kept_nodes = nodes if remote <= 512 else LANE
    scratch = [
        pltpu.VMEM((nodes, columns), narrow),
        pltpu.VMEM((stored, nodes), narrow),
        pltpu.VMEM((remote, LANE), i32),
        pltpu.VMEM((nodes // LANE * slots, LANE), i32),
        pltpu.VMEM((8, nodes // LANE, LOW), f32),
        pltpu.VMEM((8, nodes // LANE, LOW), f32),
        pltpu.VMEM((fin_pad, nodes), bf16),
        pltpu.VMEM((hid, columns), bf16),
        pltpu.VMEM((hid, columns), bf16),
        pltpu.VMEM((2 * fin_pad, nodes), narrow),
        pltpu.VMEM((2 * fin_pad, remote), narrow),
        pltpu.VMEM((fin_pad, nodes), bf16),
        pltpu.VMEM((hid, nodes), bf16),
        pltpu.VMEM((hid, LANE), f32),
        pltpu.VMEM((hid, kept_nodes), f32),
        pltpu.VMEM((hid, nodes), bf16),
        pltpu.VMEM((hid, nodes), f32),
        pltpu.VMEM((remote, hid), bf16),
        pltpu.VMEM((2, remote, hid), bf16),
        pltpu.VMEM((8, nodes), f32),
        pltpu.VMEM((chunk, width), wire),
        pltpu.VMEM((hid, width), wire),
        pltpu.VMEM((hid, width), bf16),
        pltpu.VMEM((6, hid, LANE), f32),
        pltpu.VMEM((streams, hid, block), f32),
        pltpu.VMEM((streams, hid, block), f32),
        pltpu.VMEM((streams, hid, block), f32),
        pltpu.VMEM((8, block), f32),
        pltpu.VMEM((3, hid, LANE), f32),
        pltpu.VMEM((3, hid, LANE), f32),
        pltpu.VMEM((2, n_group, hid, LANE), f32),
        pltpu.VMEM((2, n_group, hid, LANE), wire),
        pltpu.VMEM((2, n_group, hid, LANE), wire),
        pltpu.VMEM((2, n_shard, chunk, LANE), wire),
        pltpu.VMEM((2, n_shard, chunk, LANE), wire),
        pltpu.VMEM((2, chunk, LANE), f32),
        pltpu.VMEM((2, n_group, chunk, LANE), f32),
        pltpu.VMEM((2, hid, LANE), f32),
        pltpu.VMEM((units, n_shard, unit_rows, LANE), wire),
        pltpu.VMEM((devices, unit_rows, LANE), wire),
        pltpu.VMEM((unit_rows, LANE), f32),
        pltpu.VMEM((n_group, unit_rows, LANE), f32),
        pltpu.VMEM((hid, LANE), f32),
        pltpu.VMEM((n_shard, chunk, LANE), wire),
        pltpu.VMEM((n_shard, chunk, LANE), wire),
        pltpu.VMEM((chunk, LANE), f32),
        pltpu.VMEM((n_group, chunk, LANE), f32),
        pltpu.VMEM((8, LANE), f32),
        pltpu.VMEM((devices, LANE), f32),
        dma((5,)),
        dma((5,)),
        dma((3,)),
        dma((3,)),
        dma((3, 2)),
        dma((3, 2)),
        dma((2,)),
        dma((2,)),
        dma((2,)),
        dma((2,)),
        dma,
        dma,
    ]
    sums = pl.pallas_call(
        functools.partial(step_kernel, cfg),
        out_shape=(
            jax.ShapeDtypeStruct((2, n_group, chunk, LANE), f32),
            jax.ShapeDtypeStruct((chunk, LANE), f32),
            jax.ShapeDtypeStruct((2, chunk, LANE), f32),
            jax.ShapeDtypeStruct((8, LANE), f32),
        ),
        in_specs=[vmem] * 5 + [smem] + [vmem] * 6,
        out_specs=(vmem,) * 4,
        scratch_shapes=scratch,
        compiler_params=pltpu.CompilerParams(
            collective_id=0, has_side_effects=True, vmem_limit_bytes=63 * 2**20
        ),
    )(
        features.T,
        neighbours.T,
        degrees.reshape(nodes // LANE, LANE),
        labels.reshape(nodes // LANE, LANE),
        train_mask.reshape(nodes // LANE, LANE),
        node_counts,
        send_rows.T,
        weight_first.T,
        weight_rest.transpose(0, 2, 1),
        weight_head,
        biases,
        gains,
    )
    turned = lambda value: value.T
    turned_rest = lambda value: value.transpose(0, 2, 1)
    same = lambda value: value
    turns = (turned, turned_rest, same, same, same)
    states = (
        (weight_first, moment_first, square_first),
        (weight_rest, moment_rest, square_rest),
        (weight_head, moment_head, square_head),
        (biases, moment_bias, square_bias),
        (gains, moment_gain, square_gain),
    )
    flat = [turn(value) for turn, three in zip(turns, states) for value in three]
    shapes = [jax.ShapeDtypeStruct(value.shape, f32) for value in flat]
    shapes += [jax.ShapeDtypeStruct(flat[3 * k].shape, bf16) for k in range(3)]
    shapes += [jax.ShapeDtypeStruct((1, 1), f32)] * 3
    updated = pl.pallas_call(
        functools.partial(update_kernel, fin, cls),
        out_shape=tuple(shapes),
        in_specs=[vmem] * (4 + len(flat)),
        out_specs=(vmem,) * len(shapes),
    )(*sums, *flat)
    news = tuple(turns[k // 3](updated[k]) for k in range(15))
    copies = tuple(turns[k](updated[15 + k]) for k in range(3))
    return tuple(value.reshape(()) for value in updated[18:]) + news + copies


def solution(mesh):
    nodes_split = P(("group", "shard"))
    nodes_rows = P(("group", "shard"), None)
    first = P(None, "shard")
    rest = P(None, None, "shard")
    head = P("shard", None)
    return jax.shard_map(
        functools.partial(per_device, mesh.shape["group"], mesh.shape["shard"]),
        mesh=mesh,
        in_specs=(
            nodes_rows,
            nodes_split,
            nodes_split,
            nodes_rows,
            nodes_rows,
            nodes_split,
            nodes_split,
            first,
            rest,
            head,
            first,
            first,
            first,
            first,
            rest,
            rest,
            head,
            head,
            first,
            first,
            first,
            first,
        ),
        out_specs=(P(), P(), P())
        + (first,) * 3
        + (rest,) * 3
        + (head,) * 3
        + (first,) * 6
        + (first, rest, head),
        check_vma=False,
    )
```

```python
import functools

import jax
import jax.numpy as jnp
from jax import lax
from jax.experimental import pallas as pl
from jax.experimental.pallas import tpu as pltpu
from jax.sharding import PartitionSpec as P

STEP = 10
MESH = pl.DeviceIdType.MESH
bf16 = jnp.bfloat16
f32 = jnp.float32
i32 = jnp.int32

norm_epsilon = 1e-05
threshold = 0.002
beta_one = 0.5
beta_two = 0.5
adam_epsilon = 1e-08

LANE = 128
LOW = 256
narrow = jnp.float8_e4m3fn
STRIP = 32

NN = (((1,), (0,)), ((), ()))
NT = (((1,), (1,)), ((), ()))
TN = (((0,), (0,)), ((), ()))


def dot(a, b, dims):
    return lax.dot_general(a, b, dims, preferred_element_type=f32)


def round_up(value, unit):
    return -(-value // unit) * unit


def twice(half, width):
    return jnp.concatenate([half] * (width // LANE), axis=1)


def step_kernel(
    cfg,
    feat_ref,
    neighbour_ref,
    deg_ref,
    label_ref,
    mask_ref,
    count_ref,
    send_ref,
    first_ref,
    rest_ref,
    head_ref,
    bias_ref,
    gain_ref,
    part_out,
    head_out,
    first_out,
    scalar_out,
    counts,
    picked,
    send_columns,
    slot_rows,
    key_high,
    key_low,
    table1,
    table2,
    table3,
    first_own,
    first_remote,
    mean1,
    mean2,
    before1,
    before2,
    gmean,
    wide,
    outs,
    ins,
    info,
    wsend,
    wwire,
    wfull,
    vectors,
    before,
    slope,
    ghid,
    losses,
    gacc,
    bacc,
    gfull,
    gwire,
    recv1,
    send2,
    recv2,
    part3,
    recv3,
    gfirst,
    fwire,
    frecv,
    fpart,
    ffinal,
    ghead,
    hwire,
    hrecv,
    hpart,
    hfinal,
    scal_send,
    scal_recv,
    row_ssem,
    row_rsem,
    w_ssem,
    w_rsem,
    g_ssem,
    g_rsem,
    f_ssem,
    f_rsem,
    h_ssem,
    h_rsem,
    s_ssem,
    s_rsem,
):
    n_group, n_shard = cfg["n_group"], cfg["n_shard"]
    nodes, fin, cls = cfg["nodes"], cfg["fin"], cfg["cls"]
    pad, remote, chunk, wire = cfg["pad"], cfg["remote"], cfg["chunk"], cfg["wire"]
    block, fin_pad, hid = cfg["block"], cfg["fin_pad"], cfg["hid"]
    devices = n_group * n_shard
    columns = nodes + remote
    my_group, my_shard = lax.axis_index("group"), lax.axis_index("shard")
    me = my_group * n_shard + my_shard
    blocks = nodes // block
    streams, large = cfg["streams"], cfg["large"]

    def target(group, shard):
        return {"group": group, "shard": shard}

    out1, in1 = outs.at[:, pl.ds(0, fin_pad)], ins.at[1, :, pl.ds(0, fin_pad)]

    barrier = pltpu.get_barrier_semaphore()

    def greet(group, shard):
        pl.semaphore_signal(
            barrier, inc=1, device_id=target(group, shard), device_id_type=MESH
        )

    def each_shard(action, group, first):
        if n_shard <= 8:
            for i in range(first, n_shard):
                action(group, lax.rem(my_shard + i, n_shard))
        else:

            def run(i, carry):
                action(group, lax.rem(my_shard + i, n_shard))
                return carry

            lax.fori_loop(first, n_shard, run, 0)

    def each_group(action):
        for i in range(1, n_group):
            action(lax.rem(my_group + i, n_group), my_shard)

    def each_device(action):
        for i in range(n_group):
            each_shard(action, lax.rem(my_group + i, n_group), 1 if i == 0 else 0)

    each_device(greet)

    def start_rows(source, landing, ssem, rsem):
        def start(group, shard):
            peer = group * n_shard + shard
            pltpu.make_async_remote_copy(
                src_ref=source.at[pl.ds(pl.multiple_of(peer * pad, pad), pad), :],
                dst_ref=landing.at[pl.ds(pl.multiple_of(me * pad, pad), pad), :],
                send_sem=ssem,
                recv_sem=rsem,
                device_id=target(group, shard),
                device_id_type=MESH,
            ).start()

        each_device(start)
        own = pl.ds(pl.multiple_of(me * pad, pad), pad)
        landing[own, :] = source[own, :]

    def wait_bytes(ref, sem):
        pltpu.make_async_copy(ref, ref, sem).wait()

    def wait_rows(source, landing, ssem, rsem):
        rows = pl.ds(0, (devices - 1) * pad)
        wait_bytes(source.at[rows, :], ssem)
        wait_bytes(landing.at[rows, :], rsem)

    some = min(remote, 512)
    row_parts = [slice(r, r + some) for r in range(0, remote, some)]

    def make_picks(rows, off, width):
        lanes = lax.broadcasted_iota(i32, (some, LANE), 1) + off
        parts = [
            jnp.where(send_columns[rows, :] == lanes + LANE * j, 1.0, 0.0).astype(bf16)
            for j in range(width // LANE)
        ]
        return jnp.concatenate(parts, axis=1)

    def picks(rows, off):
        if picked.shape[0] == remote:
            return picked[rows, pl.ds(off, block)].astype(bf16)
        return make_picks(rows, off, block)

    def pick_rows(table, into):
        for rows in row_parts:
            if picked.shape[0] == remote:
                total = dot(picked[rows, :].astype(bf16), table[:, 0:nodes], NT)
            else:

                def add(i, total):
                    off = pl.multiple_of(i * block, block)
                    return total + dot(picks(rows, off), table[:, pl.ds(off, block)], NT)

                total = lax.fori_loop(0, blocks, add, jnp.zeros((some, table.shape[0]), f32))
            into[rows, :] = total.astype(bf16)

    total_counted = jnp.zeros((1, LANE), f32)
    lane_row = lax.broadcasted_iota(i32, (1, LANE), 1)
    for r in range(nodes // LANE):
        lanes = slice(r * LANE, (r + 1) * LANE)
        degree = deg_ref[r : r + 1, :].astype(f32)
        info[0:1, lanes] = 1.0 / degree
        info[3:4, lanes] = degree
        info[1:2, lanes] = label_ref[r : r + 1, :].astype(f32)
        counted = jnp.where(
            (lane_row + r * LANE < count_ref[0]) & (mask_ref[r : r + 1, :] > 0), 1.0, 0.0
        )
        info[2:3, lanes] = counted
        total_counted = total_counted + counted
    my_count = jnp.sum(total_counted, axis=1, keepdims=True)
    count_high = jnp.floor(my_count * (1.0 / 256.0))
    count_low = my_count - 256.0 * count_high

    table1[fin // 16 * 16 :, :] = jnp.zeros((fin_pad - fin // 16 * 16, nodes), bf16)
    table1[0:fin, :] = feat_ref[...]

    def split_in_two(value, into):
        value = value.astype(f32)
        largest = jnp.max(jnp.abs(value), axis=1, keepdims=True)
        scale = jnp.ones_like(largest)
        for power in (32, 16, 8, 4, 2, 1):
            larger = scale * 2.0**power
            scale = jnp.where(largest * larger <= 448.0, larger, scale)
        scaled = value * scale
        high = scaled.astype(narrow)
        into[0:fin_pad, :] = high
        into[fin_pad:, :] = ((scaled - high.astype(f32)) * 16.0).astype(narrow)
        return 1.0 / scale

    def joined_parts(both, unscale):
        return (both[0:fin_pad, :] + both[fin_pad:, :] * (1.0 / 16.0)) * unscale

    cap, slots = cfg["cap"], cfg["slots"]
    numbers = jnp.concatenate(
        [send_ref[...], jnp.full((pad - cap, devices), -256, i32)], axis=0
    )
    halves = jnp.concatenate([numbers >> 8, numbers & 255], axis=0).astype(f32).astype(bf16)
    for rows in row_parts:
        peers = lax.broadcasted_iota(i32, (some, devices), 1)
        row_numbers = lax.broadcasted_iota(i32, (some, devices), 0) + rows.start
        chosen = jnp.where(lax.div(row_numbers, pad) == peers, 1.0, 0.0).astype(bf16)
        found = dot(chosen, halves, NT)
        lanes = lax.broadcasted_iota(i32, (some, 2 * pad), 1)
        place = lax.rem(lax.broadcasted_iota(i32, (some, 2 * pad), 0), pad)
        found = jnp.where(lanes < pad, 256.0 * found, found)
        found = jnp.where(lax.rem(lanes, pad) == place, found, 0.0)
        column = jnp.sum(found, axis=1, keepdims=True)
        if picked.shape[0] == remote:
            high = jnp.floor(column * (1.0 / LOW))
            low = column - LOW * high
            send_columns[0] = jnp.broadcast_to(high, (remote, LANE)).astype(bf16)
            send_columns[1] = jnp.broadcast_to(low, (remote, LANE)).astype(bf16)
        else:
            send_columns[rows, :] = jnp.broadcast_to(column.astype(i32), (some, LANE))

    wsend[...] = jnp.zeros(wsend.shape, wire)
    wsend[:, 0:fin] = first_ref[:, 0:fin].astype(bf16).astype(wire)
    wsend[:, LANE : LANE + fin] = first_ref[:, fin : 2 * fin].astype(bf16).astype(wire)
    wsend[:, 3 * LANE + 4 * hid : 3 * LANE + 4 * hid + cls] = head_ref[...].astype(bf16).astype(wire)
    small = jnp.concatenate(
        [bias_ref[...], gain_ref[...], jnp.zeros((2, chunk), f32)], axis=0
    )
    wsend[:, 2 * LANE : 2 * LANE + 8] = small.T.astype(bf16).astype(wire)
    for level in range(2):
        lanes = slice(3 * LANE + level * 2 * hid, 3 * LANE + (level + 1) * 2 * hid)
        wsend[:, lanes] = rest_ref[level].astype(bf16).astype(wire)

    if picked.shape[0] == remote:

        low_lane = lax.broadcasted_iota(i32, (remote, LANE), 1).astype(f32)
        low_lanes = [(low_lane + LANE * half).astype(bf16) for half in range(LOW // LANE)]
        none, one_pick = jnp.zeros((remote, LANE), bf16), jnp.ones((remote, LANE), bf16)

        def store_picks(i, carry):
            here = jnp.full((remote, LANE), i.astype(f32)).astype(bf16)
            low = jnp.where(send_columns[0] == here, send_columns[1], none - 1)
            for half in range(LOW // LANE):
                lanes = pl.ds(pl.multiple_of(i * LOW + half * LANE, LANE), LANE)
                found = jnp.where(low == low_lanes[half], one_pick, none)
                picked[:, lanes] = found.astype(narrow)
            return carry

        lax.fori_loop(0, nodes // LOW, store_picks, 0)

    pick_rows(table1, out1)
    spare = lax.rem(lax.broadcasted_iota(i32, (remote, fin_pad), 0), pad)
    sent = out1[...].astype(f32)
    sent = jnp.where(spare == pad - 2, count_high, sent)
    sent = jnp.where(spare == pad - 1, count_low, sent)
    out1[...] = sent.astype(bf16)

    own_chunk = pl.ds(pl.multiple_of(my_shard * chunk, chunk), chunk)
    weight_parts = (
        slice(0, 3 * LANE),
        slice(3 * LANE, 3 * LANE + 2 * hid),
        slice(3 * LANE + 2 * hid, 4 * LANE + 4 * hid),
    )

    def send_weights(part):
        lanes = weight_parts[part]

        def start(group, shard):
            pltpu.make_async_remote_copy(
                src_ref=wsend.at[:, lanes],
                dst_ref=wwire.at[own_chunk, lanes],
                send_sem=w_ssem.at[part],
                recv_sem=w_rsem.at[part],
                device_id=target(group, shard),
                device_id_type=MESH,
            ).start()

        each_shard(start, my_group, 1)

    def wait_weights(part):
        lanes = weight_parts[part]
        rows = pl.ds(0, (n_shard - 1) * chunk)
        wait_bytes(wwire.at[rows, lanes], w_rsem.at[part])
        wait_bytes(wwire.at[rows, lanes], w_ssem.at[part])
        wfull[:, lanes] = wwire[:, lanes].astype(bf16)

    pl.semaphore_wait(barrier, devices - 1)
    start_rows(out1, in1, row_ssem.at[0], row_rsem.at[0])
    wwire[own_chunk, :] = wsend[...]
    send_weights(0)

    tiles = nodes // LANE
    for g in range(tiles):
        lanes = slice(g * LANE, (g + 1) * LANE)
        column = neighbour_ref[:, lanes]
        away = column - nodes
        source = ((away.astype(f32) + 0.5) * (1.0 / cap)).astype(i32)
        moved = jnp.where(away < 0, column, column + source * (pad - cap))
        live = lax.broadcasted_iota(i32, (slots, LANE), 0).astype(f32) < info[3:4, lanes]
        slot_rows[g * slots : (g + 1) * slots, :] = jnp.where(live, moved, -256)
    per_half = LANE // 16
    sixteenth = lax.div(lax.broadcasted_iota(i32, (tiles, LANE), 1), 16)
    for half in range(slots // per_half):
        made = [jnp.zeros((tiles, LANE), i32)] * per_half
        for j in range(per_half):
            rows = slot_rows[pl.ds(half * per_half + j, tiles, stride=slots), :]
            here = sixteenth == j
            for b in range(per_half):
                turned = pltpu.roll(rows, 16 * ((j - b) % per_half), 1) if j != b else rows
                made[b] = jnp.where(here, turned, made[b])
        lanes = slice(half * LANE, (half + 1) * LANE)
        for b in range(per_half):
            key_high[b, :, lanes] = (made[b] >> 8).astype(f32)
            key_low[b, :, lanes] = (made[b] & 255).astype(f32)

    high_rows = columns // LOW
    low_iota = lax.broadcasted_iota(i32, (LOW, LOW), 0).astype(f32).astype(bf16)
    same_node = (
        lax.rem(lax.broadcasted_iota(i32, (16, LOW), 1), 16)
        == lax.broadcasted_iota(i32, (16, LOW), 0)
    ).astype(f32).astype(bf16)
    zero_tile = jnp.zeros((16, LOW), bf16)
    one_low = jnp.ones((LOW, LOW), bf16)
    zero_low = jnp.zeros((LOW, LOW), bf16)
    group_rows = 32
    fold = group_rows // 16

    def build(it, carry):
        for k in range(0, 8, fold):
            made = []
            for kk in range(k, k + fold):
                high_row = jnp.broadcast_to(key_high[kk, pl.ds(it, 1), :], (16, LOW)).astype(bf16)
                low_row = jnp.broadcast_to(key_low[kk, pl.ds(it, 1), :], (16, LOW)).astype(bf16)
                left = jnp.concatenate(
                    [
                        jnp.where(high_row == jnp.asarray(h, bf16), same_node, zero_tile)
                        for h in range(high_rows)
                    ],
                    axis=0,
                ).astype(narrow)
                right = jnp.where(
                    low_iota == jnp.concatenate([low_row] * (LOW // 16), axis=0),
                    one_low,
                    zero_low,
                ).astype(narrow)
                made.append(dot(left, right, NT))
            row = pl.multiple_of(it * 128 + k * 16, group_rows)
            for h in range(high_rows):
                tile = jnp.concatenate([m[h * 16 : h * 16 + 16, :] for m in made], axis=0)
                counts[pl.ds(row, group_rows), h * LOW : (h + 1) * LOW] = tile.astype(
                    counts.dtype
                )
        return carry

    unscale_own = split_in_two(table1[...], first_own)
    spare_rows = slice(fin // 16 * 16, fin // 16 * 16 + 16)
    ones_row = lax.broadcasted_iota(i32, (16, nodes), 0) == fin % 16
    table1[spare_rows, :] = jnp.where(ones_row, 1.0, table1[spare_rows, :].astype(f32)).astype(
        bf16
    )
    lax.fori_loop(0, nodes // 256, build, 0)
    send_weights(1)
    lax.fori_loop(nodes // 256, nodes // 128, build, 0)

    wait_weights(0)
    weight_lanes = (
        slice(0, 2 * LANE),
        weight_parts[1],
        slice(3 * LANE + 2 * hid, 3 * LANE + 4 * hid),
    )
    small_full = wfull[:, 2 * LANE : 3 * LANE].astype(f32)
    for v in range(6):
        vectors[v] = jnp.broadcast_to(small_full[:, v : v + 1], (hid, LANE))

    def matrix(level):
        return wfull[:, weight_lanes[level]]

    wait_rows(out1, in1, row_ssem.at[0], row_rsem.at[0])
    received = in1[...].astype(f32)
    scale = jnp.where(spare == pad - 2, 256.0, jnp.where(spare == pad - 1, 1.0, 0.0))
    label_count = jnp.sum(received * scale, axis=0, keepdims=True)
    unscale_remote = split_in_two(
        jnp.where(spare < pad - 2, received, 0.0).T, first_remote
    )

    def c_block(off, lanes):
        return counts[pl.ds(off, block), lanes].astype(bf16)

    strips = [slice(r, r + STRIP) for r in range(0, hid, STRIP)]

    def fold_rows(value):
        return jnp.sum(value.reshape(STRIP // 8, 8, value.shape[1]), axis=0)

    def activate(level, keep_slope, kept, off, w):
        squares = jnp.zeros((8, block), f32)
        for st in strips:
            if kept is not None and keep_slope:
                b = kept[st, pl.ds(off, block)].astype(f32)
            else:
                b = before[w, st, :] + twice(vectors[level, st, :], block)
            if kept is not None and not keep_slope:
                kept[st, pl.ds(off, block)] = b.astype(kept.dtype)
            s = 0.5 + 0.5 * jnp.tanh(0.5 * b)
            a = b * s
            before[w, st, :] = a
            if keep_slope:
                slope[w, st, :] = s + a * (1.0 - s)
            squares = squares + fold_rows(a * a)
        mean_square = jnp.sum(squares, axis=0, keepdims=True) * (1.0 / hid)
        return lax.rsqrt(mean_square + norm_epsilon)

    def hidden_strip(level, st, inverse, w):
        scaled = before[w, st, :] * inverse
        return (twice(vectors[3 + level, st, :], block) * scaled).astype(bf16)

    def kept_or_none(kept):
        return kept if kept is not None and kept.shape[1] == nodes else None

    def forward_block(level, off, summed, table, mean, kept, keep_slope, w):
        lanes = pl.ds(off, block)
        mean_low = (summed * info[0:1, lanes]).astype(bf16)
        if mean is not None:
            mean[:, lanes] = mean_low
        joined = jnp.concatenate([table[:, lanes], mean_low], axis=0)
        before[w] = dot(matrix(level), joined, NN)
        yield
        return joined, activate(level, keep_slope, kept_or_none(kept), off, w)

    def run_blocks(make):
        def body(k, carry):
            live = [
                make(pl.multiple_of((k * streams + w) * block, block), w)
                for w in range(streams)
            ]
            ended, tick = set(), 0
            while len(ended) < streams:
                for w in range(streams):
                    if tick >= w and w not in ended:
                        if next(live[w], "end") == "end":
                            ended.add(w)
                tick += 1
            return carry

        lax.fori_loop(0, blocks // streams, body, 0)

    send_weights(2)
    def layer_one(off, w):
        rows = pl.ds(off, block)
        own = dot(first_own[...], counts[rows, 0:nodes], NT)
        away = dot(first_remote[...], counts[rows, nodes:], NT)
        yield
        summed = joined_parts(own, unscale_own) + joined_parts(away, unscale_remote)
        _, inverse = yield from forward_block(0, off, summed, table1, mean1, before1, False, w)
        yield
        for st in strips:
            table2[st, rows] = hidden_strip(0, st, inverse, w)

    run_blocks(layer_one)

    def own_sums(table):
        def add(i, carry):
            rows = pl.ds(pl.multiple_of(i * large, large), large)
            wide[:, rows] = dot(table[:, 0:nodes], counts[rows, 0:nodes].astype(bf16), NT)
            return carry

        lax.fori_loop(0, nodes // large, add, 0)

    def exchange_forward(table, x):
        pick_rows(table, outs)
        start_rows(outs, ins.at[x % 2], row_ssem.at[x + 1], row_rsem.at[x + 1])
        own_sums(table)
        wait_rows(outs, ins.at[x % 2], row_ssem.at[x + 1], row_rsem.at[x + 1])
        table[:, nodes:] = ins[x % 2].T

    def all_sums(table, off):
        return wide[:, pl.ds(off, block)] + dot(
            table[:, nodes:], c_block(off, slice(nodes, columns)), NT
        )

    exchange_forward(table2, 0)
    wait_weights(1)

    def layer_two(off, w):
        summed = all_sums(table2, off)
        yield
        _, inverse = yield from forward_block(1, off, summed, table2, mean2, before2, False, w)
        yield
        for st in strips:
            table3[st, pl.ds(off, block)] = hidden_strip(1, st, inverse, w)

    run_blocks(layer_two)

    exchange_forward(table3, 1)
    wait_weights(2)
    gfirst[...] = jnp.zeros(gfirst.shape, f32)
    ghead[...] = jnp.zeros(ghead.shape, f32)
    gfull[...] = jnp.zeros(gfull.shape, f32)
    gacc[...] = jnp.zeros(gacc.shape, f32)
    bacc[...] = jnp.zeros(bacc.shape, f32)
    head_low = wfull[:, 3 * LANE + 4 * hid :]
    cls_pad = round_up(cls, 16)
    one_over_count = 1.0 / label_count[0:1, 0:1]
    class_iota = lax.broadcasted_iota(i32, (cls_pad, block), 0)

    def backward_block(level, off, joined, inverse, need_input, w):
        lanes = pl.ds(off, block)
        crossed = jnp.zeros((8, block), f32)
        for st in strips:
            gain_term = ghid[w, st, :] * (before[w, st, :] * inverse)
            crossed = crossed + fold_rows(gain_term * twice(vectors[3 + level, st, :], block))
            gain_sum = gain_term[:, 0:LANE]
            for j in range(1, block // LANE):
                gain_sum = gain_sum + gain_term[:, j * LANE : (j + 1) * LANE]
            gacc[level, st, :] += gain_sum
        factor = jnp.sum(crossed, axis=0, keepdims=True) * (1.0 / hid) * inverse * inverse
        low_parts = []
        for st in strips:
            u = ghid[w, st, :] * twice(vectors[3 + level, st, :], block)
            low = (inverse * u - before[w, st, :] * factor) * slope[w, st, :]
            low_parts.append(low.astype(bf16))
        low = jnp.concatenate(low_parts, axis=0)
        yield
        into = gfirst if level == 0 else gfull.at[level - 1]
        added = dot(low, joined, NT)
        for j in range(joined.shape[0] // LANE):
            into[j] += added[:, j * LANE : (j + 1) * LANE]
        if need_input:
            bacc[level - 1] += dot(low, jnp.ones((LANE, block), bf16), NT)
            back = dot(matrix(level), low, TN)
            wide[:, lanes] = back[0:hid, :]
            gmean[:, lanes] = (back[hid:, :] * info[0:1, lanes]).astype(bf16)

    def layer_three(off, w):
        lanes = pl.ds(off, block)
        summed = all_sums(table3, off)
        yield
        joined, inverse = yield from forward_block(
            2, off, summed, table3, None, None, True, w
        )
        last = jnp.concatenate([hidden_strip(2, st, inverse, w) for st in strips], axis=0)
        yield
        logits = dot(head_low, last, TN)[0:cls_pad, :]
        yield
        logits = jnp.where(class_iota < cls, logits, -jnp.inf)
        highest = jnp.max(logits, axis=0, keepdims=True)
        shifted = logits - highest
        grown = jnp.exp(shifted)
        total = jnp.sum(grown, axis=0, keepdims=True)
        hot = class_iota == info[1:2, lanes].astype(i32)
        counted = info[2:3, lanes]
        chosen = jnp.sum(jnp.where(hot, shifted, 0.0), axis=0, keepdims=True)
        losses[w : w + 1, :] += (jnp.log(total) - chosen) * counted
        g_logits = (grown * (1.0 / total) - jnp.where(hot, 1.0, 0.0)) * (counted * one_over_count)
        g_low = jnp.concatenate(
            [g_logits, jnp.zeros((LANE - cls_pad, block), f32)], axis=0
        ).astype(bf16)
        yield
        ghead[...] += dot(last, g_low, NT)
        ghid[w] = dot(head_low, g_low, NN)
        yield
        yield from backward_block(2, off, joined, inverse, True, w)

    losses[...] = jnp.zeros(losses.shape, f32)
    run_blocks(layer_three)

    def start_first(seg):
        for piece in range(n_group):
            gwire[seg, piece] = gfull[seg, piece].astype(wire)

        def start(group, shard):
            pltpu.make_async_remote_copy(
                src_ref=gwire.at[seg, group],
                dst_ref=recv1.at[seg, my_group],
                send_sem=g_ssem.at[0, seg],
                recv_sem=g_rsem.at[0, seg],
                device_id=target(group, shard),
                device_id_type=MESH,
            ).start()

        each_group(start)
        recv1[seg, my_group] = jnp.zeros(recv1.shape[2:], wire)

    def start_second(seg):
        wait_bytes(gwire.at[seg, pl.ds(0, n_group - 1)], g_ssem.at[0, seg])
        wait_bytes(recv1.at[seg, pl.ds(0, n_group - 1)], g_rsem.at[0, seg])
        total = gfull[seg, my_group]
        for group in range(n_group):
            total = total + recv1[seg, group].astype(f32)
        gfull[seg, my_group] = total
        send2[seg] = total.astype(wire).reshape(n_shard, chunk, LANE)

        def start(group, shard):
            pltpu.make_async_remote_copy(
                src_ref=send2.at[seg, shard],
                dst_ref=recv2.at[seg, my_shard],
                send_sem=g_ssem.at[1, seg],
                recv_sem=g_rsem.at[1, seg],
                device_id=target(group, shard),
                device_id_type=MESH,
            ).start()

        each_shard(start, my_group, 1)
        recv2[seg, my_shard] = jnp.zeros(recv2.shape[2:], wire)

    def start_third(seg):
        wait_bytes(send2.at[seg, pl.ds(0, n_shard - 1)], g_ssem.at[1, seg])
        wait_bytes(recv2.at[seg, pl.ds(0, n_shard - 1)], g_rsem.at[1, seg])
        total = gfull[seg, my_group, own_chunk, :]
        for shard in range(n_shard):
            total = total + recv2[seg, shard].astype(f32)
        part3[seg] = total

        def start(group, shard):
            pltpu.make_async_remote_copy(
                src_ref=part3.at[seg],
                dst_ref=recv3.at[seg, my_group],
                send_sem=g_ssem.at[2, seg],
                recv_sem=g_rsem.at[2, seg],
                device_id=target(group, shard),
                device_id_type=MESH,
            ).start()

        each_group(start)
        recv3[seg, my_group] = total
        return jnp.sum(total * total, axis=0, keepdims=True)

    def wait_third(seg):
        for _ in range(n_group - 1):
            wait_bytes(part3.at[seg], g_ssem.at[2, seg])
        wait_bytes(recv3.at[seg, pl.ds(0, n_group - 1)], g_rsem.at[2, seg])

    def bias_and_gain(levels, first_lane):
        lane_wide = lax.broadcasted_iota(i32, (hid, LANE), 1)
        total = jnp.zeros((hid, LANE), f32)
        for n, level in enumerate(levels):
            found = jnp.sum(gacc[level], axis=1, keepdims=True)
            total = jnp.where(lane_wide == first_lane + len(levels) + n, found, total)
            if level > 0:
                total = jnp.where(lane_wide == first_lane + n, bacc[level - 1], total)
        return total

    def start_head():
        total = ghead[...] + bias_and_gain((1, 2), cls)
        ghead[...] = total
        hwire[...] = total.astype(wire).reshape(n_shard, chunk, LANE)

        def start(group, shard):
            pltpu.make_async_remote_copy(
                src_ref=hwire.at[shard],
                dst_ref=hrecv.at[my_shard],
                send_sem=h_ssem.at[0],
                recv_sem=h_rsem.at[0],
                device_id=target(group, shard),
                device_id_type=MESH,
            ).start()

        each_shard(start, my_group, 1)
        hrecv[my_shard] = jnp.zeros(hrecv.shape[1:], wire)

    def share_head():
        wait_bytes(hwire.at[pl.ds(0, n_shard - 1)], h_ssem.at[0])
        wait_bytes(hrecv.at[pl.ds(0, n_shard - 1)], h_rsem.at[0])
        total = ghead[own_chunk, :]
        for shard in range(n_shard):
            total = total + hrecv[shard].astype(f32)
        hpart[...] = total

        def start(group, shard):
            pltpu.make_async_remote_copy(
                src_ref=hpart,
                dst_ref=hfinal.at[my_group],
                send_sem=h_ssem.at[1],
                recv_sem=h_rsem.at[1],
                device_id=target(group, shard),
                device_id_type=MESH,
            ).start()

        each_group(start)
        hfinal[my_group] = total

    def wait_head():
        wait_bytes(hfinal.at[pl.ds(0, n_group - 1)], h_ssem.at[1])
        wait_bytes(hfinal.at[pl.ds(0, n_group - 1)], h_rsem.at[1])
        total = hfinal[0]
        for group in range(1, n_group):
            total = total + hfinal[group]
        head_out[...] = total
        return jnp.sum(total * total, axis=0, keepdims=True) * (1.0 / n_group)

    units, unit_rows, row_parts_first = cfg["units"], cfg["unit_rows"], cfg["units"] // 2

    def start_first_layer():
        gfirst[0] += bias_and_gain((0,), fin)
        for unit in range(units):
            tile, part = unit // row_parts_first, unit % row_parts_first
            whole = gfirst[tile].reshape(n_shard, chunk, LANE)
            fwire[unit] = whole[:, part * unit_rows : (part + 1) * unit_rows, :].astype(wire)

        def start(group, shard):
            pltpu.make_async_remote_copy(
                src_ref=fwire.at[lax.rem(group, units), shard],
                dst_ref=frecv.at[me],
                send_sem=f_ssem.at[0],
                recv_sem=f_rsem.at[0],
                device_id=target(group, shard),
                device_id_type=MESH,
            ).start()

        each_device(start)
        frecv[me] = fwire[lax.rem(my_group, units), my_shard]

    def share_first_layer():
        wait_bytes(frecv.at[pl.ds(0, devices - 1)], f_ssem.at[0])
        wait_bytes(frecv.at[pl.ds(0, devices - 1)], f_rsem.at[0])
        total = jnp.sum(frecv[...].astype(f32), axis=0)
        fpart[...] = total

        def start(group, shard):
            pltpu.make_async_remote_copy(
                src_ref=fpart,
                dst_ref=ffinal.at[my_group],
                send_sem=f_ssem.at[1],
                recv_sem=f_rsem.at[1],
                device_id=target(group, shard),
                device_id_type=MESH,
            ).start()

        each_group(start)
        ffinal[my_group] = total
        return jnp.sum(total * total, axis=0, keepdims=True) * (units / n_group)

    def wait_first_layer():
        wait_bytes(ffinal.at[pl.ds(0, n_group - 1)], f_ssem.at[1])
        wait_bytes(ffinal.at[pl.ds(0, n_group - 1)], f_rsem.at[1])
        for unit in range(units):
            tile, part = unit // row_parts_first, unit % row_parts_first
            first_out[tile, part * unit_rows : (part + 1) * unit_rows, :] = ffinal[unit]

    def exchange_backward(x, meanwhile):
        for rows in row_parts:
            lanes = slice(nodes + rows.start, nodes + rows.stop)
            back = dot(gmean[...], counts[:, lanes].astype(bf16), NN)
            outs[rows, :] = back.astype(bf16).T
        start_rows(outs, ins.at[x % 2], row_ssem.at[x + 1], row_rsem.at[x + 1])
        meanwhile()

        def add(i, carry):
            lanes = pl.ds(pl.multiple_of(i * large, large), large)
            wide[:, lanes] += dot(gmean[...], counts[:, lanes].astype(bf16), NN)
            return carry

        lax.fori_loop(0, nodes // large, add, 0)
        wait_rows(outs, ins.at[x % 2], row_ssem.at[x + 1], row_rsem.at[x + 1])

    def returned(x, off):
        total = wide[:, pl.ds(off, block)]
        for rows in row_parts:
            total = total + dot(ins[x % 2, rows, :], picks(rows, off), TN)
        return total

    exchange_backward(2, lambda: start_first(1))
    start_second(1)

    def backward_two(off, w):
        lanes = pl.ds(off, block)
        ghid[w] = returned(2, off)
        joined = jnp.concatenate([table2[:, lanes], mean2[:, lanes]], axis=0)
        if before2.shape[1] < nodes:
            before[w] = dot(matrix(1), joined, NN)
        yield
        inverse = activate(1, True, kept_or_none(before2), off, w)
        yield from backward_block(1, off, joined, inverse, True, w)

    run_blocks(backward_two)

    def meanwhile():
        start_first(0)
        start_head()

    exchange_backward(3, meanwhile)
    square = start_third(1)
    start_second(0)
    share_head()

    def backward_one(off, w):
        lanes = pl.ds(off, block)
        ghid[w] = returned(3, off)
        joined = jnp.concatenate([table1[:, lanes], mean1[:, lanes]], axis=0)
        if before1.shape[1] < nodes:
            before[w] = dot(matrix(0), joined, NN)
        yield
        inverse = activate(0, True, kept_or_none(before1), off, w)
        yield from backward_block(0, off, joined, inverse, False, w)

    run_blocks(backward_one)
    start_first_layer()
    square = square + start_third(0) + wait_head()
    square = square + share_first_layer()

    row_of = lax.broadcasted_iota(i32, (8, LANE), 0)
    loss_row = jnp.sum(losses[...], axis=0, keepdims=True)
    loss_row = sum(loss_row[:, j * LANE : (j + 1) * LANE] for j in range(block // LANE))
    mine = jnp.where(row_of == 0, square, jnp.where(row_of == 1, loss_row, 0.0))
    scal_send[...] = mine

    def send_scalars(group, shard):
        pltpu.make_async_remote_copy(
            src_ref=scal_send.at[pl.ds(0, 2), :],
            dst_ref=scal_recv.at[me, pl.ds(0, 2), :],
            send_sem=s_ssem,
            recv_sem=s_rsem,
            device_id=target(group, shard),
            device_id_type=MESH,
        ).start()

    each_device(send_scalars)
    scal_recv[me] = mine
    for seg in range(2):
        wait_third(seg)
    part_out[...] = recv3[...]
    wait_first_layer()
    others = scal_recv.at[pl.ds(0, devices - 1), pl.ds(0, 2), :]
    wait_bytes(others, s_rsem)
    wait_bytes(others, s_ssem)
    totals = jnp.sum(scal_recv[:, 0:2, :], axis=0)
    scalar_out[0:2, :] = totals
    scalar_out[2:3, :] = label_count


def adamw(weight, grad, moment, square, rate, decay):
    moment_new = beta_one * moment + (1.0 - beta_one) * grad
    square_new = beta_two * square + (1.0 - beta_two) * grad * grad
    moment_hat = moment_new / (1.0 - beta_one**STEP)
    square_hat = square_new / (1.0 - beta_two**STEP)
    weight_new = weight - rate * (
        moment_hat / (jnp.sqrt(square_hat) + adam_epsilon) + decay * weight
    )
    return (weight_new, moment_new, square_new)


def update_kernel(fin, cls, part_ref, head_ref, first_ref, scalar_ref, *refs):
    states = [refs[3 * k : 3 * k + 3] for k in range(5)]
    outs = [refs[15 + 3 * k : 18 + 3 * k] for k in range(5)]
    copies = refs[30:33]
    loss_out, count_out, norm_out = refs[33:36]
    norm = jnp.sqrt(jnp.sum(scalar_ref[0:1, :], axis=1, keepdims=True))
    loss_out[...] = jnp.sum(scalar_ref[1:2, :], axis=1, keepdims=True)
    count_out[...] = scalar_ref[2:3, 0:1]
    norm_out[...] = norm
    factor = jnp.minimum(1.0, threshold / norm)
    small_last = head_ref[...].T
    small_first = first_ref[0].T
    bias = jnp.concatenate([small_first[fin : fin + 1], small_last[cls : cls + 2]], axis=0)
    gain = jnp.concatenate(
        [small_first[fin + 1 : fin + 2], small_last[cls + 2 : cls + 4]], axis=0
    )

    def update(k, grad, where, rate, decay):
        news = adamw(
            states[k][0][where], grad * factor, states[k][1][where], states[k][2][where], rate, decay
        )
        for out, new in zip(outs[k], news):
            out[where] = new
        if k < 3:
            copies[k][where] = news[0].astype(bf16)

    everything = (slice(None), slice(None))
    update(0, first_ref[0][:, 0:fin], (slice(None), slice(0, fin)), 0.05, 0.01)
    update(0, first_ref[1][:, 0:fin], (slice(None), slice(fin, 2 * fin)), 0.05, 0.01)
    n_group = part_ref.shape[1]
    for level in range(2):
        for piece in range(n_group):
            lanes = slice(piece * LANE, (piece + 1) * LANE)
            update(1, part_ref[level, piece], (level, slice(None), lanes), 0.05, 0.01)
    update(2, head_ref[:, 0:cls], everything, 0.05, 0.01)
    update(3, bias, everything, 0.3, 0.0)
    update(4, gain, everything, 0.3, 0.0)


def per_device(
    n_group,
    n_shard,
    features,
    node_counts,
    degrees,
    neighbours,
    send_rows,
    labels,
    train_mask,
    weight_first,
    weight_rest,
    weight_head,
    biases,
    gains,
    moment_first,
    square_first,
    moment_rest,
    square_rest,
    moment_head,
    square_head,
    moment_bias,
    square_bias,
    moment_gain,
    square_gain,
):
    nodes, fin = features.shape
    devices = n_group * n_shard
    hid = weight_rest.shape[1] // 2
    chunk = hid // n_shard
    cls = weight_head.shape[1]
    cap = send_rows.shape[1]
    slots = neighbours.shape[1]
    pad = round_up(cap + 2, 16)
    remote = devices * pad
    columns = nodes + remote
    roomy = remote <= 512
    block, streams, large = (1024, 2, 2048) if roomy else (512, 1, 512)
    wire = bf16 if chunk % 16 == 0 else f32
    least = 16 if wire == bf16 else 8
    units = n_group if chunk * 2 // n_group >= least else 2
    unit_rows = chunk * 2 // units
    fin_pad = LANE
    cfg = dict(
        n_group=n_group,
        n_shard=n_shard,
        nodes=nodes,
        fin=fin,
        cls=cls,
        pad=pad,
        remote=remote,
        chunk=chunk,
        wire=wire,
        block=block,
        streams=streams,
        large=large,
        fin_pad=fin_pad,
        hid=hid,
        cap=cap,
        slots=slots,
        units=units,
        unit_rows=unit_rows,
    )

    vmem = pl.BlockSpec(memory_space=pltpu.VMEM)
    smem = pl.BlockSpec(memory_space=pltpu.SMEM)
    width = 4 * LANE + 4 * hid
    dma = pltpu.SemaphoreType.DMA
    stored = remote if remote <= 512 else 32
    kept_nodes = nodes if remote <= 512 else LANE
    scratch = [
        pltpu.VMEM((nodes, columns), narrow),
        pltpu.VMEM((stored, nodes), narrow),
        pltpu.VMEM((2, remote, LANE), bf16) if roomy else pltpu.VMEM((remote, LANE), i32),
        pltpu.VMEM((nodes // LANE * slots, LANE), i32),
        pltpu.VMEM((8, nodes // LANE, LOW), f32),
        pltpu.VMEM((8, nodes // LANE, LOW), f32),
        pltpu.VMEM((fin_pad, nodes), bf16),
        pltpu.VMEM((hid, columns), bf16),
        pltpu.VMEM((hid, columns), bf16),
        pltpu.VMEM((2 * fin_pad, nodes), narrow),
        pltpu.VMEM((2 * fin_pad, remote), narrow),
        pltpu.VMEM((fin_pad, nodes), bf16),
        pltpu.VMEM((hid, nodes), bf16),
        pltpu.VMEM((hid, kept_nodes), bf16),
        pltpu.VMEM((hid, kept_nodes), f32),
        pltpu.VMEM((hid, nodes), bf16),
        pltpu.VMEM((hid, nodes), f32),
        pltpu.VMEM((remote, hid), bf16),
        pltpu.VMEM((2, remote, hid), bf16),
        pltpu.VMEM((8, nodes), f32),
        pltpu.VMEM((chunk, width), wire),
        pltpu.VMEM((hid, width), wire),
        pltpu.VMEM((hid, width), bf16),
        pltpu.VMEM((6, hid, LANE), f32),
        pltpu.VMEM((streams, hid, block), f32),
        pltpu.VMEM((streams, hid, block), f32),
        pltpu.VMEM((streams, hid, block), f32),
        pltpu.VMEM((8, block), f32),
        pltpu.VMEM((3, hid, LANE), f32),
        pltpu.VMEM((2, hid, LANE), f32),
        pltpu.VMEM((2, n_group, hid, LANE), f32),
        pltpu.VMEM((2, n_group, hid, LANE), wire),
        pltpu.VMEM((2, n_group, hid, LANE), wire),
        pltpu.VMEM((2, n_shard, chunk, LANE), wire),
        pltpu.VMEM((2, n_shard, chunk, LANE), wire),
        pltpu.VMEM((2, chunk, LANE), f32),
        pltpu.VMEM((2, n_group, chunk, LANE), f32),
        pltpu.VMEM((2, hid, LANE), f32),
        pltpu.VMEM((units, n_shard, unit_rows, LANE), wire),
        pltpu.VMEM((devices, unit_rows, LANE), wire),
        pltpu.VMEM((unit_rows, LANE), f32),
        pltpu.VMEM((n_group, unit_rows, LANE), f32),
        pltpu.VMEM((hid, LANE), f32),
        pltpu.VMEM((n_shard, chunk, LANE), wire),
        pltpu.VMEM((n_shard, chunk, LANE), wire),
        pltpu.VMEM((chunk, LANE), f32),
        pltpu.VMEM((n_group, chunk, LANE), f32),
        pltpu.VMEM((8, LANE), f32),
        pltpu.VMEM((devices, 8, LANE), f32),
        dma((5,)),
        dma((5,)),
        dma((3,)),
        dma((3,)),
        dma((3, 2)),
        dma((3, 2)),
        dma((2,)),
        dma((2,)),
        dma((2,)),
        dma((2,)),
        dma,
        dma,
    ]
    sums = pl.pallas_call(
        functools.partial(step_kernel, cfg),
        out_shape=(
            jax.ShapeDtypeStruct((2, n_group, chunk, LANE), f32),
            jax.ShapeDtypeStruct((chunk, LANE), f32),
            jax.ShapeDtypeStruct((2, chunk, LANE), f32),
            jax.ShapeDtypeStruct((8, LANE), f32),
        ),
        in_specs=[vmem] * 5 + [smem] + [vmem] * 6,
        out_specs=(vmem,) * 4,
        scratch_shapes=scratch,
        compiler_params=pltpu.CompilerParams(
            collective_id=0, has_side_effects=True, vmem_limit_bytes=63 * 2**20
        ),
    )(
        features.T,
        neighbours.T,
        degrees.reshape(nodes // LANE, LANE),
        labels.reshape(nodes // LANE, LANE),
        train_mask.reshape(nodes // LANE, LANE),
        node_counts,
        send_rows.T,
        weight_first.T,
        weight_rest.transpose(0, 2, 1),
        weight_head,
        biases,
        gains,
    )
    turned = lambda value: value.T
    turned_rest = lambda value: value.transpose(0, 2, 1)
    same = lambda value: value
    turns = (turned, turned_rest, same, same, same)
    states = (
        (weight_first, moment_first, square_first),
        (weight_rest, moment_rest, square_rest),
        (weight_head, moment_head, square_head),
        (biases, moment_bias, square_bias),
        (gains, moment_gain, square_gain),
    )
    flat = [turn(value) for turn, three in zip(turns, states) for value in three]
    shapes = [jax.ShapeDtypeStruct(value.shape, f32) for value in flat]
    shapes += [jax.ShapeDtypeStruct(flat[3 * k].shape, bf16) for k in range(3)]
    shapes += [jax.ShapeDtypeStruct((1, 1), f32)] * 3
    updated = pl.pallas_call(
        functools.partial(update_kernel, fin, cls),
        out_shape=tuple(shapes),
        in_specs=[vmem] * (4 + len(flat)),
        out_specs=(vmem,) * len(shapes),
    )(*sums, *flat)
    news = tuple(turns[k // 3](updated[k]) for k in range(15))
    copies = tuple(turns[k](updated[15 + k]) for k in range(3))
    return tuple(value.reshape(()) for value in updated[18:]) + news + copies


def solution(mesh):
    nodes_split = P(("group", "shard"))
    nodes_rows = P(("group", "shard"), None)
    first = P(None, "shard")
    rest = P(None, None, "shard")
    head = P("shard", None)
    return jax.shard_map(
        functools.partial(per_device, mesh.shape["group"], mesh.shape["shard"]),
        mesh=mesh,
        in_specs=(
            nodes_rows,
            nodes_split,
            nodes_split,
            nodes_rows,
            nodes_rows,
            nodes_split,
            nodes_split,
            first,
            rest,
            head,
            first,
            first,
            first,
            first,
            rest,
            rest,
            head,
            head,
            first,
            first,
            first,
            first,
        ),
        out_specs=(P(), P(), P())
        + (first,) * 3
        + (rest,) * 3
        + (head,) * 3
        + (first,) * 6
        + (first, rest, head),
        check_vma=False,
    )
```

```python
import functools

import jax
import jax.numpy as jnp
from jax import lax
from jax.experimental import pallas as pl
from jax.experimental.pallas import tpu as pltpu
from jax.sharding import PartitionSpec as P

STEP = 10
MESH = pl.DeviceIdType.MESH
bf16 = jnp.bfloat16
f32 = jnp.float32
i32 = jnp.int32

norm_epsilon = 1e-05
threshold = 0.002
beta_one = 0.5
beta_two = 0.5
adam_epsilon = 1e-08

LANE = 128
LOW = 256
narrow = jnp.float8_e4m3fn
STRIP = 32

NN = (((1,), (0,)), ((), ()))
NT = (((1,), (1,)), ((), ()))
TN = (((0,), (0,)), ((), ()))


def dot(a, b, dims):
    return lax.dot_general(a, b, dims, preferred_element_type=f32)


def round_up(value, unit):
    return -(-value // unit) * unit


def twice(half, width):
    return jnp.concatenate([half] * (width // LANE), axis=1)


def step_kernel(
    cfg,
    feat_ref,
    neighbour_ref,
    deg_ref,
    label_ref,
    mask_ref,
    count_ref,
    send_ref,
    first_ref,
    rest_ref,
    head_ref,
    bias_ref,
    gain_ref,
    part_out,
    head_out,
    first_out,
    scalar_out,
    counts,
    picked,
    send_columns,
    slot_rows,
    key_high,
    key_low,
    table1,
    table2,
    table3,
    first_own,
    first_remote,
    mean1,
    mean2,
    before1,
    before2,
    gmean,
    wide,
    outs,
    ins,
    info,
    wsend,
    wwire,
    wfull,
    vectors,
    before,
    slope,
    ghid,
    losses,
    gacc,
    bacc,
    gfull,
    gwire,
    recv1,
    send2,
    recv2,
    part3,
    recv3,
    gfirst,
    fwire,
    frecv,
    fpart,
    ffinal,
    ghead,
    hwire,
    hrecv,
    hpart,
    hfinal,
    scal_send,
    scal_recv,
    row_ssem,
    row_rsem,
    w_ssem,
    w_rsem,
    g_ssem,
    g_rsem,
    f_ssem,
    f_rsem,
    h_ssem,
    h_rsem,
    s_ssem,
    s_rsem,
):
    n_group, n_shard = cfg["n_group"], cfg["n_shard"]
    nodes, fin, cls = cfg["nodes"], cfg["fin"], cfg["cls"]
    pad, remote, chunk, wire = cfg["pad"], cfg["remote"], cfg["chunk"], cfg["wire"]
    block, fin_pad, hid = cfg["block"], cfg["fin_pad"], cfg["hid"]
    devices = n_group * n_shard
    columns = nodes + remote
    my_group, my_shard = lax.axis_index("group"), lax.axis_index("shard")
    me = my_group * n_shard + my_shard
    blocks = nodes // block
    streams, large = cfg["streams"], cfg["large"]

    def target(group, shard):
        return {"group": group, "shard": shard}

    out1, in1 = outs.at[:, pl.ds(0, fin_pad)], ins.at[1, :, pl.ds(0, fin_pad)]

    barrier = pltpu.get_barrier_semaphore()

    def greet(group, shard):
        pl.semaphore_signal(
            barrier, inc=1, device_id=target(group, shard), device_id_type=MESH
        )

    def each_shard(action, group, first):
        if n_shard <= 8:
            for i in range(first, n_shard):
                action(group, lax.rem(my_shard + i, n_shard))
        else:

            def run(i, carry):
                action(group, lax.rem(my_shard + i, n_shard))
                return carry

            lax.fori_loop(first, n_shard, run, 0)

    def each_group(action):
        for i in range(1, n_group):
            action(lax.rem(my_group + i, n_group), my_shard)

    def each_device(action):
        for i in range(n_group):
            each_shard(action, lax.rem(my_group + i, n_group), 1 if i == 0 else 0)

    each_device(greet)

    def start_rows(source, landing, ssem, rsem):
        def start(group, shard):
            peer = group * n_shard + shard
            pltpu.make_async_remote_copy(
                src_ref=source.at[pl.ds(pl.multiple_of(peer * pad, pad), pad), :],
                dst_ref=landing.at[pl.ds(pl.multiple_of(me * pad, pad), pad), :],
                send_sem=ssem,
                recv_sem=rsem,
                device_id=target(group, shard),
                device_id_type=MESH,
            ).start()

        each_device(start)
        own = pl.ds(pl.multiple_of(me * pad, pad), pad)
        landing[own, :] = source[own, :]

    def wait_bytes(ref, sem):
        pltpu.make_async_copy(ref, ref, sem).wait()

    def wait_rows(source, landing, ssem, rsem):
        rows = pl.ds(0, (devices - 1) * pad)
        wait_bytes(source.at[rows, :], ssem)
        wait_bytes(landing.at[rows, :], rsem)

    some = min(remote, 512)
    row_parts = [slice(r, r + some) for r in range(0, remote, some)]

    def make_picks(rows, off, width):
        lanes = lax.broadcasted_iota(i32, (some, LANE), 1) + off
        parts = [
            jnp.where(send_columns[rows, :] == lanes + LANE * j, 1.0, 0.0).astype(bf16)
            for j in range(width // LANE)
        ]
        return jnp.concatenate(parts, axis=1)

    def picks(rows, off):
        if picked.shape[0] == remote:
            return picked[rows, pl.ds(off, block)].astype(bf16)
        return make_picks(rows, off, block)

    def pick_rows(table, into):
        for rows in row_parts:
            if picked.shape[0] == remote:
                total = dot(picked[rows, :].astype(bf16), table[:, 0:nodes], NT)
            else:

                def add(i, total):
                    off = pl.multiple_of(i * block, block)
                    return total + dot(picks(rows, off), table[:, pl.ds(off, block)], NT)

                total = lax.fori_loop(0, blocks, add, jnp.zeros((some, table.shape[0]), f32))
            into[rows, :] = total.astype(bf16)

    total_counted = jnp.zeros((1, LANE), f32)
    lane_row = lax.broadcasted_iota(i32, (1, LANE), 1)
    for r in range(nodes // LANE):
        lanes = slice(r * LANE, (r + 1) * LANE)
        degree = deg_ref[r : r + 1, :].astype(f32)
        info[0:1, lanes] = 1.0 / degree
        info[3:4, lanes] = degree
        info[1:2, lanes] = label_ref[r : r + 1, :].astype(f32)
        counted = jnp.where(
            (lane_row + r * LANE < count_ref[0]) & (mask_ref[r : r + 1, :] > 0), 1.0, 0.0
        )
        info[2:3, lanes] = counted
        total_counted = total_counted + counted
    my_count = jnp.sum(total_counted, axis=1, keepdims=True)
    count_high = jnp.floor(my_count * (1.0 / 256.0))
    count_low = my_count - 256.0 * count_high

    table1[fin // 16 * 16 :, :] = jnp.zeros((fin_pad - fin // 16 * 16, nodes), bf16)
    table1[0:fin, :] = feat_ref[...]

    def split_in_two(value, into):
        value = value.astype(f32)
        largest = jnp.max(jnp.abs(value), axis=1, keepdims=True)
        scale = jnp.ones_like(largest)
        for power in (32, 16, 8, 4, 2, 1):
            larger = scale * 2.0**power
            scale = jnp.where(largest * larger <= 448.0, larger, scale)
        scaled = value * scale
        high = scaled.astype(narrow)
        into[0:fin_pad, :] = high
        into[fin_pad:, :] = ((scaled - high.astype(f32)) * 16.0).astype(narrow)
        return 1.0 / scale

    def joined_parts(both, unscale):
        return (both[0:fin_pad, :] + both[fin_pad:, :] * (1.0 / 16.0)) * unscale

    cap, slots = cfg["cap"], cfg["slots"]
    numbers = jnp.concatenate(
        [send_ref[...], jnp.full((pad - cap, devices), -256, i32)], axis=0
    )
    halves = jnp.concatenate([numbers >> 8, numbers & 255], axis=0).astype(f32).astype(bf16)
    for rows in row_parts:
        peers = lax.broadcasted_iota(i32, (some, devices), 1)
        row_numbers = lax.broadcasted_iota(i32, (some, devices), 0) + rows.start
        chosen = jnp.where(lax.div(row_numbers, pad) == peers, 1.0, 0.0).astype(bf16)
        found = dot(chosen, halves, NT)
        lanes = lax.broadcasted_iota(i32, (some, 2 * pad), 1)
        place = lax.rem(lax.broadcasted_iota(i32, (some, 2 * pad), 0), pad)
        found = jnp.where(lanes < pad, 256.0 * found, found)
        found = jnp.where(lax.rem(lanes, pad) == place, found, 0.0)
        column = jnp.sum(found, axis=1, keepdims=True)
        if picked.shape[0] == remote:
            high = jnp.floor(column * (1.0 / LOW))
            low = column - LOW * high
            send_columns[0] = jnp.broadcast_to(high, (remote, LANE)).astype(bf16)
            send_columns[1] = jnp.broadcast_to(low, (remote, LANE)).astype(bf16)
        else:
            send_columns[rows, :] = jnp.broadcast_to(column.astype(i32), (some, LANE))

    wsend[...] = jnp.zeros(wsend.shape, wire)
    wsend[:, 0:fin] = first_ref[:, 0:fin].astype(bf16).astype(wire)
    wsend[:, LANE : LANE + fin] = first_ref[:, fin : 2 * fin].astype(bf16).astype(wire)
    wsend[:, 3 * LANE + 4 * hid : 3 * LANE + 4 * hid + cls] = head_ref[...].astype(bf16).astype(wire)
    small = jnp.concatenate(
        [bias_ref[...], gain_ref[...], jnp.zeros((2, chunk), f32)], axis=0
    )
    wsend[:, 2 * LANE : 2 * LANE + 8] = small.T.astype(bf16).astype(wire)
    for level in range(2):
        lanes = slice(3 * LANE + level * 2 * hid, 3 * LANE + (level + 1) * 2 * hid)
        wsend[:, lanes] = rest_ref[level].astype(bf16).astype(wire)

    if picked.shape[0] == remote:

        low_lane = lax.broadcasted_iota(i32, (remote, LANE), 1).astype(f32)
        low_lanes = [(low_lane + LANE * half).astype(bf16) for half in range(LOW // LANE)]
        none, one_pick = jnp.zeros((remote, LANE), bf16), jnp.ones((remote, LANE), bf16)

        def store_picks(i, carry):
            here = jnp.full((remote, LANE), i.astype(f32)).astype(bf16)
            low = jnp.where(send_columns[0] == here, send_columns[1], none - 1)
            for half in range(LOW // LANE):
                lanes = pl.ds(pl.multiple_of(i * LOW + half * LANE, LANE), LANE)
                found = jnp.where(low == low_lanes[half], one_pick, none)
                picked[:, lanes] = found.astype(narrow)
            return carry

        lax.fori_loop(0, nodes // LOW, store_picks, 0)

    pick_rows(table1, out1)
    spare = lax.rem(lax.broadcasted_iota(i32, (remote, fin_pad), 0), pad)
    sent = out1[...].astype(f32)
    sent = jnp.where(spare == pad - 2, count_high, sent)
    sent = jnp.where(spare == pad - 1, count_low, sent)
    out1[...] = sent.astype(bf16)

    own_chunk = pl.ds(pl.multiple_of(my_shard * chunk, chunk), chunk)
    weight_parts = (
        slice(0, 3 * LANE),
        slice(3 * LANE, 3 * LANE + 2 * hid),
        slice(3 * LANE + 2 * hid, 4 * LANE + 4 * hid),
    )

    def send_weights(part):
        lanes = weight_parts[part]

        def start(group, shard):
            pltpu.make_async_remote_copy(
                src_ref=wsend.at[:, lanes],
                dst_ref=wwire.at[own_chunk, lanes],
                send_sem=w_ssem.at[part],
                recv_sem=w_rsem.at[part],
                device_id=target(group, shard),
                device_id_type=MESH,
            ).start()

        each_shard(start, my_group, 1)

    def wait_weights(part):
        lanes = weight_parts[part]
        rows = pl.ds(0, (n_shard - 1) * chunk)
        wait_bytes(wwire.at[rows, lanes], w_rsem.at[part])
        wait_bytes(wwire.at[rows, lanes], w_ssem.at[part])
        wfull[:, lanes] = wwire[:, lanes].astype(bf16)

    gfirst[...] = jnp.zeros(gfirst.shape, f32)
    ghead[...] = jnp.zeros(ghead.shape, f32)
    gfull[...] = jnp.zeros(gfull.shape, f32)
    gacc[...] = jnp.zeros(gacc.shape, f32)
    bacc[...] = jnp.zeros(bacc.shape, f32)
    losses[...] = jnp.zeros(losses.shape, f32)

    pl.semaphore_wait(barrier, devices - 1)
    start_rows(out1, in1, row_ssem.at[0], row_rsem.at[0])
    wwire[own_chunk, :] = wsend[...]
    send_weights(0)

    tiles = nodes // LANE
    for g in range(tiles):
        lanes = slice(g * LANE, (g + 1) * LANE)
        column = neighbour_ref[:, lanes]
        away = column - nodes
        source = ((away.astype(f32) + 0.5) * (1.0 / cap)).astype(i32)
        moved = jnp.where(away < 0, column, column + source * (pad - cap))
        live = lax.broadcasted_iota(i32, (slots, LANE), 0).astype(f32) < info[3:4, lanes]
        slot_rows[g * slots : (g + 1) * slots, :] = jnp.where(live, moved, -256)
    per_half = LANE // 16
    sixteenth = lax.div(lax.broadcasted_iota(i32, (tiles, LANE), 1), 16)
    for half in range(slots // per_half):
        made = [jnp.zeros((tiles, LANE), i32)] * per_half
        for j in range(per_half):
            rows = slot_rows[pl.ds(half * per_half + j, tiles, stride=slots), :]
            here = sixteenth == j
            for b in range(per_half):
                turned = pltpu.roll(rows, 16 * ((j - b) % per_half), 1) if j != b else rows
                made[b] = jnp.where(here, turned, made[b])
        lanes = slice(half * LANE, (half + 1) * LANE)
        for b in range(per_half):
            key_high[b, :, lanes] = (made[b] >> 8).astype(f32)
            key_low[b, :, lanes] = (made[b] & 255).astype(f32)

    high_rows = columns // LOW
    low_iota = lax.broadcasted_iota(i32, (LOW, LOW), 0).astype(f32).astype(bf16)
    same_node = (
        lax.rem(lax.broadcasted_iota(i32, (16, LOW), 1), 16)
        == lax.broadcasted_iota(i32, (16, LOW), 0)
    ).astype(f32).astype(bf16)
    zero_tile = jnp.zeros((16, LOW), bf16)
    one_low = jnp.ones((LOW, LOW), bf16)
    zero_low = jnp.zeros((LOW, LOW), bf16)
    group_rows = 32
    fold = group_rows // 16

    def build(it, carry):
        for k in range(0, 8, fold):
            made = []
            for kk in range(k, k + fold):
                high_row = jnp.broadcast_to(key_high[kk, pl.ds(it, 1), :], (16, LOW)).astype(bf16)
                low_row = jnp.broadcast_to(key_low[kk, pl.ds(it, 1), :], (16, LOW)).astype(bf16)
                left = jnp.concatenate(
                    [
                        jnp.where(high_row == jnp.asarray(h, bf16), same_node, zero_tile)
                        for h in range(high_rows)
                    ],
                    axis=0,
                ).astype(narrow)
                right = jnp.where(
                    low_iota == jnp.concatenate([low_row] * (LOW // 16), axis=0),
                    one_low,
                    zero_low,
                ).astype(narrow)
                made.append(dot(left, right, NT))
            row = pl.multiple_of(it * 128 + k * 16, group_rows)
            for h in range(high_rows):
                tile = jnp.concatenate([m[h * 16 : h * 16 + 16, :] for m in made], axis=0)
                counts[pl.ds(row, group_rows), h * LOW : (h + 1) * LOW] = tile.astype(
                    counts.dtype
                )
        return carry

    unscale_own = split_in_two(table1[...], first_own)
    spare_rows = slice(fin // 16 * 16, fin // 16 * 16 + 16)
    ones_row = lax.broadcasted_iota(i32, (16, nodes), 0) == fin % 16
    table1[spare_rows, :] = jnp.where(ones_row, 1.0, table1[spare_rows, :].astype(f32)).astype(
        bf16
    )
    lax.fori_loop(0, nodes // 256, build, 0)
    send_weights(1)
    lax.fori_loop(nodes // 256, nodes // 128, build, 0)

    wait_weights(0)
    weight_lanes = (
        slice(0, 2 * LANE),
        weight_parts[1],
        slice(3 * LANE + 2 * hid, 3 * LANE + 4 * hid),
    )
    small_full = wfull[:, 2 * LANE : 3 * LANE].astype(f32)
    for v in range(6):
        vectors[v] = jnp.broadcast_to(small_full[:, v : v + 1], (hid, LANE))

    def matrix(level):
        return wfull[:, weight_lanes[level]]

    wait_rows(out1, in1, row_ssem.at[0], row_rsem.at[0])
    received = in1[...].astype(f32)
    scale = jnp.where(spare == pad - 2, 256.0, jnp.where(spare == pad - 1, 1.0, 0.0))
    label_count = jnp.sum(received * scale, axis=0, keepdims=True)
    unscale_remote = split_in_two(
        jnp.where(spare < pad - 2, received, 0.0).T, first_remote
    )

    def c_block(off, lanes):
        return counts[pl.ds(off, block), lanes].astype(bf16)

    strips = [slice(r, r + STRIP) for r in range(0, hid, STRIP)]

    def fold_rows(value):
        return jnp.sum(value.reshape(STRIP // 8, 8, value.shape[1]), axis=0)

    def activate(level, keep_slope, kept, off, w):
        squares = jnp.zeros((8, block), f32)
        for st in strips:
            if kept is not None and keep_slope:
                b = kept[st, pl.ds(off, block)].astype(f32)
            else:
                b = before[w, st, :] + twice(vectors[level, st, :], block)
            if kept is not None and not keep_slope:
                kept[st, pl.ds(off, block)] = b.astype(kept.dtype)
            s = 0.5 + 0.5 * jnp.tanh(0.5 * b)
            a = b * s
            before[w, st, :] = a
            if keep_slope:
                slope[w, st, :] = s + a * (1.0 - s)
            squares = squares + fold_rows(a * a)
        mean_square = jnp.sum(squares, axis=0, keepdims=True) * (1.0 / hid)
        return lax.rsqrt(mean_square + norm_epsilon)

    def hidden_strip(level, st, inverse, w):
        scaled = before[w, st, :] * inverse
        return (twice(vectors[3 + level, st, :], block) * scaled).astype(bf16)

    def kept_or_none(kept):
        return kept if kept is not None and kept.shape[1] == nodes else None

    def forward_block(level, off, summed, table, mean, kept, keep_slope, w):
        lanes = pl.ds(off, block)
        mean_low = (summed * info[0:1, lanes]).astype(bf16)
        if mean is not None:
            mean[:, lanes] = mean_low
        joined = jnp.concatenate([table[:, lanes], mean_low], axis=0)
        before[w] = dot(matrix(level), joined, NN)
        yield
        return joined, activate(level, keep_slope, kept_or_none(kept), off, w)

    def run_blocks(make):
        def body(k, carry):
            live = [
                make(pl.multiple_of((k * streams + w) * block, block), w)
                for w in range(streams)
            ]
            ended, tick = set(), 0
            while len(ended) < streams:
                for w in range(streams):
                    if tick >= w and w not in ended:
                        if next(live[w], "end") == "end":
                            ended.add(w)
                tick += 1
            return carry

        lax.fori_loop(0, blocks // streams, body, 0)

    send_weights(2)
    def layer_one(off, w):
        rows = pl.ds(off, block)
        own = dot(first_own[...], counts[rows, 0:nodes], NT)
        away = dot(first_remote[...], counts[rows, nodes:], NT)
        yield
        summed = joined_parts(own, unscale_own) + joined_parts(away, unscale_remote)
        _, inverse = yield from forward_block(0, off, summed, table1, mean1, before1, False, w)
        yield
        for st in strips:
            table2[st, rows] = hidden_strip(0, st, inverse, w)

    run_blocks(layer_one)

    def own_sums(table):
        def add(i, carry):
            rows = pl.ds(pl.multiple_of(i * large, large), large)
            wide[:, rows] = dot(table[:, 0:nodes], counts[rows, 0:nodes].astype(bf16), NT)
            return carry

        lax.fori_loop(0, nodes // large, add, 0)

    def exchange_forward(table, x):
        pick_rows(table, outs)
        start_rows(outs, ins.at[x % 2], row_ssem.at[x + 1], row_rsem.at[x + 1])
        own_sums(table)
        wait_rows(outs, ins.at[x % 2], row_ssem.at[x + 1], row_rsem.at[x + 1])
        table[:, nodes:] = ins[x % 2].T

    def all_sums(table, off):
        return wide[:, pl.ds(off, block)] + dot(
            table[:, nodes:], c_block(off, slice(nodes, columns)), NT
        )

    exchange_forward(table2, 0)
    wait_weights(1)

    def layer_two(off, w):
        summed = all_sums(table2, off)
        yield
        _, inverse = yield from forward_block(1, off, summed, table2, mean2, before2, False, w)
        yield
        for st in strips:
            table3[st, pl.ds(off, block)] = hidden_strip(1, st, inverse, w)

    run_blocks(layer_two)

    exchange_forward(table3, 1)
    wait_weights(2)
    head_low = wfull[:, 3 * LANE + 4 * hid :]
    cls_pad = round_up(cls, 16)
    one_over_count = 1.0 / label_count[0:1, 0:1]
    class_iota = lax.broadcasted_iota(i32, (cls_pad, block), 0)

    def backward_block(level, off, joined, inverse, need_input, w):
        lanes = pl.ds(off, block)
        crossed = jnp.zeros((8, block), f32)
        for st in strips:
            gain_term = ghid[w, st, :] * (before[w, st, :] * inverse)
            crossed = crossed + fold_rows(gain_term * twice(vectors[3 + level, st, :], block))
            gain_sum = gain_term[:, 0:LANE]
            for j in range(1, block // LANE):
                gain_sum = gain_sum + gain_term[:, j * LANE : (j + 1) * LANE]
            gacc[level, st, :] += gain_sum
        factor = jnp.sum(crossed, axis=0, keepdims=True) * (1.0 / hid) * inverse * inverse
        low_parts = []
        for st in strips:
            u = ghid[w, st, :] * twice(vectors[3 + level, st, :], block)
            low = (inverse * u - before[w, st, :] * factor) * slope[w, st, :]
            low_parts.append(low.astype(bf16))
        low = jnp.concatenate(low_parts, axis=0)
        yield
        into = gfirst if level == 0 else gfull.at[level - 1]
        added = dot(low, joined, NT)
        for j in range(joined.shape[0] // LANE):
            into[j] += added[:, j * LANE : (j + 1) * LANE]
        if need_input:
            bacc[level - 1] += dot(low, jnp.ones((LANE, block), bf16), NT)
            back = dot(matrix(level), low, TN)
            wide[:, lanes] = back[0:hid, :]
            gmean[:, lanes] = (back[hid:, :] * info[0:1, lanes]).astype(bf16)

    def layer_three(off, w):
        lanes = pl.ds(off, block)
        summed = all_sums(table3, off)
        yield
        joined, inverse = yield from forward_block(
            2, off, summed, table3, None, None, True, w
        )
        last = jnp.concatenate([hidden_strip(2, st, inverse, w) for st in strips], axis=0)
        yield
        logits = dot(head_low, last, TN)[0:cls_pad, :]
        yield
        logits = jnp.where(class_iota < cls, logits, -jnp.inf)
        highest = jnp.max(logits, axis=0, keepdims=True)
        shifted = logits - highest
        grown = jnp.exp(shifted)
        total = jnp.sum(grown, axis=0, keepdims=True)
        hot = class_iota == info[1:2, lanes].astype(i32)
        counted = info[2:3, lanes]
        chosen = jnp.sum(jnp.where(hot, shifted, 0.0), axis=0, keepdims=True)
        losses[w : w + 1, :] += (jnp.log(total) - chosen) * counted
        g_logits = (grown * (1.0 / total) - jnp.where(hot, 1.0, 0.0)) * (counted * one_over_count)
        g_low = jnp.concatenate(
            [g_logits, jnp.zeros((LANE - cls_pad, block), f32)], axis=0
        ).astype(bf16)
        yield
        ghead[...] += dot(last, g_low, NT)
        ghid[w] = dot(head_low, g_low, NN)
        yield
        yield from backward_block(2, off, joined, inverse, True, w)

    run_blocks(layer_three)

    def start_first(seg):
        for piece in range(n_group):
            gwire[seg, piece] = gfull[seg, piece].astype(wire)

        def start(group, shard):
            pltpu.make_async_remote_copy(
                src_ref=gwire.at[seg, group],
                dst_ref=recv1.at[seg, my_group],
                send_sem=g_ssem.at[0, seg],
                recv_sem=g_rsem.at[0, seg],
                device_id=target(group, shard),
                device_id_type=MESH,
            ).start()

        each_group(start)
        recv1[seg, my_group] = jnp.zeros(recv1.shape[2:], wire)

    def start_second(seg):
        wait_bytes(gwire.at[seg, pl.ds(0, n_group - 1)], g_ssem.at[0, seg])
        wait_bytes(recv1.at[seg, pl.ds(0, n_group - 1)], g_rsem.at[0, seg])
        total = gfull[seg, my_group]
        for group in range(n_group):
            total = total + recv1[seg, group].astype(f32)
        gfull[seg, my_group] = total
        send2[seg] = total.astype(wire).reshape(n_shard, chunk, LANE)

        def start(group, shard):
            pltpu.make_async_remote_copy(
                src_ref=send2.at[seg, shard],
                dst_ref=recv2.at[seg, my_shard],
                send_sem=g_ssem.at[1, seg],
                recv_sem=g_rsem.at[1, seg],
                device_id=target(group, shard),
                device_id_type=MESH,
            ).start()

        each_shard(start, my_group, 1)
        recv2[seg, my_shard] = jnp.zeros(recv2.shape[2:], wire)

    def start_third(seg):
        wait_bytes(send2.at[seg, pl.ds(0, n_shard - 1)], g_ssem.at[1, seg])
        wait_bytes(recv2.at[seg, pl.ds(0, n_shard - 1)], g_rsem.at[1, seg])
        total = gfull[seg, my_group, own_chunk, :]
        for shard in range(n_shard):
            total = total + recv2[seg, shard].astype(f32)
        part3[seg] = total

        def start(group, shard):
            pltpu.make_async_remote_copy(
                src_ref=part3.at[seg],
                dst_ref=recv3.at[seg, my_group],
                send_sem=g_ssem.at[2, seg],
                recv_sem=g_rsem.at[2, seg],
                device_id=target(group, shard),
                device_id_type=MESH,
            ).start()

        each_group(start)
        recv3[seg, my_group] = total
        return jnp.sum(total * total, axis=0, keepdims=True)

    def wait_third(seg):
        for _ in range(n_group - 1):
            wait_bytes(part3.at[seg], g_ssem.at[2, seg])
        wait_bytes(recv3.at[seg, pl.ds(0, n_group - 1)], g_rsem.at[2, seg])

    def bias_and_gain(levels, first_lane):
        lane_wide = lax.broadcasted_iota(i32, (hid, LANE), 1)
        total = jnp.zeros((hid, LANE), f32)
        for n, level in enumerate(levels):
            found = jnp.sum(gacc[level], axis=1, keepdims=True)
            total = jnp.where(lane_wide == first_lane + len(levels) + n, found, total)
            if level > 0:
                total = jnp.where(lane_wide == first_lane + n, bacc[level - 1], total)
        return total

    def start_head():
        total = ghead[...] + bias_and_gain((1, 2), cls)
        ghead[...] = total
        hwire[...] = total.astype(wire).reshape(n_shard, chunk, LANE)

        def start(group, shard):
            pltpu.make_async_remote_copy(
                src_ref=hwire.at[shard],
                dst_ref=hrecv.at[my_shard],
                send_sem=h_ssem.at[0],
                recv_sem=h_rsem.at[0],
                device_id=target(group, shard),
                device_id_type=MESH,
            ).start()

        each_shard(start, my_group, 1)
        hrecv[my_shard] = jnp.zeros(hrecv.shape[1:], wire)

    def share_head():
        wait_bytes(hwire.at[pl.ds(0, n_shard - 1)], h_ssem.at[0])
        wait_bytes(hrecv.at[pl.ds(0, n_shard - 1)], h_rsem.at[0])
        total = ghead[own_chunk, :]
        for shard in range(n_shard):
            total = total + hrecv[shard].astype(f32)
        hpart[...] = total

        def start(group, shard):
            pltpu.make_async_remote_copy(
                src_ref=hpart,
                dst_ref=hfinal.at[my_group],
                send_sem=h_ssem.at[1],
                recv_sem=h_rsem.at[1],
                device_id=target(group, shard),
                device_id_type=MESH,
            ).start()

        each_group(start)
        hfinal[my_group] = total

    def wait_head():
        wait_bytes(hfinal.at[pl.ds(0, n_group - 1)], h_ssem.at[1])
        wait_bytes(hfinal.at[pl.ds(0, n_group - 1)], h_rsem.at[1])
        total = hfinal[0]
        for group in range(1, n_group):
            total = total + hfinal[group]
        head_out[...] = total
        return jnp.sum(total * total, axis=0, keepdims=True) * (1.0 / n_group)

    units, unit_rows, row_parts_first = cfg["units"], cfg["unit_rows"], cfg["units"] // 2

    def start_first_layer():
        gfirst[0] += bias_and_gain((0,), fin)
        for unit in range(units):
            tile, part = unit // row_parts_first, unit % row_parts_first
            whole = gfirst[tile].reshape(n_shard, chunk, LANE)
            fwire[unit] = whole[:, part * unit_rows : (part + 1) * unit_rows, :].astype(wire)

        def start(group, shard):
            pltpu.make_async_remote_copy(
                src_ref=fwire.at[lax.rem(group, units), shard],
                dst_ref=frecv.at[me],
                send_sem=f_ssem.at[0],
                recv_sem=f_rsem.at[0],
                device_id=target(group, shard),
                device_id_type=MESH,
            ).start()

        each_device(start)
        frecv[me] = fwire[lax.rem(my_group, units), my_shard]

    def share_first_layer():
        wait_bytes(frecv.at[pl.ds(0, devices - 1)], f_ssem.at[0])
        wait_bytes(frecv.at[pl.ds(0, devices - 1)], f_rsem.at[0])
        total = jnp.sum(frecv[...].astype(f32), axis=0)
        fpart[...] = total

        def start(group, shard):
            pltpu.make_async_remote_copy(
                src_ref=fpart,
                dst_ref=ffinal.at[my_group],
                send_sem=f_ssem.at[1],
                recv_sem=f_rsem.at[1],
                device_id=target(group, shard),
                device_id_type=MESH,
            ).start()

        each_group(start)
        ffinal[my_group] = total
        return jnp.sum(total * total, axis=0, keepdims=True) * (units / n_group)

    def wait_first_layer():
        wait_bytes(ffinal.at[pl.ds(0, n_group - 1)], f_ssem.at[1])
        wait_bytes(ffinal.at[pl.ds(0, n_group - 1)], f_rsem.at[1])
        for unit in range(units):
            tile, part = unit // row_parts_first, unit % row_parts_first
            first_out[tile, part * unit_rows : (part + 1) * unit_rows, :] = ffinal[unit]

    def exchange_backward(x, meanwhile):
        for rows in row_parts:
            lanes = slice(nodes + rows.start, nodes + rows.stop)
            back = dot(gmean[...], counts[:, lanes].astype(bf16), NN)
            outs[rows, :] = back.astype(bf16).T
        start_rows(outs, ins.at[x % 2], row_ssem.at[x + 1], row_rsem.at[x + 1])
        meanwhile()

        def add(i, carry):
            lanes = pl.ds(pl.multiple_of(i * large, large), large)
            wide[:, lanes] += dot(gmean[...], counts[:, lanes].astype(bf16), NN)
            return carry

        lax.fori_loop(0, nodes // large, add, 0)
        wait_rows(outs, ins.at[x % 2], row_ssem.at[x + 1], row_rsem.at[x + 1])

    def returned(x, off):
        total = wide[:, pl.ds(off, block)]
        for rows in row_parts:
            total = total + dot(ins[x % 2, rows, :], picks(rows, off), TN)
        return total

    exchange_backward(2, lambda: start_first(1))
    start_second(1)

    def backward_two(off, w):
        lanes = pl.ds(off, block)
        ghid[w] = returned(2, off)
        joined = jnp.concatenate([table2[:, lanes], mean2[:, lanes]], axis=0)
        if before2.shape[1] < nodes:
            before[w] = dot(matrix(1), joined, NN)
        yield
        inverse = activate(1, True, kept_or_none(before2), off, w)
        yield from backward_block(1, off, joined, inverse, True, w)

    run_blocks(backward_two)

    def meanwhile():
        start_first(0)
        start_head()

    exchange_backward(3, meanwhile)
    square = start_third(1)
    start_second(0)
    share_head()

    def backward_one(off, w):
        lanes = pl.ds(off, block)
        ghid[w] = returned(3, off)
        joined = jnp.concatenate([table1[:, lanes], mean1[:, lanes]], axis=0)
        if before1.shape[1] < nodes:
            before[w] = dot(matrix(0), joined, NN)
        yield
        inverse = activate(0, True, kept_or_none(before1), off, w)
        yield from backward_block(0, off, joined, inverse, False, w)

    run_blocks(backward_one)
    start_first_layer()
    square = square + start_third(0) + wait_head()
    square = square + share_first_layer()

    row_of = lax.broadcasted_iota(i32, (8, LANE), 0)
    loss_row = jnp.sum(losses[...], axis=0, keepdims=True)
    loss_row = sum(loss_row[:, j * LANE : (j + 1) * LANE] for j in range(block // LANE))
    mine = jnp.where(row_of == 0, square, jnp.where(row_of == 1, loss_row, 0.0))
    scal_send[...] = mine

    def send_scalars(group, shard):
        pltpu.make_async_remote_copy(
            src_ref=scal_send.at[pl.ds(0, 2), :],
            dst_ref=scal_recv.at[me, pl.ds(0, 2), :],
            send_sem=s_ssem,
            recv_sem=s_rsem,
            device_id=target(group, shard),
            device_id_type=MESH,
        ).start()

    each_device(send_scalars)
    scal_recv[me] = mine
    for seg in range(2):
        wait_third(seg)
    part_out[...] = recv3[...]
    wait_first_layer()
    others = scal_recv.at[pl.ds(0, devices - 1), pl.ds(0, 2), :]
    wait_bytes(others, s_rsem)
    wait_bytes(others, s_ssem)
    totals = jnp.sum(scal_recv[:, 0:2, :], axis=0)
    scalar_out[0:2, :] = totals
    scalar_out[2:3, :] = label_count


def adamw(weight, grad, moment, square, rate, decay):
    moment_new = beta_one * moment + (1.0 - beta_one) * grad
    square_new = beta_two * square + (1.0 - beta_two) * grad * grad
    moment_hat = moment_new / (1.0 - beta_one**STEP)
    square_hat = square_new / (1.0 - beta_two**STEP)
    weight_new = weight - rate * (
        moment_hat / (jnp.sqrt(square_hat) + adam_epsilon) + decay * weight
    )
    return (weight_new, moment_new, square_new)


def update_kernel(fin, cls, part_ref, head_ref, first_ref, scalar_ref, *refs):
    states = [refs[3 * k : 3 * k + 3] for k in range(5)]
    outs = [refs[15 + 3 * k : 18 + 3 * k] for k in range(5)]
    copies = refs[30:33]
    loss_out, count_out, norm_out = refs[33:36]
    norm = jnp.sqrt(jnp.sum(scalar_ref[0:1, :], axis=1, keepdims=True))
    loss_out[...] = jnp.sum(scalar_ref[1:2, :], axis=1, keepdims=True)
    count_out[...] = scalar_ref[2:3, 0:1]
    norm_out[...] = norm
    factor = jnp.minimum(1.0, threshold / norm)
    small_last = head_ref[...].T
    small_first = first_ref[0].T
    bias = jnp.concatenate([small_first[fin : fin + 1], small_last[cls : cls + 2]], axis=0)
    gain = jnp.concatenate(
        [small_first[fin + 1 : fin + 2], small_last[cls + 2 : cls + 4]], axis=0
    )

    def update(k, grad, where, rate, decay):
        news = adamw(
            states[k][0][where], grad * factor, states[k][1][where], states[k][2][where], rate, decay
        )
        for out, new in zip(outs[k], news):
            out[where] = new
        if k < 3:
            copies[k][where] = news[0].astype(bf16)

    everything = (slice(None), slice(None))
    update(0, first_ref[0][:, 0:fin], (slice(None), slice(0, fin)), 0.05, 0.01)
    update(0, first_ref[1][:, 0:fin], (slice(None), slice(fin, 2 * fin)), 0.05, 0.01)
    n_group = part_ref.shape[1]
    for level in range(2):
        for piece in range(n_group):
            lanes = slice(piece * LANE, (piece + 1) * LANE)
            update(1, part_ref[level, piece], (level, slice(None), lanes), 0.05, 0.01)
    update(2, head_ref[:, 0:cls], everything, 0.05, 0.01)
    update(3, bias, everything, 0.3, 0.0)
    update(4, gain, everything, 0.3, 0.0)


def per_device(
    n_group,
    n_shard,
    features,
    node_counts,
    degrees,
    neighbours,
    send_rows,
    labels,
    train_mask,
    weight_first,
    weight_rest,
    weight_head,
    biases,
    gains,
    moment_first,
    square_first,
    moment_rest,
    square_rest,
    moment_head,
    square_head,
    moment_bias,
    square_bias,
    moment_gain,
    square_gain,
):
    nodes, fin = features.shape
    devices = n_group * n_shard
    hid = weight_rest.shape[1] // 2
    chunk = hid // n_shard
    cls = weight_head.shape[1]
    cap = send_rows.shape[1]
    slots = neighbours.shape[1]
    pad = round_up(cap + 2, 16)
    remote = devices * pad
    columns = nodes + remote
    roomy = remote <= 512
    block, streams, large = (1024, 2, 2048) if roomy else (512, 1, 512)
    wire = bf16 if chunk % 16 == 0 else f32
    least = 16 if wire == bf16 else 8
    units = n_group if chunk * 2 // n_group >= least else 2
    unit_rows = chunk * 2 // units
    fin_pad = LANE
    cfg = dict(
        n_group=n_group,
        n_shard=n_shard,
        nodes=nodes,
        fin=fin,
        cls=cls,
        pad=pad,
        remote=remote,
        chunk=chunk,
        wire=wire,
        block=block,
        streams=streams,
        large=large,
        fin_pad=fin_pad,
        hid=hid,
        cap=cap,
        slots=slots,
        units=units,
        unit_rows=unit_rows,
    )

    vmem = pl.BlockSpec(memory_space=pltpu.VMEM)
    smem = pl.BlockSpec(memory_space=pltpu.SMEM)
    width = 4 * LANE + 4 * hid
    dma = pltpu.SemaphoreType.DMA
    stored = remote if remote <= 512 else 32
    kept_nodes = nodes if remote <= 512 else LANE
    scratch = [
        pltpu.VMEM((nodes, columns), narrow),
        pltpu.VMEM((stored, nodes), narrow),
        pltpu.VMEM((2, remote, LANE), bf16) if roomy else pltpu.VMEM((remote, LANE), i32),
        pltpu.VMEM((nodes // LANE * slots, LANE), i32),
        pltpu.VMEM((8, nodes // LANE, LOW), f32),
        pltpu.VMEM((8, nodes // LANE, LOW), f32),
        pltpu.VMEM((fin_pad, nodes), bf16),
        pltpu.VMEM((hid, columns), bf16),
        pltpu.VMEM((hid, columns), bf16),
        pltpu.VMEM((2 * fin_pad, nodes), narrow),
        pltpu.VMEM((2 * fin_pad, remote), narrow),
        pltpu.VMEM((fin_pad, nodes), bf16),
        pltpu.VMEM((hid, nodes), bf16),
        pltpu.VMEM((hid, kept_nodes), bf16),
        pltpu.VMEM((hid, kept_nodes), f32),
        pltpu.VMEM((hid, nodes), bf16),
        pltpu.VMEM((hid, nodes), f32),
        pltpu.VMEM((remote, hid), bf16),
        pltpu.VMEM((2, remote, hid), bf16),
        pltpu.VMEM((8, nodes), f32),
        pltpu.VMEM((chunk, width), wire),
        pltpu.VMEM((hid, width), wire),
        pltpu.VMEM((hid, width), bf16),
        pltpu.VMEM((6, hid, LANE), f32),
        pltpu.VMEM((streams, hid, block), f32),
        pltpu.VMEM((streams, hid, block), f32),
        pltpu.VMEM((streams, hid, block), f32),
        pltpu.VMEM((8, block), f32),
        pltpu.VMEM((3, hid, LANE), f32),
        pltpu.VMEM((2, hid, LANE), f32),
        pltpu.VMEM((2, n_group, hid, LANE), f32),
        pltpu.VMEM((2, n_group, hid, LANE), wire),
        pltpu.VMEM((2, n_group, hid, LANE), wire),
        pltpu.VMEM((2, n_shard, chunk, LANE), wire),
        pltpu.VMEM((2, n_shard, chunk, LANE), wire),
        pltpu.VMEM((2, chunk, LANE), f32),
        pltpu.VMEM((2, n_group, chunk, LANE), f32),
        pltpu.VMEM((2, hid, LANE), f32),
        pltpu.VMEM((units, n_shard, unit_rows, LANE), wire),
        pltpu.VMEM((devices, unit_rows, LANE), wire),
        pltpu.VMEM((unit_rows, LANE), f32),
        pltpu.VMEM((n_group, unit_rows, LANE), f32),
        pltpu.VMEM((hid, LANE), f32),
        pltpu.VMEM((n_shard, chunk, LANE), wire),
        pltpu.VMEM((n_shard, chunk, LANE), wire),
        pltpu.VMEM((chunk, LANE), f32),
        pltpu.VMEM((n_group, chunk, LANE), f32),
        pltpu.VMEM((8, LANE), f32),
        pltpu.VMEM((devices, 8, LANE), f32),
        dma((5,)),
        dma((5,)),
        dma((3,)),
        dma((3,)),
        dma((3, 2)),
        dma((3, 2)),
        dma((2,)),
        dma((2,)),
        dma((2,)),
        dma((2,)),
        dma,
        dma,
    ]
    sums = pl.pallas_call(
        functools.partial(step_kernel, cfg),
        out_shape=(
            jax.ShapeDtypeStruct((2, n_group, chunk, LANE), f32),
            jax.ShapeDtypeStruct((chunk, LANE), f32),
            jax.ShapeDtypeStruct((2, chunk, LANE), f32),
            jax.ShapeDtypeStruct((8, LANE), f32),
        ),
        in_specs=[vmem] * 5 + [smem] + [vmem] * 6,
        out_specs=(vmem,) * 4,
        scratch_shapes=scratch,
        compiler_params=pltpu.CompilerParams(
            collective_id=0, has_side_effects=True, vmem_limit_bytes=63 * 2**20
        ),
    )(
        features.T,
        neighbours.T,
        degrees.reshape(nodes // LANE, LANE),
        labels.reshape(nodes // LANE, LANE),
        train_mask.reshape(nodes // LANE, LANE),
        node_counts,
        send_rows.T,
        weight_first.T,
        weight_rest.transpose(0, 2, 1),
        weight_head,
        biases,
        gains,
    )
    turned = lambda value: value.T
    turned_rest = lambda value: value.transpose(0, 2, 1)
    same = lambda value: value
    turns = (turned, turned_rest, same, same, same)
    states = (
        (weight_first, moment_first, square_first),
        (weight_rest, moment_rest, square_rest),
        (weight_head, moment_head, square_head),
        (biases, moment_bias, square_bias),
        (gains, moment_gain, square_gain),
    )
    flat = [turn(value) for turn, three in zip(turns, states) for value in three]
    shapes = [jax.ShapeDtypeStruct(value.shape, f32) for value in flat]
    shapes += [jax.ShapeDtypeStruct(flat[3 * k].shape, bf16) for k in range(3)]
    shapes += [jax.ShapeDtypeStruct((1, 1), f32)] * 3
    updated = pl.pallas_call(
        functools.partial(update_kernel, fin, cls),
        out_shape=tuple(shapes),
        in_specs=[vmem] * (4 + len(flat)),
        out_specs=(vmem,) * len(shapes),
    )(*sums, *flat)
    news = tuple(turns[k // 3](updated[k]) for k in range(15))
    copies = tuple(turns[k](updated[15 + k]) for k in range(3))
    return tuple(value.reshape(()) for value in updated[18:]) + news + copies


def solution(mesh):
    nodes_split = P(("group", "shard"))
    nodes_rows = P(("group", "shard"), None)
    first = P(None, "shard")
    rest = P(None, None, "shard")
    head = P("shard", None)
    return jax.shard_map(
        functools.partial(per_device, mesh.shape["group"], mesh.shape["shard"]),
        mesh=mesh,
        in_specs=(
            nodes_rows,
            nodes_split,
            nodes_split,
            nodes_rows,
            nodes_rows,
            nodes_split,
            nodes_split,
            first,
            rest,
            head,
            first,
            first,
            first,
            first,
            rest,
            rest,
            head,
            head,
            first,
            first,
            first,
            first,
        ),
        out_specs=(P(), P(), P())
        + (first,) * 3
        + (rest,) * 3
        + (head,) * 3
        + (first,) * 6
        + (first, rest, head),
        check_vma=False,
    )
```
